32 devices in a mesh: row: 4 (over y, x), col: 8 (over z, core).
Axes of the slice: x: 2, y: 2, z: 4, core: 2. Of those that a mesh axis runs over, the one named last changes fastest.
Arguments:
- lower_panel: float32 [8, 10, 5, 2, 256, 256], P('col', None, None, None, 'row'), may hold values from -0.0625 to 0.0625
- diag_inverse: float32 [8, 10, 2, 256, 256], P('col', None, None, 'row'), may hold values from -3 to 3, as said below
- structure: int32 [8, 10, 5], P('col'), may hold values 0 or 1
Outputs:
- sel_panel: float32 [8, 10, 5, 2, 256, 256], P('col', None, None, None, 'row')
- sel_diag: float32 [8, 10, 2, 256, 256], P('col', None, None, 'row')
The draws below stay inside these ranges and needn't reach their ends.
Inputs may be any that keep to these rules, and one draw needn't show every extreme that they name: Every block diag_inverse[c, s, k] equals its own transpose.
All inputs are finite; a program needn't handle non-finite values. No bound on the sum of `structure` on one device may be relied on, other than what follows from the above.
Results may differ from the reference program's by a relative error of at most 0.0001.
Values sent between devices are 32-bit elements; how exact they have to be, the bound alone decides.
No kernel may reach another device: no remote copies, remote signals or barrier semaphores. Data moves between devices by JAX's collectives and lax.ppermute only.
A program may use at most 128 MiB of HBM per device.

```python
import math
import jax
import jax.numpy as jnp
from jax import lax

W = 256
LEVELS = 6
ANC = 5
SLOTS = 10
N_COL = 8


def draw_diag_inverse(key, part):
    shape = (N_COL, SLOTS, 2, W, W)
    first_key, second_key = jax.random.split(key)
    noise_draw = jax.random.normal(first_key, shape, jnp.float32)
    symmetric = (noise_draw + jnp.swapaxes(noise_draw, -1, -2)) * (0.5 / math.sqrt(W))
    row_ids = lax.broadcasted_iota(jnp.int32, (W, W), 0)
    col_ids = lax.broadcasted_iota(jnp.int32, (W, W), 1)
    identity = (row_ids == col_ids).astype(jnp.float32)
    scales = jax.random.uniform(second_key, (N_COL, SLOTS, 2, W), jnp.float32, 0.5, 1.5)
    real_only = (lax.broadcasted_iota(jnp.int32, (2, 1, 1), 0) == 0).astype(jnp.float32)
    return symmetric + identity * scales[..., None] * real_only


def plant(values, key, smallest, top_value):
    longest = values.shape.index(max(values.shape))
    spots = []
    for shift in (0, 1):
        where = [jax.random.randint(jax.random.fold_in(key, axis), (), 0, length) for axis, length in enumerate(values.shape)]
        where[longest] = (where[longest] + shift) % values.shape[longest]
        spots.append(tuple(where))
    return values.at[spots[0]].set(smallest).at[spots[1]].set(top_value)


def block_scale(stream_key, shape, cuts, least, high):
    loudness, own = 1.0, jax.random.fold_in(stream_key, 6)
    for axis_at, blocks in cuts:
        draws = jnp.exp(jax.random.uniform(jax.random.fold_in(own, axis_at), (blocks,), jnp.float32, least / len(cuts), high / len(cuts)))
        loudness = loudness * jnp.repeat(draws, shape[axis_at] // blocks).reshape([-1 if axis == axis_at else 1 for axis in range(len(shape))])
    return loudness


def noise(stream_key, extent, width, reach, shards=(), dtype=jnp.bfloat16):
    array = jax.random.normal(stream_key, extent, jnp.float32) * width
    if len(shards) > 0:
        array = block_scale(stream_key, extent, shards, -0.22, 0.18) * array
    return jnp.clip(array, min=-reach, max=reach).astype(dtype)


def setup_inputs(seed: int = 0) -> dict:
    key_list = jax.random.split(jax.random.key(seed), 4)
    return {
        "lower_panel": noise(key_list[0], (N_COL, SLOTS, ANC, 2, W, W), (8 * ANC * W) ** -0.5, 0.0625, ((0, 8), (4, 4)), jnp.float32),
        "diag_inverse": draw_diag_inverse(jax.random.fold_in(key_list[3], 71), 0),
        "structure": plant((jax.random.randint(key_list[2], (N_COL, SLOTS, ANC), 0, 4) < 3).astype(jnp.int32), jax.random.fold_in(key_list[2], 1), 0, 1),
    }


def complex_product(first_factor, second_factor):
    highest = lax.Precision.HIGHEST
    real_part = jnp.dot(first_factor[0], second_factor[0], precision=highest) - jnp.dot(first_factor[1], second_factor[1], precision=highest)
    imag_part = jnp.dot(first_factor[0], second_factor[1], precision=highest) + jnp.dot(first_factor[1], second_factor[0], precision=highest)
    return jnp.stack([real_part, imag_part])


def transposed(matrix):
    return jnp.swapaxes(matrix, -1, -2)


def reference(lower_panel, diag_inverse, structure):
    block_width = lower_panel.shape[-1]
    slot_count = lower_panel.shape[1]
    anc_count = lower_panel.shape[2]
    zero_panel = jnp.zeros((anc_count, 2, block_width, block_width), jnp.float32)
    zero_block = jnp.zeros((2, block_width, block_width), jnp.float32)
    panel_table = [[zero_panel for slot_index in range(slot_count)] for column in range(N_COL)]
    diag_table = [[zero_block for slot_index in range(slot_count)] for column in range(N_COL)]
    previous = {}
    offset = 0
    for tree_depth in range(LEVELS):
        per_col = max(1, 2 ** tree_depth // N_COL)
        current = {}
        for member in range(2 ** tree_depth):
            column = (member * N_COL) // 2 ** tree_depth
            slot_index = offset + member % per_col
            inverse_block = diag_inverse[column, slot_index]
            if tree_depth == 0:
                diagonal = inverse_block
                chain_new = inverse_block
            else:
                present = structure[column, slot_index, :tree_depth].astype(jnp.float32)
                panels = lower_panel[column, slot_index, :tree_depth] * present[:, None, None, None]
                stacked = jnp.concatenate([panels[row_pos] for row_pos in range(tree_depth)], axis=1)
                parent_chain = previous[member // 2]
                lifted = -complex_product(parent_chain, stacked)
                diagonal = inverse_block - complex_product(transposed(stacked), lifted)
                top_row = jnp.concatenate([diagonal, transposed(lifted)], axis=2)
                bottom_rows = jnp.concatenate([lifted, parent_chain], axis=2)
                chain_new = jnp.concatenate([top_row, bottom_rows], axis=1)
                pieces = [lifted[:, row_pos * block_width:(row_pos + 1) * block_width] for row_pos in range(tree_depth)]
                pieces = pieces + [zero_block for row_pos in range(anc_count - tree_depth)]
                panel_table[column][slot_index] = jnp.stack(pieces)
            diag_table[column][slot_index] = diagonal
            current[member] = chain_new
        previous = current
        offset = offset + per_col
    sel_panel = jnp.stack([jnp.stack(panel_table[column]) for column in range(N_COL)])
    sel_diag = jnp.stack([jnp.stack(diag_table[column]) for column in range(N_COL)])
    return sel_panel, sel_diag
```

```python
import jax
import jax.numpy as jnp
from jax import lax
from jax.sharding import PartitionSpec as P

LEVELS = 6
HIGH = lax.Precision.HIGH


def xor_swap(value, axis, mask):
    count = lax.axis_size(axis)
    return lax.ppermute(value, axis, [(source, source ^ mask) for source in range(count)])


def natural_order(relative, index):
    count = relative.shape[0]
    bit = 1
    while bit < count:
        pairs = relative.reshape((count // (2 * bit), 2, bit) + relative.shape[1:])
        flipped = jnp.where((index // bit) % 2 == 1, pairs[:, ::-1], pairs)
        relative = flipped.reshape(relative.shape)
        bit *= 2
    return relative


def gather_bits(stacked, axis, masks):
    for mask in masks:
        stacked = jnp.stack([stacked, xor_swap(stacked, axis, mask)], axis=0)
    return stacked


def gather_rows(chunks, masks):
    parts = []
    for which, order in ((0, masks), (1, masks[::-1])):
        got = gather_bits(chunks[:, which], "row", order)
        axes = [order[::-1].index(mask) for mask in masks[::-1]]
        got = jnp.transpose(got, axes + list(range(len(masks), got.ndim)))
        parts.append(got.reshape((2 ** len(masks),) + got.shape[len(masks):]))
    return jnp.stack(parts, axis=2)


def whole_blocks(by_place):
    rows, blocks, two, chunk, width = by_place.shape
    return jnp.transpose(by_place, (1, 2, 0, 3, 4)).reshape(blocks, two, rows * chunk, width)


def bits_below(count):
    masks = []
    mask = 1
    while mask < count:
        masks.append(mask)
        mask *= 2
    return masks


def complex_rhs(value):
    real, imag = value[0], value[1]
    return jnp.concatenate(
        [jnp.concatenate([real, imag], axis=1), jnp.concatenate([-imag, real], axis=1)], axis=0
    )


def stacked_rows(blocks):
    depth, two, width, _ = blocks.shape
    return jnp.transpose(blocks, (1, 0, 2, 3)).reshape(two, depth * width, width)


def chain_step(parent, panels, inverse):
    depth, _, width, _ = panels.shape
    stacked = stacked_rows(panels)
    left = jnp.concatenate([parent[0], parent[1]], axis=1)
    product = jnp.dot(left, complex_rhs(stacked), precision=HIGH)
    lifted = -jnp.stack([product[:, :width], product[:, width:]])
    flat = stacked.reshape(2 * depth * width, width)
    product = lax.dot_general(
        flat, complex_rhs(lifted), (((0,), (0,)), ((), ())), precision=HIGH
    )
    correction = jnp.stack([product[:, :width], product[:, width:]])
    return lifted, correction


def grow(parent, lifted, diagonal):
    top = jnp.concatenate([diagonal, jnp.swapaxes(lifted, -1, -2)], axis=2)
    bottom = jnp.concatenate([lifted, parent], axis=2)
    return jnp.concatenate([top, bottom], axis=1)


def my_rows(blocks, place, chunk):
    return lax.dynamic_slice_in_dim(blocks, place * chunk, chunk, axis=blocks.ndim - 2)


def body(lower_panel, diag_inverse, structure):
    columns = lax.axis_size("col")
    rows = lax.axis_size("row")
    position = lax.axis_index("col")
    place = lax.axis_index("row")
    anc_count, chunk, width = lower_panel.shape[2], lower_panel.shape[4], lower_panel.shape[5]
    row_masks = bits_below(rows)
    per_col = [max(1, 2**depth // columns) for depth in range(LEVELS)]
    offsets = [sum(per_col[:depth]) for depth in range(LEVELS)]

    def packed(depth):
        span = slice(offsets[depth], offsets[depth] + per_col[depth])
        present = structure[0, span, :depth].astype(jnp.float32)
        panels = lower_panel[0, span, :depth] * present[:, :, None, None, None]
        return jnp.concatenate([diag_inverse[0, span][:, None], panels], axis=1)

    shared = [depth for depth in range(LEVELS) if 2**depth < columns]
    local = [depth for depth in range(LEVELS) if 2**depth >= columns]

    own_pack = packed(shared[-1])[0]
    upper = shared[:-1]
    sizes = [1 + depth for depth in upper]
    starts = [sum(sizes[:place_at]) for place_at in range(len(sizes))]
    strides = [columns // 2**depth for depth in upper]
    upper_pack = jnp.concatenate([packed(depth)[0] for depth in upper], axis=0)
    got = [None for _ in upper]
    for step in range(1, columns, 2):
        held = [index for index, stride in enumerate(strides) if stride > step]
        count = sum(sizes[index] for index in held)
        smallest = min(strides[index] for index in held)
        pairs = [(source, source + step) for source in range(0, columns, smallest)]
        pairs = [pair for pair in pairs if pair[1] < columns]
        arrived = lax.ppermute(upper_pack[:count], "col", pairs)
        for index in held:
            part = arrived[starts[index] : starts[index] + sizes[index]]
            mine = position % strides[index] == step
            got[index] = part if got[index] is None else jnp.where(mine, part, got[index])
    upper_got = jnp.concatenate(got, axis=0)
    pack_size = max(own_pack.shape[0], upper_got.shape[0])

    def fill(pack):
        return jnp.pad(pack, ((0, pack_size - pack.shape[0]), (0, 0), (0, 0), (0, 0)))

    odd = position % 2 == 1

    def whole_from_rows(chunks):
        return whole_blocks(natural_order(gather_rows(chunks, row_masks), place))

    half = whole_from_rows(jnp.where(odd, fill(upper_got), fill(own_pack)))
    other = xor_swap(half, "col", 1)
    upper_whole = jnp.where(odd, half, other)
    own_whole = jnp.where(odd, other, half)

    def node_in(depth):
        nodes = per_col[depth]
        group = rows // nodes
        chunks = packed(depth)
        if depth == LEVELS - 1 and nodes == rows:
            chunks = chunks[:, 1:]
        node = place // group
        parts = []
        for step in range(nodes):
            piece = lax.dynamic_index_in_dim(chunks, node ^ step, 0, keepdims=False)
            parts.append(xor_swap(piece, "row", step * group) if step else piece)
        if nodes == 1:
            relative = gather_rows(parts[0], bits_below(group))
            return whole_blocks(natural_order(relative, place))
        relative = jnp.stack(parts, axis=0)
        within = gather_bits(relative, "row", bits_below(group))
        relative = jnp.moveaxis(
            within.reshape((group,) + relative.shape), 0, 1
        ).reshape((rows,) + relative.shape[1:])
        return whole_blocks(natural_order(relative, place))

    def node_out(blocks, depth):
        nodes = per_col[depth]
        group = rows // nodes
        node = place // group
        parts = []
        for step in range(nodes):
            piece = my_rows(blocks, place ^ (step * group), chunk)
            parts.append(xor_swap(piece, "row", step * group) if step else piece)
        return natural_order(jnp.stack(parts, axis=0), node)

    inputs = {}
    for index, depth in enumerate(upper):
        inputs[depth] = upper_whole[starts[index] : starts[index] + sizes[index]]
    inputs[shared[-1]] = own_whole[: 1 + shared[-1]]
    for depth in local:
        inputs[depth] = node_in(depth)

    chain = inputs[0][0]
    panel_parts = []
    diag_parts = []
    for depth in range(LEVELS):
        nodes = per_col[depth]
        span = slice(offsets[depth], offsets[depth] + nodes)
        if depth == 0:
            lifted_rows = jnp.zeros((1, 0, 2, chunk, width), jnp.float32)
            diagonal_rows = diag_inverse[0, span]
        else:
            taken = inputs[depth]
            with_diagonal = taken.shape[0] == depth + 1
            panels = taken[1:] if with_diagonal else taken
            lifted, correction = chain_step(chain, panels, None)
            blocks = jnp.transpose(lifted.reshape(2, depth, width, width), (1, 0, 2, 3))
            if depth == LEVELS - 1:
                back = node_out(jnp.concatenate([correction[None], blocks], axis=0), depth)
                diagonal_rows = diag_inverse[0, span] - back[:, 0]
                lifted_rows = back[:, 1:]
            else:
                diagonal = taken[0] - correction
                chain = grow(chain, lifted, diagonal)
                back = node_out(jnp.concatenate([diagonal[None], blocks], axis=0), depth)
                diagonal_rows, lifted_rows = back[:, 0], back[:, 1:]
        filler = jnp.zeros((nodes, anc_count - depth, 2, chunk, width), jnp.float32)
        lifted_pad = jnp.concatenate([lifted_rows, filler], axis=1)
        if 2**depth < columns:
            active = position % (columns // 2**depth) == 0
            lifted_pad = jnp.where(active, lifted_pad, 0.0)
            diagonal_rows = jnp.where(active, diagonal_rows, 0.0)
        panel_parts.append(lifted_pad)
        diag_parts.append(diagonal_rows)
    sel_panel = jnp.concatenate(panel_parts, axis=0)[None]
    sel_diag = jnp.concatenate(diag_parts, axis=0)[None]
    return (sel_panel, sel_diag)


def solution(mesh):
    in_specs = (
        P("col", None, None, None, "row", None),
        P("col", None, None, "row", None),
        P("col", None, None),
    )
    out_specs = (P("col", None, None, None, "row", None), P("col", None, None, "row", None))
    return jax.shard_map(body, mesh=mesh, in_specs=in_specs, out_specs=out_specs, check_vma=False)
```

```python
import functools

import jax
import jax.numpy as jnp
from jax import lax
from jax.experimental import pallas as pl
from jax.experimental.pallas import tpu as pltpu
from jax.sharding import PartitionSpec as P

LEVELS = 6
HALVES = 2
VMEM_BYTES = 56 * 2**20
F32 = jnp.float32
BF16 = jnp.bfloat16


def xor_swap(value, axis, mask):
    count = lax.axis_size(axis)
    return lax.ppermute(value, axis, [(source, source ^ mask) for source in range(count)])


def split(value):
    high = value.astype(BF16)
    return high, (value - high.astype(F32)).astype(BF16)


def three_products(left_high, left_low, right_high, right_low):
    left = jnp.concatenate([left_high, left_high, left_low], axis=1)
    right = jnp.concatenate([right_high, right_low, right_high], axis=0)
    return jnp.dot(left, right, preferred_element_type=F32)


def complex_apply(real_parts, imag_parts, right_parts, half):
    by_real = three_products(*real_parts, *right_parts)
    by_imag = three_products(*imag_parts, *right_parts)
    return jnp.concatenate(
        [by_real[:, :half] - by_imag[:, half:], by_real[:, half:] + by_imag[:, :half]], axis=1
    )


def run_kernel(kernel, outs, scalars, arrays, scratch, flops):
    size = sum(2 * value.size for value in arrays) + sum(2 * out.size for out in outs)
    return pl.pallas_call(
        kernel,
        out_shape=outs,
        in_specs=[pl.BlockSpec(memory_space=pltpu.SMEM)]
        + [pl.BlockSpec(memory_space=pltpu.VMEM)] * len(arrays),
        out_specs=[pl.BlockSpec(memory_space=pltpu.VMEM)] * len(outs),
        scratch_shapes=scratch,
        compiler_params=pltpu.CompilerParams(vmem_limit_bytes=VMEM_BYTES),
        cost_estimate=pl.CostEstimate(flops=flops, bytes_accessed=2 * size, transcendentals=0),
    )(scalars, *arrays)


def pieces_of(listed):
    out = []
    for position, (mask, part, value) in enumerate(listed):
        if part is None:
            out.append((mask, 0, position, 0))
            out.append((mask, 1, position, 1))
        else:
            out.append((mask, part, position, None))
    return out


def read_piece(refs, block, index):
    return (lambda ref: ref[block] if index is None else ref[block, index])(refs)


def prep_kernel(levels, table, n_arrays, chunk, width, n_src, *refs):
    scalars = refs[0]
    arrays = refs[1 : 1 + n_arrays]
    outs = list(refs[1 + n_arrays :])
    place = scalars[0]
    odd = scalars[1] == 1
    for depth, sources in levels:
        whole = None if depth == 0 else outs.pop(0)
        if depth:
            fwd_high, fwd_low = outs.pop(0), outs.pop(0)
        back_high, back_low = outs.pop(0), outs.pop(0)
        for block in range(depth + 1):
            for mask, part, position, index in table:
                if n_src == 1:
                    value = read_piece(arrays[position], sources[0][1] + block, index)
                else:
                    half = n_arrays // 2
                    from_even = arrays[position + (0 if sources[0][0] == 0 else half)]
                    from_odd = arrays[position + (half if sources[0][0] == 0 else 0)]
                    at = sources[0][1] + block
                    value = jnp.where(
                        odd, read_piece(from_odd, at, index), read_piece(from_even, at, index)
                    )
                start = pl.multiple_of((place ^ mask) * chunk, chunk)
                if block == 0:
                    high, low = split(value)
                    lanes = pl.ds(depth * width, width)
                    back_high[part, pl.ds(start, chunk), lanes] = high
                    back_low[part, pl.ds(start, chunk), lanes] = low
                else:
                    row = (depth - block) * width
                    whole[pl.ds(pl.multiple_of(row + start, chunk), chunk), pl.ds(part * width, width)] = value
        for row in range(0, depth * width, width):
            for part in range(2):
                value = whole[pl.ds(row, width), pl.ds(part * width, width)]
                high, low = split(value)
                fwd_high[pl.ds(row, width), pl.ds(part * width, width)] = high
                fwd_low[pl.ds(row, width), pl.ds(part * width, width)] = low
                high, low = split(-value.T)
                back_high[part, :, pl.ds(row, width)] = high
                back_low[part, :, pl.ds(row, width)] = low


def prep(levels, listed, scalars, chunk, width, n_src=1):
    table = pieces_of(listed[: len(listed) // n_src])
    arrays = [value for _, _, value in listed]
    outs = []
    for depth, _ in levels:
        if depth:
            outs.append(jax.ShapeDtypeStruct((depth * width, 2 * width), F32))
            outs += [jax.ShapeDtypeStruct((depth * width, 2 * width), BF16)] * 2
        outs += [jax.ShapeDtypeStruct((2, width, (depth + 1) * width), BF16)] * 2
    kernel = functools.partial(prep_kernel, levels, table, len(arrays), chunk, width, n_src)
    made = list(run_kernel(kernel, outs, scalars, arrays, [], 0))
    result = {}
    for depth, _ in levels:
        if depth:
            result[depth] = tuple(made[:5])
            made = made[5:]
        else:
            result[depth] = (None, None, None, made[0], made[1])
            made = made[2:]
    return result


def substitute(depth, width, cols, forward, backward, sums, right_high, right_low, emit):
    def rows(first, count=1):
        return pl.ds(first * width, count * width)

    for level in range(depth - 1, 0, -1):
        high, low = split(sums[rows(level)])
        right_high[rows(level)] = high
        right_low[rows(level)] = low
        fwd_high, fwd_low = forward[level]
        for block in range(level - 1, -1, -1):
            real = (fwd_high[rows(block), :width], fwd_low[rows(block), :width])
            imag = (fwd_high[rows(block), width:], fwd_low[rows(block), width:])
            sums[rows(block)] -= complex_apply(real, imag, (high, low), cols)
    high, low = split(sums[rows(0)])
    right_high[rows(0)] = high
    right_low[rows(0)] = low
    for level in range(depth):
        back_high, back_low = backward[level]
        right = (right_high[rows(0, level + 1)], right_low[rows(0, level + 1)])
        real = (back_high[0], back_low[0])
        imag = (back_high[1], back_low[1])
        solved = complex_apply(real, imag, right, cols)
        high, low = split(solved)
        right_high[rows(level)] = high
        right_low[rows(level)] = low
        emit(level, solved)


def solve_kernel(depth, chunk, width, steps, *refs):
    refs = list(refs)
    scalars = refs.pop(0)
    whole = refs.pop(0)
    forward = {level: (refs.pop(0), refs.pop(0)) for level in range(1, depth)}
    backward = {level: (refs.pop(0), refs.pop(0)) for level in range(depth + 1)}
    outs = [refs.pop(0) for _ in steps]
    sums, right_high, right_low, solved_ref = refs
    place = scalars[0]
    sums[...] = whole[...]

    def send(block, value, sign):
        solved_ref[...] = value
        for out, step in zip(outs, steps):
            start = pl.multiple_of((place ^ step) * chunk, chunk)
            piece = solved_ref[pl.ds(start, chunk)]
            out[block, 0] = sign * piece[:, :width]
            out[block, 1] = sign * piece[:, width:]

    substitute(
        depth, width, width, forward, backward, sums, right_high, right_low,
        lambda level, solved: send(depth - level, solved, -1.0),
    )
    back_high, back_low = backward[depth]
    span = depth * width
    correction = complex_apply(
        (back_high[0, :, :span], back_low[0, :, :span]),
        (back_high[1, :, :span], back_low[1, :, :span]),
        (right_high[...], right_low[...]),
        width,
    )
    send(0, correction, 1.0)


def solve(depth, made, scalars, steps, chunk, width):
    arrays = [made[depth][0]]
    for level in range(1, depth):
        arrays += made[level][1:3]
    for level in range(depth + 1):
        arrays += made[level][3:5]
    outs = [jax.ShapeDtypeStruct((1 + depth, 2, chunk, width), F32) for _ in steps]
    scratch = [
        pltpu.VMEM((depth * width, 2 * width), F32),
        pltpu.VMEM((depth * width, 2 * width), BF16),
        pltpu.VMEM((depth * width, 2 * width), BF16),
        pltpu.VMEM((width, 2 * width), F32),
    ]
    kernel = functools.partial(solve_kernel, depth, chunk, width, steps)
    flops = 24 * (depth * depth + depth) * width**3
    return run_kernel(kernel, outs, scalars, arrays, scratch, flops)


def last_kernel(depth, chunk, width, cols, steps, table, n_arrays, *refs):
    refs = list(refs)
    scalars = refs.pop(0)
    arrays = [refs.pop(0) for _ in range(n_arrays)]
    forward = {level: (refs.pop(0), refs.pop(0)) for level in range(1, depth)}
    backward = {level: (refs.pop(0), refs.pop(0)) for level in range(depth)}
    outs = [refs.pop(0) for _ in steps]
    left_high, left_low, right_high, right_low, sums, solved_ref = refs
    place = scalars[0]
    for mask, part, position, index in table:
        start = pl.multiple_of((place ^ mask) * chunk, chunk)
        for block in range(depth):
            row = pl.multiple_of((depth - 1 - block) * width + start, chunk)
            sums[pl.ds(row, chunk), pl.ds(part * cols, cols)] = read_piece(arrays[position], block, index)
    for level in range(depth):
        for part in range(2):
            value = sums[pl.ds(level * width, width), pl.ds(part * cols, cols)]
            high, low = split(value.T)
            left_high[part, :, pl.ds(level * width, width)] = high
            left_low[part, :, pl.ds(level * width, width)] = low

    def emit(level, value):
        solved_ref[...] = value
        for out, step in zip(outs, steps):
            start = pl.multiple_of((place ^ step) * chunk, chunk)
            piece = solved_ref[pl.ds(start, chunk)]
            out[depth - 1 - level, 0] = -piece[:, :cols]
            out[depth - 1 - level, 1] = -piece[:, cols:]

    substitute(depth, width, cols, forward, backward, sums, right_high, right_low, emit)


def solve_last(depth, made, listed, scalars, steps, chunk, width, cols):
    table = pieces_of(listed)
    arrays = [value for _, _, value in listed]
    n_arrays = len(arrays)
    for level in range(1, depth):
        arrays += made[level][1:3]
    for level in range(depth):
        arrays += made[level][3:5]
    outs = [jax.ShapeDtypeStruct((depth, 2, chunk, cols), F32) for _ in steps]
    outs += [jax.ShapeDtypeStruct((2, cols, depth * width), BF16)] * 2
    outs += [jax.ShapeDtypeStruct((depth * width, 2 * cols), BF16)] * 2
    scratch = [pltpu.VMEM((depth * width, 2 * cols), F32), pltpu.VMEM((width, 2 * cols), F32)]
    kernel = functools.partial(last_kernel, depth, chunk, width, cols, steps, table, n_arrays)
    flops = 24 * depth * depth * width * width * cols
    made_now = run_kernel(kernel, outs, scalars, arrays, scratch, flops)
    return made_now[: len(steps)], made_now[len(steps) :]


def correction_kernel(chunk, width, cols, steps, parts, *refs):
    refs = list(refs)
    scalars = refs.pop(0)
    lefts = [(refs.pop(0), refs.pop(0), refs.pop(0), refs.pop(0)) for _ in range(parts)]
    outs = [refs.pop(0) for _ in steps]
    (total,) = refs
    place = scalars[0]
    for row, (left_high, left_low, _, _) in enumerate(lefts):
        for col, (_, _, right_high, right_low) in enumerate(lefts):
            product = complex_apply(
                (left_high[0], left_low[0]),
                (left_high[1], left_low[1]),
                (right_high[...], right_low[...]),
                cols,
            )
            total[0, pl.ds(row * cols, cols), pl.ds(col * cols, cols)] = -product[:, :cols]
            total[1, pl.ds(row * cols, cols), pl.ds(col * cols, cols)] = -product[:, cols:]
    for out, step in zip(outs, steps):
        start = pl.multiple_of((place ^ step) * chunk, chunk)
        out[0] = total[0, pl.ds(start, chunk)]
        out[1] = total[1, pl.ds(start, chunk)]


def last_correction(lefts, scalars, steps, chunk, width, cols):
    arrays = [value for left in lefts for value in left]
    outs = [jax.ShapeDtypeStruct((2, chunk, width), F32) for _ in steps]
    kernel = functools.partial(correction_kernel, chunk, width, cols, steps, len(lefts))
    flops = 24 * lefts[0][2].shape[0] * width * width
    return run_kernel(kernel, outs, scalars, arrays, [pltpu.VMEM((2, width, width), F32)], flops)


def gather(piece, group):
    if group == 4:
        near, far = xor_swap(piece, "row", 1), xor_swap(piece, "row", 2)
        return [
            (0, None, piece),
            (1, None, near),
            (2, None, far),
            (3, 0, xor_swap(far[:, 0], "row", 1)),
            (3, 1, xor_swap(near[:, 1], "row", 2)),
        ]
    listed = [(0, None, piece)]
    mask = 1
    while mask < group:
        listed += [(mask | at, part, xor_swap(value, "row", mask)) for at, part, value in listed]
        mask *= 2
    return listed


def body(lower_panel, diag_inverse, structure):
    columns = lax.axis_size("col")
    rows = lax.axis_size("row")
    position = lax.axis_index("col")
    place = lax.axis_index("row")
    anc_count, chunk, width = lower_panel.shape[2], lower_panel.shape[4], lower_panel.shape[5]
    per_col = [max(1, 2**depth // columns) for depth in range(LEVELS)]
    offsets = [sum(per_col[:depth]) for depth in range(LEVELS)]
    last = LEVELS - 1
    scalars = jnp.stack([place, position % 2]).astype(jnp.int32)

    def panels_of(depth, node, lanes=slice(None)):
        slot = offsets[depth] + node
        present = lax.dynamic_index_in_dim(structure[0], slot, 0, keepdims=False)[:depth]
        panels = lax.dynamic_index_in_dim(lower_panel[0], slot, 0, keepdims=False)[:depth, ..., lanes]
        return panels * present.astype(F32)[:, None, None, None]

    def packed(depth, node):
        own = lax.dynamic_index_in_dim(diag_inverse[0], offsets[depth] + node, 0, keepdims=True)
        return jnp.concatenate([own, panels_of(depth, node)], axis=0)

    def fetch(depth, cut):
        nodes = per_col[depth]
        group = rows // nodes
        node = place // group
        listed = []
        for step in range(nodes):
            piece = cut(node ^ step)
            if step:
                piece = xor_swap(piece, "row", step * group)
            for mask, part, value in gather(piece, group):
                listed.append((step * group + mask, part, value))
        return listed

    def give_back(pieces, depth):
        group = rows // per_col[depth]
        return [
            xor_swap(piece, "row", step * group) if step else piece
            for step, piece in enumerate(pieces)
        ]

    def steps_of(depth):
        group = rows // per_col[depth]
        return [step * group for step in range(per_col[depth])]

    shared = [depth for depth in range(LEVELS) if 2**depth < columns]
    local = [depth for depth in range(LEVELS) if 2**depth >= columns]

    own_pack = packed(shared[-1], 0)
    upper = shared[:-1]
    sizes = [1 + depth for depth in upper]
    starts = [sum(sizes[:at]) for at in range(len(sizes))]
    strides = [columns // 2**depth for depth in upper]
    upper_pack = jnp.concatenate([packed(depth, 0) for depth in upper], axis=0)
    got = [None for _ in upper]
    for step in range(1, columns, 2):
        held = [index for index, stride in enumerate(strides) if stride > step]
        count = sum(sizes[index] for index in held)
        smallest = min(strides[index] for index in held)
        pairs = [(source, source + step) for source in range(0, columns, smallest)]
        pairs = [pair for pair in pairs if pair[1] < columns]
        arrived = lax.ppermute(upper_pack[:count], "col", pairs)
        for index in held:
            part = arrived[starts[index] : starts[index] + sizes[index]]
            mine = position % strides[index] == step
            got[index] = part if got[index] is None else jnp.where(mine, part, got[index])
    upper_got = jnp.concatenate(got, axis=0)
    pack_size = max(own_pack.shape[0], upper_got.shape[0])

    def fill(pack):
        return jnp.pad(pack, ((0, pack_size - pack.shape[0]), (0, 0), (0, 0), (0, 0)))

    odd = position % 2 == 1
    mine = gather(jnp.where(odd, fill(upper_got), fill(own_pack)), rows)
    theirs = [(mask, part, xor_swap(value, "col", 1)) for mask, part, value in mine]

    made = {}
    for depth in local:
        if depth < last:
            listed = fetch(depth, functools.partial(packed, depth))
            made.update(prep([(depth, [(0, 0)])], listed, scalars, chunk, width))
    levels = [(depth, [(1, starts[index])]) for index, depth in enumerate(upper)]
    levels.append((shared[-1], [(0, 0)]))
    made.update(prep(levels, mine + theirs, scalars, chunk, width, n_src=2))

    cols = width // HALVES
    last_pieces = [
        fetch(last, functools.partial(panels_of, last, lanes=slice(half * cols, (half + 1) * cols)))
        for half in range(HALVES)
    ]

    panel_parts = [jnp.zeros((1, anc_count, 2, chunk, width), F32)]
    diag_parts = [diag_inverse[0, :1]]
    for depth in range(1, last):
        nodes = per_col[depth]
        back = give_back(solve(depth, made, scalars, steps_of(depth), chunk, width), depth)
        node = place // (rows // nodes)
        stacked = jnp.zeros((nodes, anc_count + 1, 2, chunk, width), F32)
        for step, piece in enumerate(back):
            stacked = lax.dynamic_update_slice(stacked, piece[None], (node ^ step, 0, 0, 0, 0))
        diag_parts.append(diag_inverse[0, offsets[depth] : offsets[depth] + nodes] - stacked[:, 0])
        panel_parts.append(stacked[:, 1:])
    for depth in shared:
        active = position % (columns // 2**depth) == 0
        panel_parts[depth] = jnp.where(active, panel_parts[depth], 0.0)
        diag_parts[depth] = jnp.where(active, diag_parts[depth], 0.0)

    nodes = per_col[last]
    panel_parts.append(jnp.zeros((nodes, anc_count, 2, chunk, width), F32))
    diag_parts.append(diag_inverse[0, offsets[last] : offsets[last] + nodes])
    sel_panel = jnp.concatenate(panel_parts, axis=0)
    sel_diag = jnp.concatenate(diag_parts, axis=0)
    node = place // (rows // nodes)
    lefts = []
    backs = []
    for half in range(HALVES):
        pieces, left = solve_last(
            last, made, last_pieces[half], scalars, steps_of(last), chunk, width, cols
        )
        lefts.append(left)
        backs.append(give_back(pieces, last))
    corrections = give_back(
        last_correction(lefts, scalars, steps_of(last), chunk, width, cols), last
    )
    for half, back in enumerate(backs):
        for step, piece in enumerate(back):
            sel_panel = lax.dynamic_update_slice(
                sel_panel, piece[None], (offsets[last] + (node ^ step), 0, 0, 0, half * cols)
            )
    for step, piece in enumerate(corrections):
        slot = offsets[last] + (node ^ step)
        own = lax.dynamic_index_in_dim(diag_inverse[0], slot, 0, keepdims=True)
        sel_diag = lax.dynamic_update_slice(sel_diag, own - piece[None], (slot, 0, 0, 0))
    return (sel_panel[None], sel_diag[None])


def solution(mesh):
    in_specs = (
        P("col", None, None, None, "row", None),
        P("col", None, None, "row", None),
        P("col", None, None),
    )
    out_specs = (P("col", None, None, None, "row", None), P("col", None, None, "row", None))
    return jax.shard_map(body, mesh=mesh, in_specs=in_specs, out_specs=out_specs, check_vma=False)
```

```python
import functools

import jax
import jax.numpy as jnp
from jax import lax
from jax.experimental import pallas as pl
from jax.experimental.pallas import tpu as pltpu
from jax.sharding import PartitionSpec as P

LEVELS = 6
HALVES = 2
VMEM_BYTES = 56 * 2**20
F32 = jnp.float32
BF16 = jnp.bfloat16
ANY = pl.BlockSpec(memory_space=pl.ANY)
VMEM = pl.BlockSpec(memory_space=pltpu.VMEM)
SMEM = pl.BlockSpec(memory_space=pltpu.SMEM)


def xor_swap(value, axis, mask):
    count = lax.axis_size(axis)
    return lax.ppermute(value, axis, [(source, source ^ mask) for source in range(count)])


def split(value):
    high = value.astype(BF16)
    return high, (value - high.astype(F32)).astype(BF16)


def three_products(left_high, left_low, right_high, right_low):
    left = jnp.concatenate([left_high, left_high, left_low], axis=1)
    right = jnp.concatenate([right_high, right_low, right_high], axis=0)
    return jnp.dot(left, right, preferred_element_type=F32)


def complex_sum(product, half):
    count = product.shape[0] // 2
    by_real, by_imag = product[:count], product[count:]
    return jnp.concatenate(
        [by_real[:, :half] - by_imag[:, half:], by_real[:, half:] + by_imag[:, :half]], axis=1
    )


def run_kernel(kernel, outs, ins, scratch, flops, aliases=None):
    moved = sum(value.size for value, _ in ins)
    return pl.pallas_call(
        kernel,
        out_shape=[jax.ShapeDtypeStruct(shape, dtype) for shape, dtype, _ in outs],
        in_specs=[spec for _, spec in ins],
        out_specs=[spec for _, _, spec in outs],
        scratch_shapes=scratch,
        input_output_aliases=aliases or {},
        compiler_params=pltpu.CompilerParams(vmem_limit_bytes=VMEM_BYTES),
        cost_estimate=pl.CostEstimate(flops=flops, bytes_accessed=2 * moved, transcendentals=0),
    )(*[value for value, _ in ins])


class Loads:
    def __init__(self, sources, buffers, sems):
        self.buffers = buffers
        self.copies = [
            pltpu.make_async_copy(source, buffer, sems.at[at])
            for at, (source, buffer) in enumerate(zip(sources, buffers))
        ]
        for copy in self.copies:
            copy.start()

    def get(self, at):
        if self.copies[at] is not None:
            self.copies[at].wait()
            self.copies[at] = None
        return self.buffers[at]


def both_parts(mask, array, base=0):
    return [(mask, 0, array, 2 * base, 2), (mask, 1, array, 2 * base + 1, 2)]


def pack_kernel(spans, plan, n_outs, chunk, *refs):
    scalars, present, panel_ref, diag_ref = refs[:4]
    outs = refs[4 : 4 + n_outs]
    panel_bufs = refs[4 + n_outs : -2]
    diag_buf, sems = refs[-2:]
    sources, buffers = [], []
    for (first, nodes, depth), buffer in zip(spans, panel_bufs):
        sources.append(panel_ref.at[0, pl.ds(first, nodes), pl.ds(0, depth)])
        buffers.append(buffer)
    if any(block == 0 for blocks in plan for _, _, block in blocks):
        sources.append(diag_ref.at[0])
        buffers.append(diag_buf)
    loads = Loads(sources, buffers, sems)
    where = {first: at for at, (first, _, _) in enumerate(spans)}
    for out, blocks in zip(outs, plan):
        for at, (first, node_of, block) in enumerate(blocks):
            node = node_of(scalars[0])
            if block == 0:
                value = loads.get(len(spans))[first + node]
            else:
                scale = present[first + node, block - 1].astype(F32)
                value = loads.get(where[first])[node, block - 1] * scale
            out[pl.ds(2 * at, 2)] = value


def pack(plan, spans, scalars, present, lower_panel, diag_inverse):
    chunk, width = lower_panel.shape[-2:]
    outs = [((2 * len(blocks), chunk, width), F32, VMEM) for blocks in plan]
    scratch = [pltpu.VMEM((nodes, depth, 2, chunk, width), F32) for _, nodes, depth in spans]
    scratch += [pltpu.VMEM(diag_inverse.shape[1:], F32), pltpu.SemaphoreType.DMA((len(spans) + 1,))]
    kernel = functools.partial(pack_kernel, spans, plan, len(outs), chunk)
    ins = [(scalars, SMEM), (present, SMEM), (lower_panel, ANY), (diag_inverse, ANY)]
    return run_kernel(kernel, outs, ins, scratch, 0)


def pack_last_kernel(first, nodes, depth, steps, cols, *refs):
    scalars, present, panel_ref = refs[:3]
    outs = refs[3 : 3 + len(steps) * HALVES]
    buffer, sem = refs[-2:]
    copy = pltpu.make_async_copy(panel_ref.at[0, pl.ds(first, nodes), pl.ds(0, depth)], buffer, sem)
    copy.start()
    copy.wait()
    for at, (step, group) in enumerate(steps):
        node = (scalars[0] // group) ^ step
        for block in range(depth):
            value = buffer[node, block] * present[first + node, block].astype(F32)
            for half in range(HALVES):
                outs[half * len(steps) + at][pl.ds(2 * block, 2)] = value[
                    :, :, half * cols : (half + 1) * cols
                ]


def pack_last(first, nodes, depth, steps, cols, scalars, present, lower_panel):
    chunk, width = lower_panel.shape[-2:]
    outs = [((2 * depth, chunk, cols), F32, VMEM)] * (len(steps) * HALVES)
    scratch = [pltpu.VMEM((nodes, depth, 2, chunk, width), F32), pltpu.SemaphoreType.DMA]
    kernel = functools.partial(pack_last_kernel, first, nodes, depth, steps, cols)
    ins = [(scalars, SMEM), (present, SMEM), (lower_panel, ANY)]
    return run_kernel(kernel, outs, ins, scratch, 0)


def prep_kernel(levels, table, chunk, width, n_arrays, *refs):
    scalars = refs[0]
    arrays = refs[1 : 1 + n_arrays]
    outs = list(refs[1 + n_arrays :])
    place = scalars[0]
    odd = scalars[1] == 1
    for depth, swapped, first in levels:
        if depth:
            whole, fwd_high, fwd_low = outs.pop(0), outs.pop(0), outs.pop(0)
        else:
            whole = None
        back_high, back_low = outs.pop(0), outs.pop(0)
        for block in range(depth + 1):
            for mask, part, position, base, stride in table:
                plane = base + stride * (first + block)
                if swapped is None:
                    value = arrays[position][plane]
                else:
                    half = n_arrays // 2
                    from_odd = arrays[position + (0 if swapped else half)]
                    from_even = arrays[position + (half if swapped else 0)]
                    value = jnp.where(odd, from_odd[plane], from_even[plane])
                start = pl.multiple_of((place ^ mask) * chunk, chunk)
                if block == 0:
                    high, low = split(value)
                    lanes = pl.ds(depth * width, width)
                    rows = pl.ds(pl.multiple_of(part * width + start, chunk), chunk)
                    back_high[rows, lanes] = high
                    back_low[rows, lanes] = low
                else:
                    rows = pl.ds(pl.multiple_of((depth - block) * width + start, chunk), chunk)
                    whole[rows, pl.ds(part * width, width)] = value
        for level in range(depth):
            for part in range(2):
                value = whole[pl.ds(level * width, width), pl.ds(part * width, width)]
                high, low = split(value)
                rows = pl.ds((2 * level + part) * width, width)
                fwd_high[rows] = high
                fwd_low[rows] = low
                high, low = split(-value.T)
                rows, lanes = pl.ds(part * width, width), pl.ds(level * width, width)
                back_high[rows, lanes] = high
                back_low[rows, lanes] = low


def prep(levels, pieces, scalars, chunk, width, others=()):
    arrays, table = [], []
    for mask, part, array, base, stride in pieces:
        position = next((at for at, value in enumerate(arrays) if value is array), None)
        if position is None:
            position = len(arrays)
            arrays.append(array)
        table.append((mask, part, position, base, stride))
    arrays = arrays + list(others)
    outs = []
    for depth, _, _ in levels:
        if depth:
            outs.append(((depth * width, 2 * width), F32, VMEM))
            outs += [((2 * depth * width, width), BF16, VMEM)] * 2
        outs += [((2 * width, (depth + 1) * width), BF16, VMEM)] * 2
    kernel = functools.partial(prep_kernel, levels, table, chunk, width, len(arrays))
    ins = [(scalars, SMEM)] + [(value, VMEM) for value in arrays]
    made = list(run_kernel(kernel, outs, ins, [], 0))
    result = {}
    for depth, _, _ in levels:
        if depth:
            result[depth], made = tuple(made[:5]), made[5:]
        else:
            result[depth], made = (None, None, None) + tuple(made[:2]), made[2:]
    return result


def substitute(depth, width, cols, forward, backward, sums, right_high, right_low, emit):
    def rows(first, count=1):
        return pl.ds(first * width, count * width)

    for level in range(depth - 1, 0, -1):
        high, low = split(sums[rows(level)])
        right_high[rows(level)] = high
        right_low[rows(level)] = low
        fwd_high, fwd_low = forward(level)
        for block in range(level - 1, -1, -1):
            product = three_products(
                fwd_high[rows(2 * block, 2)], fwd_low[rows(2 * block, 2)], high, low
            )
            sums[rows(block)] -= complex_sum(product, cols)
    high, low = split(sums[rows(0)])
    right_high[rows(0)] = high
    right_low[rows(0)] = low
    for level in range(depth):
        back_high, back_low = backward(level)
        product = three_products(
            back_high[...],
            back_low[...],
            right_high[rows(0, level + 1)],
            right_low[rows(0, level + 1)],
        )
        solved = complex_sum(product, cols)
        high, low = split(solved)
        right_high[rows(level)] = high
        right_low[rows(level)] = low
        emit(level, solved)


def solve_kernel(depths, chunk, width, steps, order, masked, *refs):
    refs = list(refs)
    scalars = refs.pop(0)
    sources = [refs.pop(0) for _ in order]
    outs = {depth: [(refs.pop(0), refs.pop(0)) for _ in steps] for depth in depths}
    buffers = [refs.pop(0) for _ in order]
    sems, sums_ref, high_ref, low_ref, solved_ref = refs
    loads = Loads(sources, buffers, sems)

    def get(kind, level):
        return loads.get(order.index((kind, level)))

    place = scalars[0]
    for depth in depths:
        span = pl.ds(0, depth * width)
        sums, right_high, right_low = sums_ref.at[span], high_ref.at[span], low_ref.at[span]
        sums[...] = get("whole", depth)[...]

        def send(block, value, sign):
            solved_ref[...] = value
            for (out, correction), step in zip(outs[depth], steps):
                start = pl.multiple_of((place ^ step) * chunk, chunk)
                piece = solved_ref[pl.ds(start, chunk)] * sign
                if depth in masked:
                    piece = jnp.where(scalars[2 + depth] == 1, piece, 0.0)
                for part in range(2):
                    plane = piece[:, part * width : (part + 1) * width]
                    if block == 0:
                        correction[part] = plane
                    else:
                        out[block - 1, part] = plane

        substitute(
            depth, width, width,
            lambda level: (get("fh", level), get("fl", level)),
            lambda level: (get("bh", level), get("bl", level)),
            sums, right_high, right_low,
            lambda level, solved: send(depth - level, solved, -1.0),
        )
        back_high, back_low = get("bh", depth), get("bl", depth)
        product = three_products(
            back_high[:, : depth * width], back_low[:, : depth * width],
            right_high[...], right_low[...],
        )
        send(0, complex_sum(product, width), 1.0)


def operands(made, names):
    index = {"whole": 0, "fh": 1, "fl": 2, "bh": 3, "bl": 4}
    return [made[level][index[kind]] for kind, level in names]


def solve(depths, made, scalars, steps, chunk, width, masked):
    top = depths[0]
    order = [("whole", top)]
    for level in range(top - 1, 0, -1):
        order += [("fh", level), ("fl", level)]
    for level in range(top + 1):
        order += [("bh", level), ("bl", level)]
    order += [("whole", depth) for depth in depths[1:]]
    sources = operands(made, order)
    outs = []
    for depth in depths:
        for _ in steps:
            outs.append(((depth, 2, chunk, width), F32, VMEM))
            outs.append(((2, chunk, width), F32, VMEM))
    scratch = [pltpu.VMEM(value.shape, value.dtype) for value in sources]
    scratch += [
        pltpu.SemaphoreType.DMA((len(order),)),
        pltpu.VMEM((top * width, 2 * width), F32),
        pltpu.VMEM((top * width, 2 * width), BF16),
        pltpu.VMEM((top * width, 2 * width), BF16),
        pltpu.VMEM((width, 2 * width), F32),
    ]
    kernel = functools.partial(solve_kernel, depths, chunk, width, steps, order, masked)
    flops = sum(24 * (depth * depth + depth) * width**3 for depth in depths)
    ins = [(scalars, SMEM)] + [(value, ANY) for value in sources]
    got = list(run_kernel(kernel, outs, ins, scratch, flops))
    result = {}
    for depth in depths:
        result[depth] = [(got.pop(0), got.pop(0)) for _ in steps]
    return result


def last_kernel(depth, chunk, width, cols, steps, table, n_arrays, order, *refs):
    refs = list(refs)
    scalars = refs.pop(0)
    arrays = [refs.pop(0) for _ in range(n_arrays)]
    sources = [refs.pop(0) for _ in order]
    outs = [refs.pop(0) for _ in steps]
    left_high, left_low, right_high, right_low = (refs.pop(0) for _ in range(4))
    buffers = [refs.pop(0) for _ in order]
    sems, sums, solved_ref = refs
    loads = Loads(sources, buffers, sems)

    def get(kind, level):
        return loads.get(order.index((kind, level)))

    place = scalars[0]
    for mask, part, position, base, stride in table:
        start = pl.multiple_of((place ^ mask) * chunk, chunk)
        for block in range(depth):
            row = pl.multiple_of((depth - 1 - block) * width + start, chunk)
            sums[pl.ds(row, chunk), pl.ds(part * cols, cols)] = arrays[position][base + stride * block]
    for level in range(depth):
        for part in range(2):
            value = sums[pl.ds(level * width, width), pl.ds(part * cols, cols)]
            high, low = split(value.T)
            rows, lanes = pl.ds(part * cols, cols), pl.ds(level * width, width)
            left_high[rows, lanes] = high
            left_low[rows, lanes] = low

    def emit(level, value):
        solved_ref[...] = value
        for out, step in zip(outs, steps):
            start = pl.multiple_of((place ^ step) * chunk, chunk)
            piece = -solved_ref[pl.ds(start, chunk)]
            out[depth - 1 - level, 0] = piece[:, :cols]
            out[depth - 1 - level, 1] = piece[:, cols:]

    substitute(
        depth, width, cols,
        lambda level: (get("fh", level), get("fl", level)),
        lambda level: (get("bh", level), get("bl", level)),
        sums, right_high, right_low, emit,
    )


def solve_last(depth, made, pieces, scalars, steps, chunk, width, cols):
    arrays, table = [], []
    for mask, part, array, base, stride in pieces:
        position = next((at for at, value in enumerate(arrays) if value is array), None)
        if position is None:
            position = len(arrays)
            arrays.append(array)
        table.append((mask, part, position, base, stride))
    order = []
    for level in range(depth - 1, 0, -1):
        order += [("fh", level), ("fl", level)]
    for level in range(depth):
        order += [("bh", level), ("bl", level)]
    sources = operands(made, order)
    outs = [((depth, 2, chunk, cols), F32, VMEM)] * len(steps)
    outs += [((2 * cols, depth * width), BF16, VMEM)] * 2
    outs += [((depth * width, 2 * cols), BF16, VMEM)] * 2
    scratch = [pltpu.VMEM(value.shape, value.dtype) for value in sources]
    scratch += [
        pltpu.SemaphoreType.DMA((len(order),)),
        pltpu.VMEM((depth * width, 2 * cols), F32),
        pltpu.VMEM((width, 2 * cols), F32),
    ]
    kernel = functools.partial(
        last_kernel, depth, chunk, width, cols, steps, table, len(arrays), order
    )
    flops = 24 * depth * depth * width * width * cols
    ins = [(scalars, SMEM)] + [(value, VMEM) for value in arrays]
    ins += [(value, ANY) for value in sources]
    got = run_kernel(kernel, outs, ins, scratch, flops)
    return got[: len(steps)], got[len(steps) :]


def correction_kernel(chunk, width, cols, steps, parts, *refs):
    refs = list(refs)
    scalars = refs.pop(0)
    lefts = [tuple(refs.pop(0) for _ in range(4)) for _ in range(parts)]
    outs = [refs.pop(0) for _ in steps]
    (total,) = refs
    place = scalars[0]
    product = three_products(
        jnp.concatenate([left[0][...] for left in lefts], axis=0),
        jnp.concatenate([left[1][...] for left in lefts], axis=0),
        jnp.concatenate([left[2][...] for left in lefts], axis=1),
        jnp.concatenate([left[3][...] for left in lefts], axis=1),
    )
    size = 2 * cols
    for row in range(parts):
        for col in range(parts):
            block = product[row * size : (row + 1) * size, col * size : (col + 1) * size]
            block = -complex_sum(block, cols)
            rows, lanes = pl.ds(row * cols, cols), pl.ds(col * cols, cols)
            total[0, rows, lanes] = block[:, :cols]
            total[1, rows, lanes] = block[:, cols:]
    for out, step in zip(outs, steps):
        start = pl.multiple_of((place ^ step) * chunk, chunk)
        out[0] = total[0, pl.ds(start, chunk)]
        out[1] = total[1, pl.ds(start, chunk)]


def last_correction(lefts, scalars, steps, chunk, width, cols):
    outs = [((2, chunk, width), F32, VMEM)] * len(steps)
    kernel = functools.partial(correction_kernel, chunk, width, cols, steps, len(lefts))
    flops = 24 * lefts[0][2].shape[0] * width * width
    ins = [(scalars, SMEM)] + [(value, VMEM) for left in lefts for value in left]
    return run_kernel(kernel, outs, ins, [pltpu.VMEM((2, width, width), F32)], flops)


def begin_kernel(plan, zeros, *refs):
    scalars = refs[0]
    pieces = refs[1 : 1 + len(plan)]
    out, zero_ref, sem = refs[1 + len(plan) :]
    zero_ref[...] = jnp.zeros_like(zero_ref)
    copies = []
    for slot, depth, count in zeros:
        copies.append((zero_ref.at[pl.ds(0, count)], out.at[0, slot, pl.ds(depth, count)]))
    for piece, (first, group, step, depth) in zip(pieces, plan):
        slot = first + ((scalars[0] // group) ^ step)
        copies.append((piece, out.at[0, slot, pl.ds(0, depth)]))
    copies = [
        pltpu.make_async_copy(source, target, sem.at[at])
        for at, (source, target) in enumerate(copies)
    ]
    for copy in copies:
        copy.start()
    for copy in copies:
        copy.wait()


def place_kernel(plan, cols, half, *refs):
    scalars = refs[0]
    pieces = refs[1 : 1 + len(plan)]
    out, sem = refs[-2:]
    copies = []
    for at, (piece, (first, group, step)) in enumerate(zip(pieces, plan)):
        slot = first + ((scalars[0] // group) ^ step)
        target = out.at[0, slot, :, :, :, pl.ds(half * cols, cols)]
        copies.append(pltpu.make_async_copy(piece, target, sem.at[at]))
    for copy in copies:
        copy.start()
    for copy in copies:
        copy.wait()


def diagonal_kernel(plan, shared, *refs):
    scalars, own = refs[:2]
    pieces = refs[2 : 2 + len(plan)]
    out = refs[-1]
    for slot in range(out.shape[1]):
        value = own[0, slot]
        if slot in shared:
            value = jnp.where(scalars[2 + shared[slot]] == 1, value, 0.0)
        out[0, slot] = value
    for piece, (first, group, step) in zip(pieces, plan):
        slot = first + ((scalars[0] // group) ^ step)
        out[0, slot] = out[0, slot] - piece[...]


def body(lower_panel, diag_inverse, structure):
    columns = lax.axis_size("col")
    rows = lax.axis_size("row")
    position = lax.axis_index("col")
    place = lax.axis_index("row")
    slots, anc_count, _, chunk, width = lower_panel.shape[1:]
    per_col = [max(1, 2**depth // columns) for depth in range(LEVELS)]
    offsets = [sum(per_col[:depth]) for depth in range(LEVELS)]
    last = LEVELS - 1
    cols = width // HALVES
    groups = [rows // nodes for nodes in per_col]
    steps = [[step * groups[depth] for step in range(per_col[depth])] for depth in range(LEVELS)]
    shared = [depth for depth in range(LEVELS) if 2**depth < columns]
    middle = [depth for depth in range(LEVELS - 1) if 2**depth >= columns]
    active = [position % max(1, columns // 2**depth) == 0 for depth in range(LEVELS)]
    scalars = jnp.stack([place, position % 2] + active).astype(jnp.int32)
    present = structure[0]

    upper = shared[:-1]
    starts = [sum(1 + depth for depth in upper[:at]) for at in range(len(upper))]

    def level_blocks(depth, step=0):
        group = groups[depth]
        return [
            (offsets[depth], lambda at, group=group, step=step: (at // group) ^ step, block)
            for block in range(depth + 1)
        ]

    near_plan, far_plan = [], []
    bases = {}
    for depth in middle:
        bases[depth] = len(near_plan)
        near_plan += level_blocks(depth)
        far_plan += level_blocks(depth, 0 if groups[depth] > 2 else 1)
    plan = [sum([level_blocks(depth) for depth in upper], []), level_blocks(shared[-1])]
    if middle:
        plan += [near_plan, far_plan]
    spans = [
        (offsets[depth], per_col[depth], depth) for depth in shared[1:] + middle
    ]
    packed = list(pack(plan, spans, scalars, present, lower_panel, diag_inverse))
    upper_pack, own_pack = packed[:2]

    stride = columns // 2
    while stride >= 4:
        held = [at for at, depth in enumerate(upper) if columns // 2**depth >= 2 * stride]
        count = 2 * (starts[held[-1]] + 1 + upper[held[-1]])
        pairs = [(source, source + stride) for source in range(0, columns, 2 * stride)]
        if stride == columns // 2 and count == 2:
            travelling = diag_inverse[0, 0]
        else:
            travelling = upper_pack[:count]
        arrived = lax.ppermute(travelling, "col", pairs)
        fresh = position % (2 * stride) == stride
        upper_pack = jnp.concatenate(
            [jnp.where(fresh, arrived, upper_pack[:count]), upper_pack[count:]], axis=0
        )
        stride //= 2
    from_one = lax.ppermute(
        upper_pack, "col", [(source, source + 1) for source in range(0, columns, 4)]
    )
    from_three = lax.ppermute(
        upper_pack, "col", [(source, source + 3) for source in range(0, columns, 4)]
    )
    upper_got = jnp.where(position % 4 == 1, from_one, from_three)
    planes = max(own_pack.shape[0], upper_got.shape[0])

    def fill(value):
        return jnp.pad(value, ((0, planes - value.shape[0]), (0, 0), (0, 0)))

    own = jnp.where(position % 2 == 1, fill(upper_got), fill(own_pack))

    if middle:
        near_pack, far_pack = packed[2:]
        near_got = xor_swap(near_pack, "row", 1)
        far_got = xor_swap(far_pack, "row", 2)
    near = xor_swap(own, "row", 1)
    far = xor_swap(own, "row", 2)
    far_split = far.reshape(planes // 2, 2, chunk, width)
    near_split = near.reshape(planes // 2, 2, chunk, width)
    near_sends, far_sends = [far_split[:, 0]], [near_split[:, 1]]
    homes = {}
    near_size = far_size = planes // 2
    for depth in middle:
        first, count = 2 * bases[depth], 2 * (depth + 1)
        homes[depth] = (near_size, far_size)
        if groups[depth] > 2:
            far_level = far_got[first : first + count].reshape(depth + 1, 2, chunk, width)
            near_level = near_got[first : first + count].reshape(depth + 1, 2, chunk, width)
            near_sends.append(far_level[:, 0])
            far_sends.append(near_level[:, 1])
            near_size += depth + 1
            far_size += depth + 1
        else:
            near_sends.append(far_got[first : first + count])
            near_size += count
    near_more = xor_swap(jnp.concatenate(near_sends, axis=0), "row", 1)
    far_more = xor_swap(jnp.concatenate(far_sends, axis=0), "row", 2)

    blocks = planes // 2
    mine = jnp.concatenate([own, near, far, near_more[:blocks], far_more[:blocks]], axis=0)
    theirs = xor_swap(mine, "col", 1)
    shared_pieces = (
        both_parts(0, mine)
        + both_parts(1, mine, blocks)
        + both_parts(2, mine, 2 * blocks)
        + [(3, 0, mine, 6 * blocks, 1), (3, 1, mine, 7 * blocks, 1)]
    )

    made = {}
    for depth in middle:
        base = bases[depth]
        near_home, far_home = homes[depth]
        pieces = both_parts(0, near_pack, base) + both_parts(1, near_got, base)
        pieces += both_parts(2, far_got, base)
        if groups[depth] > 2:
            pieces += [(3, 0, near_more, near_home, 1), (3, 1, far_more, far_home, 1)]
        else:
            pieces += [(3, 0, near_more, near_home, 2), (3, 1, near_more, near_home + 1, 2)]
        made.update(prep([(depth, None, 0)], pieces, scalars, chunk, width))
    levels = [(depth, True, starts[at]) for at, depth in enumerate(upper)]
    levels.append((shared[-1], False, 0))
    made.update(prep(levels, shared_pieces, scalars, chunk, width, others=[theirs]))

    nodes, group = per_col[last], groups[last]
    last_packs = pack_last(
        offsets[last], nodes, last, [(step, group) for step in range(nodes)], cols,
        scalars, present, lower_panel,
    )
    last_pieces = []
    for half in range(HALVES):
        packs = last_packs[half * nodes : (half + 1) * nodes]
        if half == 0:
            packs, _ = lax.optimization_barrier((packs, near))
        else:
            packs, _ = lax.optimization_barrier((packs, near_more))
        pieces = []
        for step, value in zip(steps[last], packs):
            arrived = xor_swap(value, "row", step) if step else value
            if group == 1:
                pieces += both_parts(step, arrived)
                continue
            listed = [(step, arrived)]
            mask = 1
            while mask < group:
                listed += [(mask | at, xor_swap(held, "row", mask)) for at, held in listed]
                mask *= 2
            for at, held in listed:
                pieces += both_parts(at, held)
        last_pieces.append(pieces)

    lefts, backs = [], []
    for half in range(HALVES):
        outward, left = solve_last(
            last, made, last_pieces[half], scalars, steps[last], chunk, width, cols
        )
        lefts.append(left)
        backs.append(
            [xor_swap(piece, "row", step) if step else piece for piece, step in zip(outward, steps[last])]
        )
    corrections = last_correction(lefts, scalars, steps[last], chunk, width, cols)
    corrections = [
        xor_swap(piece, "row", step) if step else piece
        for piece, step in zip(corrections, steps[last])
    ]

    single = [depth for depth in range(last - 1, 0, -1) if per_col[depth] == 1]
    solved = {}
    for depth in range(1, last):
        if per_col[depth] > 1:
            solved.update(solve([depth], made, scalars, steps[depth], chunk, width, ()))
    solved.update(solve(single, made, scalars, [0], chunk, width, tuple(shared)))

    begin_plan, begin_pieces, diag_plan, diag_pieces = [], [], [], []
    for depth in range(1, last):
        for step, (piece, correction) in enumerate(solved[depth]):
            if step:
                both = jnp.concatenate([piece, correction[None]], axis=0)
                both = xor_swap(both, "row", steps[depth][step])
                piece, correction = both[:depth], both[depth]
            begin_plan.append((offsets[depth], groups[depth], step, depth))
            begin_pieces.append(piece)
            diag_plan.append((offsets[depth], groups[depth], step))
            diag_pieces.append(correction)
    zeros = [
        (offsets[depth] + node, depth, anc_count - depth)
        for depth in range(LEVELS)
        for node in range(per_col[depth])
        if depth < anc_count
    ]
    panel_shape = lower_panel.shape
    (sel_panel,) = run_kernel(
        functools.partial(begin_kernel, begin_plan, zeros),
        [(panel_shape, F32, ANY)],
        [(scalars, SMEM)] + [(piece, VMEM) for piece in begin_pieces],
        [
            pltpu.VMEM((anc_count, 2, chunk, width), F32),
            pltpu.SemaphoreType.DMA((len(zeros) + len(begin_plan),)),
        ],
        0,
    )
    last_plan = [(offsets[last], group, step) for step in range(nodes)]
    for half, back in enumerate(backs):
        def write(scalar_ref, *refs, half=half):
            place_kernel(last_plan, cols, half, scalar_ref, *refs[:nodes], *refs[nodes + 1 :])

        (sel_panel,) = run_kernel(
            write,
            [(panel_shape, F32, ANY)],
            [(scalars, SMEM)] + [(piece, ANY) for piece in back] + [(sel_panel, ANY)],
            [pltpu.SemaphoreType.DMA((nodes,))],
            0,
            aliases={1 + nodes: 0},
        )
    diag_plan += last_plan
    diag_pieces += list(corrections)
    (sel_diag,) = run_kernel(
        functools.partial(diagonal_kernel, diag_plan, {offsets[depth]: depth for depth in shared}),
        [(diag_inverse.shape, F32, VMEM)],
        [(scalars, SMEM), (diag_inverse, VMEM)] + [(piece, VMEM) for piece in diag_pieces],
        [],
        0,
    )
    return (sel_panel, sel_diag)


def solution(mesh):
    in_specs = (
        P("col", None, None, None, "row", None),
        P("col", None, None, "row", None),
        P("col", None, None),
    )
    out_specs = (P("col", None, None, None, "row", None), P("col", None, None, "row", None))
    return jax.shard_map(body, mesh=mesh, in_specs=in_specs, out_specs=out_specs, check_vma=False)
```

```python
import functools

import jax
import jax.numpy as jnp
from jax import lax
from jax.experimental import pallas as pl
from jax.experimental.pallas import tpu as pltpu
from jax.sharding import PartitionSpec as P

LEVELS = 6
HALVES = 2
VMEM_BYTES = 24 * 2**20
F32 = jnp.float32
BF16 = jnp.bfloat16
ANY = pl.BlockSpec(memory_space=pl.ANY)
VMEM = pl.BlockSpec(memory_space=pltpu.VMEM)
SMEM = pl.BlockSpec(memory_space=pltpu.SMEM)


def turned(mask, rows):
    if rows < 4:
        return mask
    return (mask & ~3) | ((mask & 1) << 1) | ((mask >> 1) & 1)


def col_swap(value):
    count = lax.axis_size("col")
    return lax.ppermute(value, "col", [(source, source ^ 1) for source in range(count)])


def row_swap(value, mask):
    rows, columns = lax.axis_size("row"), lax.axis_size("col")
    pairs = []
    for row in range(rows):
        for col in range(columns):
            other = row ^ (turned(mask, rows) if col % 2 else mask)
            pairs.append((row * columns + col, other * columns + col))
    return lax.ppermute(value, ("row", "col"), pairs)


def rows_of(scalars, mask, chunk):
    away = mask & ~3
    if mask & 1:
        away = away | scalars[3]
    if mask & 2:
        away = away | scalars[4]
    return pl.multiple_of((scalars[0] ^ away) * chunk, chunk)


def split(value):
    high = value.astype(BF16)
    return high, (value - high.astype(F32)).astype(BF16)


def three_products(left_high, left_low, right_high, right_low):
    left = jnp.concatenate([left_high, left_high, left_low], axis=1)
    right = jnp.concatenate([right_high, right_low, right_high], axis=0)
    return jnp.dot(left, right, preferred_element_type=F32)


def complex_sum(product, half):
    count = product.shape[0] // 2
    by_real, by_imag = product[:count], product[count:]
    return jnp.concatenate(
        [by_real[:, :half] - by_imag[:, half:], by_real[:, half:] + by_imag[:, :half]], axis=1
    )


def run_kernel(kernel, outs, ins, scratch, flops, aliases=None):
    moved = sum(value.size for value, _ in ins)
    return pl.pallas_call(
        kernel,
        out_shape=[jax.ShapeDtypeStruct(shape, dtype) for shape, dtype, _ in outs],
        in_specs=[spec for _, spec in ins],
        out_specs=[spec for _, _, spec in outs],
        scratch_shapes=scratch,
        input_output_aliases=aliases or {},
        compiler_params=pltpu.CompilerParams(vmem_limit_bytes=VMEM_BYTES),
        cost_estimate=pl.CostEstimate(flops=flops, bytes_accessed=2 * moved, transcendentals=0),
    )(*[value for value, _ in ins])


class Loads:
    def __init__(self, sources, buffers, sems):
        self.buffers = buffers
        self.copies = [
            pltpu.make_async_copy(source, buffer, sems.at[at])
            for at, (source, buffer) in enumerate(zip(sources, buffers))
        ]
        for copy in self.copies:
            copy.start()

    def get(self, at):
        if self.copies[at] is not None:
            self.copies[at].wait()
            self.copies[at] = None
        return self.buffers[at]


def both_parts(mask, array, base=0):
    return [(mask, 0, array, 2 * base, 2), (mask, 1, array, 2 * base + 1, 2)]


def pack_kernel(spans, plan, n_outs, chunk, *refs):
    scalars, present, panel_ref, diag_ref = refs[:4]
    outs = refs[4 : 4 + n_outs]
    panel_bufs = refs[4 + n_outs : -2]
    diag_buf, sems = refs[-2:]
    sources, buffers = [], []
    for (first, nodes, depth), buffer in zip(spans, panel_bufs):
        sources.append(panel_ref.at[0, pl.ds(first, nodes), pl.ds(0, depth)])
        buffers.append(buffer)
    if any(block == 0 for blocks in plan for _, _, block in blocks):
        sources.append(diag_ref.at[0])
        buffers.append(diag_buf)
    loads = Loads(sources, buffers, sems)
    where = {first: at for at, (first, _, _) in enumerate(spans)}
    for out, blocks in zip(outs, plan):
        for at, (first, node_of, block) in enumerate(blocks):
            node = node_of(scalars[2])
            if block == 0:
                value = loads.get(len(spans))[first + node]
            else:
                scale = present[first + node, block - 1].astype(F32)
                value = loads.get(where[first])[node, block - 1] * scale
            out[pl.ds(2 * at, 2)] = value


def pack(plan, spans, scalars, present, lower_panel, diag_inverse):
    chunk, width = lower_panel.shape[-2:]
    outs = [((2 * len(blocks), chunk, width), F32, VMEM) for blocks in plan]
    scratch = [pltpu.VMEM((nodes, depth, 2, chunk, width), F32) for _, nodes, depth in spans]
    scratch += [pltpu.VMEM(diag_inverse.shape[1:], F32), pltpu.SemaphoreType.DMA((len(spans) + 1,))]
    kernel = functools.partial(pack_kernel, spans, plan, len(outs), chunk)
    ins = [(scalars, SMEM), (present, SMEM), (lower_panel, ANY), (diag_inverse, ANY)]
    return run_kernel(kernel, outs, ins, scratch, 0)


def pack_last_kernel(first, nodes, depth, steps, cols, *refs):
    scalars, present, panel_ref = refs[:3]
    outs = refs[3 : 3 + len(steps) * HALVES]
    buffer, sem = refs[-2:]
    copy = pltpu.make_async_copy(panel_ref.at[0, pl.ds(first, nodes), pl.ds(0, depth)], buffer, sem)
    copy.start()
    copy.wait()
    for at, (step, group) in enumerate(steps):
        node = (scalars[2] // group) ^ step
        for block in range(depth):
            value = buffer[node, block] * present[first + node, block].astype(F32)
            for half in range(HALVES):
                outs[half * len(steps) + at][pl.ds(2 * block, 2)] = value[
                    :, :, half * cols : (half + 1) * cols
                ]


def pack_last(first, nodes, depth, steps, cols, scalars, present, lower_panel):
    chunk, width = lower_panel.shape[-2:]
    outs = [((2 * depth, chunk, cols), F32, VMEM)] * (len(steps) * HALVES)
    scratch = [pltpu.VMEM((nodes, depth, 2, chunk, width), F32), pltpu.SemaphoreType.DMA]
    kernel = functools.partial(pack_last_kernel, first, nodes, depth, steps, cols)
    ins = [(scalars, SMEM), (present, SMEM), (lower_panel, ANY)]
    return run_kernel(kernel, outs, ins, scratch, 0)


def prep_kernel(levels, table, rows_count, chunk, width, n_arrays, *refs):
    scalars = refs[0]
    arrays = refs[1 : 1 + n_arrays]
    outs = list(refs[1 + n_arrays :])
    odd = scalars[1] == 1
    for depth, swapped, first in levels:
        if depth:
            whole, fwd_high, fwd_low = outs.pop(0), outs.pop(0), outs.pop(0)
        else:
            whole = None
        back_high, back_low = outs.pop(0), outs.pop(0)
        for block in range(depth + 1):
            for mask, part, position, base, stride in table:
                plane = base + stride * (first + block)
                start = rows_of(scalars, mask, chunk)
                if swapped is None:
                    value = arrays[position][plane]
                else:
                    half = n_arrays // 2
                    from_odd = arrays[position + (0 if swapped else half)]
                    from_even = arrays[position + (half if swapped else 0)]
                    value = jnp.where(odd, from_odd[plane], from_even[plane])
                    away = turned(mask, rows_count) if swapped else mask
                    start = pl.multiple_of((scalars[0] ^ away) * chunk, chunk)
                if block == 0:
                    high, low = split(value)
                    lanes = pl.ds(depth * width, width)
                    rows = pl.ds(pl.multiple_of(part * width + start, chunk), chunk)
                    back_high[rows, lanes] = high
                    back_low[rows, lanes] = low
                else:
                    rows = pl.ds(pl.multiple_of((depth - block) * width + start, chunk), chunk)
                    whole[rows, pl.ds(part * width, width)] = value
        for level in range(depth):
            for part in range(2):
                value = whole[pl.ds(level * width, width), pl.ds(part * width, width)]
                high, low = split(value)
                rows = pl.ds((2 * level + part) * width, width)
                fwd_high[rows] = high
                fwd_low[rows] = low
                high, low = split(-value.T)
                rows, lanes = pl.ds(part * width, width), pl.ds(level * width, width)
                back_high[rows, lanes] = high
                back_low[rows, lanes] = low


def prep(levels, pieces, scalars, rows, chunk, width, others=()):
    arrays, table = [], []
    for mask, part, array, base, stride in pieces:
        position = next((at for at, value in enumerate(arrays) if value is array), None)
        if position is None:
            position = len(arrays)
            arrays.append(array)
        table.append((mask, part, position, base, stride))
    arrays = arrays + list(others)
    outs = []
    for depth, _, _ in levels:
        if depth:
            outs.append(((depth * width, 2 * width), F32, VMEM))
            outs += [((2 * depth * width, width), BF16, VMEM)] * 2
        outs += [((2 * width, (depth + 1) * width), BF16, VMEM)] * 2
    kernel = functools.partial(prep_kernel, levels, table, rows, chunk, width, len(arrays))
    ins = [(scalars, SMEM)] + [(value, VMEM) for value in arrays]
    made = list(run_kernel(kernel, outs, ins, [], 0))
    result = {}
    for depth, _, _ in levels:
        if depth:
            result[depth], made = tuple(made[:5]), made[5:]
        else:
            result[depth], made = (None, None, None) + tuple(made[:2]), made[2:]
    return result


def substitute(depth, width, cols, forward, backward, sums, right_high, right_low, emit):
    def rows(first, count=1):
        return pl.ds(first * width, count * width)

    for level in range(depth - 1, 0, -1):
        high, low = split(sums[rows(level)])
        right_high[rows(level)] = high
        right_low[rows(level)] = low
        fwd_high, fwd_low = forward(level)
        for block in range(level - 1, -1, -1):
            product = three_products(
                fwd_high[rows(2 * block, 2)], fwd_low[rows(2 * block, 2)], high, low
            )
            sums[rows(block)] -= complex_sum(product, cols)
    high, low = split(sums[rows(0)])
    right_high[rows(0)] = high
    right_low[rows(0)] = low
    for level in range(depth):
        back_high, back_low = backward(level)
        product = three_products(
            back_high[...],
            back_low[...],
            right_high[rows(0, level + 1)],
            right_low[rows(0, level + 1)],
        )
        solved = complex_sum(product, cols)
        high, low = split(solved)
        right_high[rows(level)] = high
        right_low[rows(level)] = low
        emit(level, solved)


def solve_kernel(depths, chunk, width, steps, order, masked, *refs):
    refs = list(refs)
    scalars = refs.pop(0)
    sources = [refs.pop(0) for _ in order]
    outs = {depth: [(refs.pop(0), refs.pop(0)) for _ in steps] for depth in depths}
    sums_ref, high_ref, low_ref, solved_ref = refs

    def get(kind, level):
        return sources[order.index((kind, level))]

    for depth in depths:
        span = pl.ds(0, depth * width)
        sums, right_high, right_low = sums_ref.at[span], high_ref.at[span], low_ref.at[span]
        sums[...] = get("whole", depth)[...]

        def send(block, value, sign):
            solved_ref[...] = value
            for (out, correction), step in zip(outs[depth], steps):
                start = rows_of(scalars, step, chunk)
                piece = solved_ref[pl.ds(start, chunk)] * sign
                if depth in masked:
                    piece = jnp.where(scalars[5 + depth] == 1, piece, 0.0)
                for part in range(2):
                    plane = piece[:, part * width : (part + 1) * width]
                    if block == 0:
                        correction[part] = plane
                    else:
                        out[block - 1, part] = plane

        substitute(
            depth, width, width,
            lambda level: (get("fh", level), get("fl", level)),
            lambda level: (get("bh", level), get("bl", level)),
            sums, right_high, right_low,
            lambda level, solved: send(depth - level, solved, -1.0),
        )
        back_high, back_low = get("bh", depth), get("bl", depth)
        product = three_products(
            back_high[:, : depth * width], back_low[:, : depth * width],
            right_high[...], right_low[...],
        )
        send(0, complex_sum(product, width), 1.0)


def operands(made, names):
    index = {"whole": 0, "fh": 1, "fl": 2, "bh": 3, "bl": 4}
    return [made[level][index[kind]] for kind, level in names]


def solve(depths, made, scalars, steps, chunk, width, masked):
    top = depths[0]
    order = [("whole", top)]
    for level in range(top - 1, 0, -1):
        order += [("fh", level), ("fl", level)]
    for level in range(top + 1):
        order += [("bh", level), ("bl", level)]
    order += [("whole", depth) for depth in depths[1:]]
    sources = operands(made, order)
    outs = []
    for depth in depths:
        for _ in steps:
            outs.append(((depth, 2, chunk, width), F32, VMEM))
            outs.append(((2, chunk, width), F32, VMEM))
    scratch = [
        pltpu.VMEM((top * width, 2 * width), F32),
        pltpu.VMEM((top * width, 2 * width), BF16),
        pltpu.VMEM((top * width, 2 * width), BF16),
        pltpu.VMEM((width, 2 * width), F32),
    ]
    kernel = functools.partial(solve_kernel, depths, chunk, width, steps, order, masked)
    flops = sum(24 * (depth * depth + depth) * width**3 for depth in depths)
    ins = [(scalars, SMEM)] + [(value, VMEM) for value in sources]
    got = list(run_kernel(kernel, outs, ins, scratch, flops))
    result = {}
    for depth in depths:
        result[depth] = [(got.pop(0), got.pop(0)) for _ in steps]
    return result


def last_kernel(depth, chunk, width, cols, steps, table, n_arrays, order, n_done, *refs):
    refs = list(refs)
    scalars = refs.pop(0)
    arrays = [refs.pop(0) for _ in range(n_arrays)]
    sources = [refs.pop(0) for _ in order]
    lefts = [tuple(refs.pop(0) for _ in range(4)) for _ in range(n_done)]
    outs = [refs.pop(0) for _ in steps]
    left_high, left_low, right_high, right_low = (refs.pop(0) for _ in range(4))
    sums, solved_ref, total = refs

    def get(kind, level):
        return sources[order.index((kind, level))]

    for mask, part, position, base, stride in table:
        start = rows_of(scalars, mask, chunk)
        for block in range(depth):
            row = pl.multiple_of((depth - 1 - block) * width + start, chunk)
            sums[pl.ds(row, chunk), pl.ds(part * cols, cols)] = arrays[position][base + stride * block]
    for level in range(depth):
        for part in range(2):
            value = sums[pl.ds(level * width, width), pl.ds(part * cols, cols)]
            high, low = split(value.T)
            rows, lanes = pl.ds(part * cols, cols), pl.ds(level * width, width)
            left_high[rows, lanes] = high
            left_low[rows, lanes] = low

    def emit(level, value):
        solved_ref[...] = value
        for out, step in zip(outs, steps):
            start = rows_of(scalars, step, chunk)
            piece = -solved_ref[pl.ds(start, chunk)]
            out[depth - 1 - level, 0] = piece[:, :cols]
            out[depth - 1 - level, 1] = piece[:, cols:]

    substitute(
        depth, width, cols,
        lambda level: (get("fh", level), get("fl", level)),
        lambda level: (get("bh", level), get("bl", level)),
        sums, right_high, right_low, emit,
    )


    if n_done + 1 < HALVES:
        return
    lefts.append((left_high, left_low, right_high, right_low))
    product = three_products(
        jnp.concatenate([left[0][...] for left in lefts], axis=0),
        jnp.concatenate([left[1][...] for left in lefts], axis=0),
        jnp.concatenate([left[2][...] for left in lefts], axis=1),
        jnp.concatenate([left[3][...] for left in lefts], axis=1),
    )
    size = 2 * cols
    for row in range(HALVES):
        for col in range(HALVES):
            block = product[row * size : (row + 1) * size, col * size : (col + 1) * size]
            block = -complex_sum(block, cols)
            for part in range(2):
                total[col, part, pl.ds(row * cols, cols)] = block[:, part * cols : (part + 1) * cols]
    for out, step in zip(outs, steps):
        start = rows_of(scalars, step, chunk)
        for col in range(HALVES):
            for part in range(2):
                out[depth + col, part] = total[col, part, pl.ds(start, chunk)]


def solve_last(depth, made, pieces, scalars, steps, chunk, width, cols, lefts):
    arrays, table = [], []
    for mask, part, array, base, stride in pieces:
        position = next((at for at, value in enumerate(arrays) if value is array), None)
        if position is None:
            position = len(arrays)
            arrays.append(array)
        table.append((mask, part, position, base, stride))
    order = []
    for level in range(depth - 1, 0, -1):
        order += [("fh", level), ("fl", level)]
    for level in range(depth):
        order += [("bh", level), ("bl", level)]
    done = len(lefts) + 1 == HALVES
    sources = operands(made, order) + ([value for left in lefts for value in left] if done else [])
    blocks = depth + (HALVES if done else 0)
    outs = [((blocks, 2, chunk, cols), F32, VMEM)] * len(steps)
    outs += [((2 * cols, depth * width), BF16, VMEM)] * 2
    outs += [((depth * width, 2 * cols), BF16, VMEM)] * 2
    scratch = [
        pltpu.VMEM((depth * width, 2 * cols), F32),
        pltpu.VMEM((width, 2 * cols), F32),
        pltpu.VMEM((HALVES, 2, width, cols), F32),
    ]
    kernel = functools.partial(
        last_kernel, depth, chunk, width, cols, steps, table, len(arrays), order,
        len(lefts) if done else 0,
    )
    flops = 24 * depth * depth * width * width * cols
    ins = [(scalars, SMEM)] + [(value, VMEM) for value in arrays]
    ins += [(value, VMEM) for value in sources]
    got = run_kernel(kernel, outs, ins, scratch, flops)
    return got[: len(steps)], got[len(steps) :]


def begin_kernel(plan, zeros, *refs):
    scalars = refs[0]
    pieces = refs[1 : 1 + len(plan)]
    out, zero_ref, sem = refs[1 + len(plan) :]
    zero_ref[...] = jnp.zeros_like(zero_ref)
    copies = []
    for slot, depth, count in zeros:
        copies.append((zero_ref.at[pl.ds(0, count)], out.at[0, slot, pl.ds(depth, count)]))
    for piece, (first, group, step, depth) in zip(pieces, plan):
        slot = first + ((scalars[2] // group) ^ step)
        copies.append((piece, out.at[0, slot, pl.ds(0, depth)]))
    copies = [
        pltpu.make_async_copy(source, target, sem.at[at])
        for at, (source, target) in enumerate(copies)
    ]
    for copy in copies:
        copy.start()
    for copy in copies:
        copy.wait()


def place_kernel(plan, depth, cols, half, diag_plan, shared, *refs):
    refs = list(refs)
    scalars = refs.pop(0)
    pieces = [refs.pop(0) for _ in plan]
    refs.pop(0)
    last_half = half + 1 == HALVES
    own = refs.pop(0) if last_half else None
    corrections = [refs.pop(0) for _ in diag_plan] if last_half else []
    out = refs.pop(0)
    diag = refs.pop(0) if last_half else None
    (sem,) = refs
    copies = []
    slots = [first + ((scalars[2] // group) ^ step) for first, group, step in plan]
    for at, (piece, slot) in enumerate(zip(pieces, slots)):
        target = out.at[0, slot, :, :, :, pl.ds(half * cols, cols)]
        copies.append(pltpu.make_async_copy(piece.at[pl.ds(0, depth)], target, sem.at[at]))
    for copy in copies:
        copy.start()
    if last_half:
        for slot in range(diag.shape[1]):
            value = own[0, slot]
            if slot in shared:
                value = jnp.where(scalars[5 + shared[slot]] == 1, value, 0.0)
            diag[0, slot] = value
        for correction, (first, group, step) in zip(corrections, diag_plan):
            slot = first + ((scalars[2] // group) ^ step)
            diag[0, slot] = diag[0, slot] - correction[...]
        for piece, slot in zip(pieces, slots):
            for col in range(HALVES):
                lanes = slice(col * cols, (col + 1) * cols)
                diag[0, slot, :, :, lanes] = diag[0, slot, :, :, lanes] - piece[depth + col]
    for copy in copies:
        copy.wait()


def body(lower_panel, diag_inverse, structure):
    columns = lax.axis_size("col")
    rows = lax.axis_size("row")
    position = lax.axis_index("col")
    place = lax.axis_index("row")
    slots, anc_count, _, chunk, width = lower_panel.shape[1:]
    per_col = [max(1, 2**depth // columns) for depth in range(LEVELS)]
    offsets = [sum(per_col[:depth]) for depth in range(LEVELS)]
    last = LEVELS - 1
    cols = width // HALVES
    groups = [rows // nodes for nodes in per_col]
    steps = [[step * groups[depth] for step in range(per_col[depth])] for depth in range(LEVELS)]
    shared = [depth for depth in range(LEVELS) if 2**depth < columns]
    middle = [depth for depth in range(LEVELS - 1) if 2**depth >= columns]
    active = [position % max(1, columns // 2**depth) == 0 for depth in range(LEVELS)]
    odd = position % 2 == 1
    scalars = [place, odd, jnp.where(odd, turned(place, rows), place)]
    scalars += [jnp.where(odd, turned(mask, rows), mask) for mask in (1, 2)]
    scalars = jnp.stack([jnp.asarray(value, jnp.int32) for value in scalars + active])
    present = structure[0]

    upper = shared[:-1]
    starts = [sum(1 + depth for depth in upper[:at]) for at in range(len(upper))]

    def level_blocks(depth, step=0):
        group = groups[depth]
        return [
            (offsets[depth], lambda at, group=group, step=step: (at // group) ^ step, block)
            for block in range(depth + 1)
        ]

    whole_plan, near_plan, far_plan, bases = [], [], [], {}
    for depth in middle:
        if groups[depth] > 2:
            bases[depth] = len(whole_plan)
            whole_plan += level_blocks(depth)
        else:
            bases[depth] = len(near_plan)
            near_plan += level_blocks(depth)
            far_plan += level_blocks(depth, 1)

    def packs(plan, depths):
        spans = [(offsets[depth], per_col[depth], depth) for depth in depths if depth]
        return list(pack(plan, spans, scalars, present, lower_panel, diag_inverse))

    plan = [sum([level_blocks(depth) for depth in upper], []), level_blocks(shared[-1])]
    plan += [whole_plan] if whole_plan else []
    packed = packs(plan, shared + [depth for depth in middle if groups[depth] > 2])
    upper_pack, own_pack = packed[:2]

    stride = columns // 2
    while stride >= 4:
        held = [at for at, depth in enumerate(upper) if columns // 2**depth >= 2 * stride]
        count = 2 * (starts[held[-1]] + 1 + upper[held[-1]])
        pairs = [(source, source + stride) for source in range(0, columns, 2 * stride)]
        if stride == columns // 2 and count == 2:
            travelling = diag_inverse[0, 0]
        else:
            travelling = upper_pack[:count]
        arrived = lax.ppermute(travelling, "col", pairs)
        fresh = position % (2 * stride) == stride
        upper_pack = jnp.concatenate(
            [jnp.where(fresh, arrived, upper_pack[:count]), upper_pack[count:]], axis=0
        )
        stride //= 2
    from_one = lax.ppermute(
        upper_pack, "col", [(source, source + 1) for source in range(0, columns, 4)]
    )
    from_three = lax.ppermute(
        upper_pack, "col", [(source, source + 3) for source in range(0, columns, 4)]
    )
    upper_got = jnp.where(position % 4 == 1, from_one, from_three)
    planes = max(own_pack.shape[0], upper_got.shape[0])

    def fill(value):
        return jnp.pad(value, ((0, planes - value.shape[0]), (0, 0), (0, 0)))

    own = jnp.where(odd, fill(upper_got), fill(own_pack))

    if whole_plan:
        whole_pack = packed[2]
        near_got = row_swap(whole_pack, 1)
        far_got = row_swap(whole_pack, 2)
    near = row_swap(own, 1)
    far = row_swap(own, 2)

    def halves(value):
        return value.reshape(value.shape[0] // 2, 2, chunk, width)

    near_sends, far_sends = [halves(far)[:, 0]], [halves(near)[:, 1]]
    if whole_plan:
        near_sends.append(halves(far_got)[:, 0])
        far_sends.append(halves(near_got)[:, 1])
    near_sends = jnp.concatenate(near_sends, axis=0)
    far_sends = jnp.concatenate(far_sends, axis=0)
    near_sends, far_sends = lax.optimization_barrier((near_sends, far_sends))
    near_more = row_swap(near_sends, 1)
    far_more = row_swap(far_sends, 2)

    if near_plan:
        near_four, far_four = packs([near_plan, far_plan], [d for d in middle if groups[d] <= 2])
        near_four, far_four, near_more, far_more = lax.optimization_barrier(
            (near_four, far_four, near_more, far_more)
        )
        far_four_got = row_swap(far_four, 2)
        near_four_got = row_swap(near_four, 1)

    blocks = planes // 2
    mine = jnp.concatenate([own, near, far, near_more[:blocks], far_more[:blocks]], axis=0)
    theirs = col_swap(mine)
    shared_pieces = (
        both_parts(0, mine)
        + both_parts(1, mine, blocks)
        + both_parts(2, mine, 2 * blocks)
        + [(3, 0, mine, 6 * blocks, 1), (3, 1, mine, 7 * blocks, 1)]
    )

    made = {}
    for depth in middle:
        if groups[depth] > 2:
            base = bases[depth]
            pieces = both_parts(0, whole_pack, base) + both_parts(1, near_got, base)
            pieces += both_parts(2, far_got, base)
            pieces += [(3, 0, near_more, blocks + base, 1), (3, 1, far_more, blocks + base, 1)]
            made.update(prep([(depth, None, 0)], pieces, scalars, rows, chunk, width))
    levels = [(depth, True, starts[at]) for at, depth in enumerate(upper)]
    levels.append((shared[-1], False, 0))
    made.update(prep(levels, shared_pieces, scalars, rows, chunk, width, others=[theirs]))
    if near_plan:
        far_four_got, near_four_got, _ = lax.optimization_barrier(
            (far_four_got, near_four_got, made[shared[-1]][3:])
        )
        near_four_more = row_swap(far_four_got, 1)
    nodes, group = per_col[last], groups[last]
    last_packs = pack_last(
        offsets[last], nodes, last, [(step, group) for step in range(nodes)], cols,
        scalars, present, lower_panel,
    )
    last_pieces = []
    for half in range(HALVES):
        sent = last_packs[half * nodes : (half + 1) * nodes]
        if near_plan:
            sent, _ = lax.optimization_barrier((sent, near_four_more if half else far_four_got))
        pieces = []
        for step, value in zip(steps[last], sent):
            arrived = row_swap(value, step) if step else value
            if group == 1:
                pieces.append((step, arrived))
                continue
            listed = [(step, arrived)]
            mask = 1
            while mask < group:
                listed += [(mask | at, row_swap(held, mask)) for at, held in listed]
                mask *= 2
            pieces += listed
        last_pieces.append(pieces)

    single = [depth for depth in range(last - 1, 0, -1) if per_col[depth] == 1]
    solved = solve(single, made, scalars, [0], chunk, width, tuple(shared))
    arrived = [value for _, value in last_pieces[0]]
    solved, arrived, later = lax.optimization_barrier((solved, arrived, scalars))
    last_pieces[0] = [(at, value) for (at, _), value in zip(last_pieces[0], arrived)]
    for depth in middle:
        if groups[depth] <= 2:
            base = bases[depth]
            pieces = both_parts(0, near_four, base) + both_parts(1, near_four_got, base)
            pieces += both_parts(2, far_four_got, base) + both_parts(3, near_four_more, base)
            made.update(prep([(depth, None, 0)], pieces, later, rows, chunk, width))

    for depth in range(1, last):
        if per_col[depth] > 1:
            solved.update(solve([depth], made, scalars, steps[depth], chunk, width, ()))
    solved, later = lax.optimization_barrier((solved, scalars))
    lefts, backs = [], []
    for half in range(HALVES):
        outward, left = solve_last(
            last, made, sum([both_parts(at, held) for at, held in last_pieces[half]], []),
            later, steps[last], chunk, width, cols, lefts
        )
        lefts.append(left)
        backs.append(
            [row_swap(piece, step) if step else piece for piece, step in zip(outward, steps[last])]
        )
    begin_plan, begin_pieces, diag_plan, diag_pieces = [], [], [], []
    for depth in range(1, last):
        for step, (piece, correction) in enumerate(solved[depth]):
            if step:
                both = jnp.concatenate([piece, correction[None]], axis=0)
                both = row_swap(both, steps[depth][step])
                piece, correction = both[:depth], both[depth]
            begin_plan.append((offsets[depth], groups[depth], step, depth))
            begin_pieces.append(piece)
            diag_plan.append((offsets[depth], groups[depth], step))
            diag_pieces.append(correction)
    zeros = [
        (offsets[depth] + node, depth, anc_count - depth)
        for depth in range(LEVELS)
        for node in range(per_col[depth])
        if depth < anc_count
    ]
    panel_shape = lower_panel.shape
    (sel_panel,) = run_kernel(
        functools.partial(begin_kernel, begin_plan, zeros),
        [(panel_shape, F32, ANY)],
        [(scalars, SMEM)] + [(piece, VMEM) for piece in begin_pieces],
        [
            pltpu.VMEM((anc_count, 2, chunk, width), F32),
            pltpu.SemaphoreType.DMA((len(zeros) + len(begin_plan),)),
        ],
        0,
    )
    last_plan = [(offsets[last], group, step) for step in range(nodes)]
    masked = {offsets[depth]: depth for depth in shared}
    for half, back in enumerate(backs):
        ins = [(scalars, SMEM)] + [(piece, VMEM) for piece in back] + [(sel_panel, ANY)]
        outs = [(panel_shape, F32, ANY)]
        if half + 1 == HALVES:
            ins += [(diag_inverse, VMEM)] + [(piece, VMEM) for piece in diag_pieces]
            outs.append((diag_inverse.shape, F32, VMEM))
        made_now = run_kernel(
            functools.partial(place_kernel, last_plan, last, cols, half, diag_plan, masked),
            outs,
            ins,
            [pltpu.SemaphoreType.DMA((nodes,))],
            0,
            aliases={1 + nodes: 0},
        )
        sel_panel = made_now[0]
    return (sel_panel, made_now[1])


def solution(mesh):
    in_specs = (
        P("col", None, None, None, "row", None),
        P("col", None, None, "row", None),
        P("col", None, None),
    )
    out_specs = (P("col", None, None, None, "row", None), P("col", None, None, "row", None))
    return jax.shard_map(body, mesh=mesh, in_specs=in_specs, out_specs=out_specs, check_vma=False)
```

```python
import functools

import jax
import jax.numpy as jnp
from jax import lax
from jax.experimental import pallas as pl
from jax.experimental.pallas import tpu as pltpu
from jax.sharding import PartitionSpec as P

LEVELS = 6
HALVES = 2
VMEM_BYTES = 18 * 2**20
PACK_BYTES = 58 * 2**20
F32 = jnp.float32
BF16 = jnp.bfloat16
ANY = pl.BlockSpec(memory_space=pl.ANY)
VMEM = pl.BlockSpec(memory_space=pltpu.VMEM)
SMEM = pl.BlockSpec(memory_space=pltpu.SMEM)


def turned(mask, rows):
    if rows < 4:
        return mask
    return (mask & ~3) | ((mask & 1) << 1) | ((mask >> 1) & 1)


def col_swap(value):
    count = lax.axis_size("col")
    return lax.ppermute(value, "col", [(source, source ^ 1) for source in range(count)])


def row_swap(value, mask):
    rows, columns = lax.axis_size("row"), lax.axis_size("col")
    pairs = []
    for row in range(rows):
        for col in range(columns):
            other = row ^ (turned(mask, rows) if col % 2 else mask)
            pairs.append((row * columns + col, other * columns + col))
    return lax.ppermute(value, ("row", "col"), pairs)


def rows_of(scalars, mask, chunk):
    away = mask & ~3
    if mask & 1:
        away = away | scalars[3]
    if mask & 2:
        away = away | scalars[4]
    return pl.multiple_of((scalars[0] ^ away) * chunk, chunk)


def split(value):
    high = value.astype(BF16)
    return high, (value - high.astype(F32)).astype(BF16)


WIDE = 3


def store_left(ref, rows, first, value):
    high, low = split(value)
    size = value.shape[1]
    for at, part in enumerate((high, high, low)):
        ref[rows, pl.ds(first + at * size, size)] = part


def store_right(ref, first, value):
    high, low = split(value)
    size = value.shape[0]
    for at, part in enumerate((high, low, high)):
        ref[pl.ds(first + at * size, size)] = part


def times(left, right):
    return jnp.dot(left, right, preferred_element_type=F32)


def complex_sum(product, half):
    count = product.shape[0] // 2
    by_real, by_imag = product[:count], product[count:]
    return jnp.concatenate(
        [by_real[:, :half] - by_imag[:, half:], by_real[:, half:] + by_imag[:, :half]], axis=1
    )


def run_kernel(kernel, outs, ins, scratch, flops, aliases=None, limit=VMEM_BYTES):
    moved = sum(value.size for value, _ in ins)
    return pl.pallas_call(
        kernel,
        out_shape=[jax.ShapeDtypeStruct(shape, dtype) for shape, dtype, _ in outs],
        in_specs=[spec for _, spec in ins],
        out_specs=[spec for _, _, spec in outs],
        scratch_shapes=scratch,
        input_output_aliases=aliases or {},
        compiler_params=pltpu.CompilerParams(vmem_limit_bytes=limit),
        cost_estimate=pl.CostEstimate(flops=flops, bytes_accessed=2 * moved, transcendentals=0),
    )(*[value for value, _ in ins])


class Loads:
    def __init__(self, sources, buffers, sems):
        self.buffers = buffers
        self.copies = [
            pltpu.make_async_copy(source, buffer, sems.at[at])
            for at, (source, buffer) in enumerate(zip(sources, buffers))
        ]
        for copy in self.copies:
            copy.start()

    def get(self, at):
        if self.copies[at] is not None:
            self.copies[at].wait()
            self.copies[at] = None
        return self.buffers[at]


def both_parts(mask, array, base=0):
    return [(mask, 0, array, 2 * base, 2), (mask, 1, array, 2 * base + 1, 2)]


def pack_kernel(spans, plan, n_outs, chunk, *refs):
    scalars, present, panel_ref, diag_ref = refs[:4]
    outs = refs[4 : 4 + n_outs]
    panel_bufs = refs[4 + n_outs : -2]
    diag_buf, sems = refs[-2:]
    sources, buffers = [], []
    for (first, nodes, depth), buffer in zip(spans, panel_bufs):
        sources.append(panel_ref.at[0, pl.ds(first, nodes), pl.ds(0, depth)])
        buffers.append(buffer)
    if any(block == 0 for blocks in plan for _, _, block in blocks):
        sources.append(diag_ref.at[0])
        buffers.append(diag_buf)
    loads = Loads(sources, buffers, sems)
    where = {first: at for at, (first, _, _) in enumerate(spans)}
    for out, blocks in zip(outs, plan):
        for at, (first, node_of, block) in enumerate(blocks):
            node = node_of(scalars[2])
            if block == 0:
                value = loads.get(len(spans))[first + node]
            else:
                scale = present[first + node, block - 1].astype(F32)
                value = loads.get(where[first])[node, block - 1] * scale
            out[pl.ds(2 * at, 2)] = value


def pack(plan, spans, scalars, present, lower_panel, diag_inverse, limit):
    chunk, width = lower_panel.shape[-2:]
    outs = [((2 * len(blocks), chunk, width), F32, VMEM) for blocks in plan]
    scratch = [pltpu.VMEM((nodes, depth, 2, chunk, width), F32) for _, nodes, depth in spans]
    scratch += [pltpu.VMEM(diag_inverse.shape[1:], F32), pltpu.SemaphoreType.DMA((len(spans) + 1,))]
    kernel = functools.partial(pack_kernel, spans, plan, len(outs), chunk)
    ins = [(scalars, SMEM), (present, SMEM), (lower_panel, ANY), (diag_inverse, ANY)]
    return run_kernel(kernel, outs, ins, scratch, 0, limit=limit)


def pack_last_kernel(first, nodes, depth, steps, cols, *refs):
    scalars, present, panel_ref = refs[:3]
    outs = refs[3 : 3 + len(steps) * HALVES]
    buffer, sem = refs[-2:]
    copy = pltpu.make_async_copy(panel_ref.at[0, pl.ds(first, nodes), pl.ds(0, depth)], buffer, sem)
    copy.start()
    copy.wait()
    for at, (step, group) in enumerate(steps):
        node = (scalars[2] // group) ^ step
        for block in range(depth):
            value = buffer[node, block] * present[first + node, block].astype(F32)
            for half in range(HALVES):
                outs[half * len(steps) + at][pl.ds(2 * block, 2)] = value[
                    :, :, half * cols : (half + 1) * cols
                ]


def pack_last(first, nodes, depth, steps, cols, scalars, present, lower_panel):
    chunk, width = lower_panel.shape[-2:]
    outs = [((2 * depth, chunk, cols), F32, VMEM)] * (len(steps) * HALVES)
    scratch = [pltpu.VMEM((nodes, depth, 2, chunk, width), F32), pltpu.SemaphoreType.DMA]
    kernel = functools.partial(pack_last_kernel, first, nodes, depth, steps, cols)
    ins = [(scalars, SMEM), (present, SMEM), (lower_panel, ANY)]
    return run_kernel(kernel, outs, ins, scratch, 0)


def prep_kernel(levels, table, rows_count, chunk, width, n_arrays, *refs):
    scalars = refs[0]
    arrays = refs[1 : 1 + n_arrays]
    outs = list(refs[1 + n_arrays :])
    odd = scalars[1] == 1
    for depth, swapped, first in levels:
        if depth:
            whole, forward = outs.pop(0), outs.pop(0)
        else:
            whole = None
        backward = outs.pop(0)
        for block in range(depth + 1):
            for mask, part, position, base, stride in table:
                plane = base + stride * (first + block)
                start = rows_of(scalars, mask, chunk)
                if swapped is None:
                    value = arrays[position][plane]
                else:
                    half = n_arrays // 2
                    from_odd = arrays[position + (0 if swapped else half)]
                    from_even = arrays[position + (half if swapped else 0)]
                    value = jnp.where(odd, from_odd[plane], from_even[plane])
                    away = turned(mask, rows_count) if swapped else mask
                    start = pl.multiple_of((scalars[0] ^ away) * chunk, chunk)
                if block == 0:
                    rows = pl.ds(pl.multiple_of(part * width + start, chunk), chunk)
                    store_left(backward, rows, WIDE * depth * width, value)
                else:
                    rows = pl.ds(pl.multiple_of((depth - block) * width + start, chunk), chunk)
                    whole[rows, pl.ds(part * width, width)] = value
        for level in range(depth):
            for part in range(2):
                value = whole[pl.ds(level * width, width), pl.ds(part * width, width)]
                store_left(forward, pl.ds((2 * level + part) * width, width), 0, value)
                rows = pl.ds(part * width, width)
                store_left(backward, rows, WIDE * level * width, -value.T)


def prep(levels, pieces, scalars, rows, chunk, width, others=()):
    arrays, table = [], []
    for mask, part, array, base, stride in pieces:
        position = next((at for at, value in enumerate(arrays) if value is array), None)
        if position is None:
            position = len(arrays)
            arrays.append(array)
        table.append((mask, part, position, base, stride))
    arrays = arrays + list(others)
    outs = []
    for depth, _, _ in levels:
        if depth:
            outs.append(((depth * width, 2 * width), F32, VMEM))
            outs.append(((2 * depth * width, WIDE * width), BF16, VMEM))
        outs.append(((2 * width, WIDE * (depth + 1) * width), BF16, VMEM))
    kernel = functools.partial(prep_kernel, levels, table, rows, chunk, width, len(arrays))
    ins = [(scalars, SMEM)] + [(value, VMEM) for value in arrays]
    made = list(run_kernel(kernel, outs, ins, [], 0))
    result = {}
    for depth, _, _ in levels:
        if depth:
            result[depth], made = tuple(made[:3]), made[3:]
        else:
            result[depth], made = (None, None, made[0]), made[1:]
    return result


def substitute(depth, width, cols, get, sums, right, emit):
    def rows(first, count=1):
        return pl.ds(first * width, count * width)

    for level in range(depth - 1, 0, -1):
        store_right(right, WIDE * level * width, sums[rows(level)])
        forward = get("forward", level)
        for block in range(level - 1, -1, -1):
            product = times(forward[rows(2 * block, 2)], right[rows(WIDE * level, WIDE)])
            sums[rows(block)] -= complex_sum(product, cols)
    store_right(right, 0, sums[rows(0)])
    for level in range(depth):
        product = times(get("backward", level)[...], right[rows(0, WIDE * (level + 1))])
        solved = complex_sum(product, cols)
        store_right(right, WIDE * level * width, solved)
        emit(level, solved)


def solve_kernel(depths, chunk, width, steps, order, masked, *refs):
    refs = list(refs)
    scalars = refs.pop(0)
    sources = [refs.pop(0) for _ in order]
    outs = {depth: [(refs.pop(0), refs.pop(0)) for _ in steps] for depth in depths}
    sums_ref, right_ref, solved_ref = refs

    def get(kind, level):
        return sources[order.index((kind, level))]

    for depth in depths:
        sums = sums_ref.at[pl.ds(0, depth * width)]
        right = right_ref.at[pl.ds(0, WIDE * depth * width)]
        sums[...] = get("whole", depth)[...]

        def send(block, value, sign):
            solved_ref[...] = value
            for (out, correction), step in zip(outs[depth], steps):
                start = rows_of(scalars, step, chunk)
                piece = solved_ref[pl.ds(start, chunk)] * sign
                if depth in masked:
                    piece = jnp.where(scalars[5 + depth] == 1, piece, 0.0)
                for part in range(2):
                    plane = piece[:, part * width : (part + 1) * width]
                    if block == 0:
                        correction[part] = plane
                    else:
                        out[block - 1, part] = plane

        substitute(
            depth, width, width, get, sums, right,
            lambda level, solved: send(depth - level, solved, -1.0),
        )
        product = times(get("backward", depth)[:, : WIDE * depth * width], right[...])
        send(0, complex_sum(product, width), 1.0)


def operands(made, names):
    index = {"whole": 0, "forward": 1, "backward": 2}
    return [made[level][index[kind]] for kind, level in names]


def solve(depths, made, scalars, steps, chunk, width, masked):
    top = depths[0]
    order = [("whole", top)]
    for level in range(top - 1, 0, -1):
        order.append(("forward", level))
    for level in range(top + 1):
        order.append(("backward", level))
    order += [("whole", depth) for depth in depths[1:]]
    sources = operands(made, order)
    outs = []
    for depth in depths:
        for _ in steps:
            outs.append(((depth, 2, chunk, width), F32, VMEM))
            outs.append(((2, chunk, width), F32, VMEM))
    scratch = [
        pltpu.VMEM((top * width, 2 * width), F32),
        pltpu.VMEM((WIDE * top * width, 2 * width), BF16),
        pltpu.VMEM((width, 2 * width), F32),
    ]
    kernel = functools.partial(solve_kernel, depths, chunk, width, steps, order, masked)
    flops = sum(24 * (depth * depth + depth) * width**3 for depth in depths)
    ins = [(scalars, SMEM)] + [(value, VMEM) for value in sources]
    got = list(run_kernel(kernel, outs, ins, scratch, flops))
    result = {}
    for depth in depths:
        result[depth] = [(got.pop(0), got.pop(0)) for _ in steps]
    return result


def last_kernel(depth, chunk, width, cols, steps, table, n_arrays, order, n_done, *refs):
    refs = list(refs)
    scalars = refs.pop(0)
    arrays = [refs.pop(0) for _ in range(n_arrays)]
    sources = [refs.pop(0) for _ in order]
    lefts = [(refs.pop(0), refs.pop(0)) for _ in range(n_done)]
    outs = [refs.pop(0) for _ in steps]
    left, right = refs.pop(0), refs.pop(0)
    sums, solved_ref, total = refs

    def get(kind, level):
        return sources[order.index((kind, level))]

    for mask, part, position, base, stride in table:
        start = rows_of(scalars, mask, chunk)
        for block in range(depth):
            row = pl.multiple_of((depth - 1 - block) * width + start, chunk)
            sums[pl.ds(row, chunk), pl.ds(part * cols, cols)] = arrays[position][base + stride * block]
    for level in range(depth):
        for part in range(2):
            value = sums[pl.ds(level * width, width), pl.ds(part * cols, cols)]
            store_left(left, pl.ds(part * cols, cols), WIDE * level * width, value.T)

    def emit(level, value):
        solved_ref[...] = value
        for out, step in zip(outs, steps):
            start = rows_of(scalars, step, chunk)
            piece = -solved_ref[pl.ds(start, chunk)]
            out[depth - 1 - level, 0] = piece[:, :cols]
            out[depth - 1 - level, 1] = piece[:, cols:]

    substitute(depth, width, cols, get, sums, right, emit)


    if n_done + 1 < HALVES:
        return
    lefts.append((left, right))
    for row in range(HALVES):
        for col in range(HALVES):
            block = -complex_sum(times(lefts[row][0][...], lefts[col][1][...]), cols)
            for part in range(2):
                total[col, part, pl.ds(row * cols, cols)] = block[:, part * cols : (part + 1) * cols]
    for out, step in zip(outs, steps):
        start = rows_of(scalars, step, chunk)
        for col in range(HALVES):
            for part in range(2):
                out[depth + col, part] = total[col, part, pl.ds(start, chunk)]


def solve_last(depth, made, pieces, scalars, steps, chunk, width, cols, lefts):
    arrays, table = [], []
    for mask, part, array, base, stride in pieces:
        position = next((at for at, value in enumerate(arrays) if value is array), None)
        if position is None:
            position = len(arrays)
            arrays.append(array)
        table.append((mask, part, position, base, stride))
    order = []
    for level in range(depth - 1, 0, -1):
        order.append(("forward", level))
    for level in range(depth):
        order.append(("backward", level))
    done = len(lefts) + 1 == HALVES
    sources = operands(made, order) + ([value for left in lefts for value in left] if done else [])
    blocks = depth + (HALVES if done else 0)
    outs = [((blocks, 2, chunk, cols), F32, VMEM)] * len(steps)
    outs.append(((2 * cols, WIDE * depth * width), BF16, VMEM))
    outs.append(((WIDE * depth * width, 2 * cols), BF16, VMEM))
    scratch = [
        pltpu.VMEM((depth * width, 2 * cols), F32),
        pltpu.VMEM((width, 2 * cols), F32),
        pltpu.VMEM((HALVES, 2, width, cols), F32),
    ]
    kernel = functools.partial(
        last_kernel, depth, chunk, width, cols, steps, table, len(arrays), order,
        len(lefts) if done else 0,
    )
    flops = 24 * depth * depth * width * width * cols
    ins = [(scalars, SMEM)] + [(value, VMEM) for value in arrays]
    ins += [(value, VMEM) for value in sources]
    got = run_kernel(kernel, outs, ins, scratch, flops)
    return got[: len(steps)], got[len(steps) :]


def begin_kernel(plan, zeros, *refs):
    scalars = refs[0]
    pieces = refs[1 : 1 + len(plan)]
    out, zero_ref, sem = refs[1 + len(plan) :]
    zero_ref[...] = jnp.zeros_like(zero_ref)
    copies = []
    for slot, depth, count in zeros:
        copies.append((zero_ref.at[pl.ds(0, count)], out.at[0, slot, pl.ds(depth, count)]))
    for piece, (first, group, step, depth) in zip(pieces, plan):
        slot = first + ((scalars[2] // group) ^ step)
        copies.append((piece, out.at[0, slot, pl.ds(0, depth)]))
    copies = [
        pltpu.make_async_copy(source, target, sem.at[at])
        for at, (source, target) in enumerate(copies)
    ]
    for copy in copies:
        copy.start()
    for copy in copies:
        copy.wait()


def place_kernel(plan, depth, cols, half, diag_plan, shared, *refs):
    refs = list(refs)
    scalars = refs.pop(0)
    pieces = [refs.pop(0) for _ in plan]
    refs.pop(0)
    last_half = half + 1 == HALVES
    own = refs.pop(0) if last_half else None
    corrections = [refs.pop(0) for _ in diag_plan] if last_half else []
    out = refs.pop(0)
    diag = refs.pop(0) if last_half else None
    (sem,) = refs
    copies = []
    slots = [first + ((scalars[2] // group) ^ step) for first, group, step in plan]
    for at, (piece, slot) in enumerate(zip(pieces, slots)):
        target = out.at[0, slot, :, :, :, pl.ds(half * cols, cols)]
        copies.append(pltpu.make_async_copy(piece.at[pl.ds(0, depth)], target, sem.at[at]))
    for copy in copies:
        copy.start()
    if last_half:
        for slot in range(diag.shape[1]):
            value = own[0, slot]
            if slot in shared:
                value = jnp.where(scalars[5 + shared[slot]] == 1, value, 0.0)
            diag[0, slot] = value
        for correction, (first, group, step) in zip(corrections, diag_plan):
            slot = first + ((scalars[2] // group) ^ step)
            diag[0, slot] = diag[0, slot] - correction[...]
        for piece, slot in zip(pieces, slots):
            for col in range(HALVES):
                lanes = slice(col * cols, (col + 1) * cols)
                diag[0, slot, :, :, lanes] = diag[0, slot, :, :, lanes] - piece[depth + col]
    for copy in copies:
        copy.wait()


def body(lower_panel, diag_inverse, structure):
    columns = lax.axis_size("col")
    rows = lax.axis_size("row")
    position = lax.axis_index("col")
    place = lax.axis_index("row")
    slots, anc_count, _, chunk, width = lower_panel.shape[1:]
    per_col = [max(1, 2**depth // columns) for depth in range(LEVELS)]
    offsets = [sum(per_col[:depth]) for depth in range(LEVELS)]
    last = LEVELS - 1
    cols = width // HALVES
    groups = [rows // nodes for nodes in per_col]
    steps = [[step * groups[depth] for step in range(per_col[depth])] for depth in range(LEVELS)]
    shared = [depth for depth in range(LEVELS) if 2**depth < columns]
    middle = [depth for depth in range(LEVELS - 1) if 2**depth >= columns]
    active = [position % max(1, columns // 2**depth) == 0 for depth in range(LEVELS)]
    odd = position % 2 == 1
    scalars = [place, odd, jnp.where(odd, turned(place, rows), place)]
    scalars += [jnp.where(odd, turned(mask, rows), mask) for mask in (1, 2)]
    scalars = jnp.stack([jnp.asarray(value, jnp.int32) for value in scalars + active])
    present = structure[0]

    upper = shared[:-1]
    starts = [sum(1 + depth for depth in upper[:at]) for at in range(len(upper))]

    def level_blocks(depth, step=0):
        group = groups[depth]
        return [
            (offsets[depth], lambda at, group=group, step=step: (at // group) ^ step, block)
            for block in range(depth + 1)
        ]

    whole_plan, near_plan, far_plan, bases = [], [], [], {}
    for depth in middle:
        if groups[depth] > 2:
            bases[depth] = len(whole_plan)
            whole_plan += level_blocks(depth)
        else:
            bases[depth] = len(near_plan)
            near_plan += level_blocks(depth)
            far_plan += level_blocks(depth, 1)

    def packs(plan, depths, limit):
        spans = [(offsets[depth], per_col[depth], depth) for depth in depths if depth]
        return list(pack(plan, spans, scalars, present, lower_panel, diag_inverse, limit))

    plan = [sum([level_blocks(depth) for depth in upper], []), level_blocks(shared[-1])]
    plan += [whole_plan] if whole_plan else []
    spread = [depth for depth in middle if groups[depth] > 2]
    packed = packs(plan, shared + spread, PACK_BYTES)
    upper_pack, own_pack = packed[:2]

    stride = columns // 2
    while stride >= 4:
        held = [at for at, depth in enumerate(upper) if columns // 2**depth >= 2 * stride]
        count = 2 * (starts[held[-1]] + 1 + upper[held[-1]])
        pairs = [(source, source + stride) for source in range(0, columns, 2 * stride)]
        if stride == columns // 2 and count == 2:
            travelling = diag_inverse[0, 0]
        else:
            travelling = upper_pack[:count]
        arrived = lax.ppermute(travelling, "col", pairs)
        fresh = position % (2 * stride) == stride
        upper_pack = jnp.concatenate(
            [jnp.where(fresh, arrived, upper_pack[:count]), upper_pack[count:]], axis=0
        )
        stride //= 2
    from_one = lax.ppermute(
        upper_pack, "col", [(source, source + 1) for source in range(0, columns, 4)]
    )
    from_three = lax.ppermute(
        upper_pack, "col", [(source, source + 3) for source in range(0, columns, 4)]
    )
    upper_got = jnp.where(position % 4 == 1, from_one, from_three)
    planes = max(own_pack.shape[0], upper_got.shape[0])

    def fill(value):
        return jnp.pad(value, ((0, planes - value.shape[0]), (0, 0), (0, 0)))

    own = jnp.where(odd, fill(upper_got), fill(own_pack))

    if whole_plan:
        whole_pack = packed[2]
        near_got = row_swap(whole_pack, 1)
        far_got = row_swap(whole_pack, 2)
    near = row_swap(own, 1)
    far = row_swap(own, 2)

    def halves(value):
        return value.reshape(value.shape[0] // 2, 2, chunk, width)

    near_sends, far_sends = [halves(far)[:, 0]], [halves(near)[:, 1]]
    if whole_plan:
        near_sends.append(halves(far_got)[:, 0])
        far_sends.append(halves(near_got)[:, 1])
    near_sends = jnp.concatenate(near_sends, axis=0)
    far_sends = jnp.concatenate(far_sends, axis=0)
    pair_packs = []
    if near_plan:
        pairs = [depth for depth in middle if groups[depth] <= 2]
        pair_packs = packs([near_plan, far_plan], pairs, VMEM_BYTES)
    nodes, group = per_col[last], groups[last]
    last_packs = pack_last(
        offsets[last], nodes, last, [(step, group) for step in range(nodes)], cols,
        scalars, present, lower_panel,
    )
    near_sends, far_sends, pair_packs, last_packs = lax.optimization_barrier(
        (near_sends, far_sends, pair_packs, last_packs)
    )
    near_more = row_swap(near_sends, 1)
    far_more = row_swap(far_sends, 2)

    if near_plan:
        near_four, far_four = pair_packs
        near_four, far_four, near_more, far_more = lax.optimization_barrier(
            (near_four, far_four, near_more, far_more)
        )
        far_four_got = row_swap(far_four, 2)
        near_four_got = row_swap(near_four, 1)

    blocks = planes // 2
    mine = jnp.concatenate([own, near, far, near_more[:blocks], far_more[:blocks]], axis=0)
    theirs = col_swap(mine)
    shared_pieces = (
        both_parts(0, mine)
        + both_parts(1, mine, blocks)
        + both_parts(2, mine, 2 * blocks)
        + [(3, 0, mine, 6 * blocks, 1), (3, 1, mine, 7 * blocks, 1)]
    )

    made = {}
    for depth in middle:
        if groups[depth] > 2:
            base = bases[depth]
            pieces = both_parts(0, whole_pack, base) + both_parts(1, near_got, base)
            pieces += both_parts(2, far_got, base)
            pieces += [(3, 0, near_more, blocks + base, 1), (3, 1, far_more, blocks + base, 1)]
            made.update(prep([(depth, None, 0)], pieces, scalars, rows, chunk, width))
    levels = [(depth, True, starts[at]) for at, depth in enumerate(upper)]
    levels.append((shared[-1], False, 0))
    made.update(prep(levels, shared_pieces, scalars, rows, chunk, width, others=[theirs]))
    single = [depth for depth in range(last - 1, 0, -1) if per_col[depth] == 1]
    early = [depth for depth in single if depth in middle]
    solved = {}
    if early:
        solved.update(solve(early, made, scalars, [0], chunk, width, ()))
    if near_plan:
        far_four_got, near_four_got, solved = lax.optimization_barrier(
            (far_four_got, near_four_got, solved)
        )
        near_four_more = row_swap(far_four_got, 1)
    last_pieces = []
    for half in range(HALVES):
        sent = last_packs[half * nodes : (half + 1) * nodes]
        if near_plan:
            sent, _ = lax.optimization_barrier((sent, near_four_more if half else far_four_got))
        pieces = []
        for step, value in zip(steps[last], sent):
            arrived = row_swap(value, step) if step else value
            if group == 1:
                pieces.append((step, arrived))
                continue
            listed = [(step, arrived)]
            mask = 1
            while mask < group:
                listed += [(mask | at, row_swap(held, mask)) for at, held in listed]
                mask *= 2
            pieces += listed
        last_pieces.append(pieces)

    for depth in middle:
        if groups[depth] <= 2:
            base = bases[depth]
            pieces = both_parts(0, near_four, base) + both_parts(1, near_four_got, base)
            pieces += both_parts(2, far_four_got, base) + both_parts(3, near_four_more, base)
            made.update(prep([(depth, None, 0)], pieces, scalars, rows, chunk, width))

    for depth in range(1, last):
        if per_col[depth] > 1:
            solved.update(solve([depth], made, scalars, steps[depth], chunk, width, ()))
    solved, later = lax.optimization_barrier((solved, scalars))
    lefts, backs = [], []
    for half in range(HALVES):
        outward, left = solve_last(
            last, made, sum([both_parts(at, held) for at, held in last_pieces[half]], []),
            later, steps[last], chunk, width, cols, lefts
        )
        lefts.append(left)
        if half + 1 == HALVES:
            outward, later = lax.optimization_barrier((outward, scalars))
        backs.append(
            [row_swap(piece, step) if step else piece for piece, step in zip(outward, steps[last])]
        )
    late = [depth for depth in single if depth not in middle]
    solved.update(solve(late, made, later, [0], chunk, width, tuple(shared)))

    begin_plan, begin_pieces, diag_plan, diag_pieces = [], [], [], []
    for depth in range(1, last):
        for step, (piece, correction) in enumerate(solved[depth]):
            if step:
                both = jnp.concatenate([piece, correction[None]], axis=0)
                both = row_swap(both, steps[depth][step])
                piece, correction = both[:depth], both[depth]
            begin_plan.append((offsets[depth], groups[depth], step, depth))
            begin_pieces.append(piece)
            diag_plan.append((offsets[depth], groups[depth], step))
            diag_pieces.append(correction)
    zeros = [
        (offsets[depth] + node, depth, anc_count - depth)
        for depth in range(LEVELS)
        for node in range(per_col[depth])
        if depth < anc_count
    ]
    panel_shape = lower_panel.shape
    (sel_panel,) = run_kernel(
        functools.partial(begin_kernel, begin_plan, zeros),
        [(panel_shape, F32, ANY)],
        [(scalars, SMEM)] + [(piece, VMEM) for piece in begin_pieces],
        [
            pltpu.VMEM((anc_count, 2, chunk, width), F32),
            pltpu.SemaphoreType.DMA((len(zeros) + len(begin_plan),)),
        ],
        0,
    )
    last_plan = [(offsets[last], group, step) for step in range(nodes)]
    masked = {offsets[depth]: depth for depth in shared}
    for half, back in enumerate(backs):
        ins = [(scalars, SMEM)] + [(piece, VMEM) for piece in back] + [(sel_panel, ANY)]
        outs = [(panel_shape, F32, ANY)]
        if half + 1 == HALVES:
            ins += [(diag_inverse, VMEM)] + [(piece, VMEM) for piece in diag_pieces]
            outs.append((diag_inverse.shape, F32, VMEM))
        made_now = run_kernel(
            functools.partial(place_kernel, last_plan, last, cols, half, diag_plan, masked),
            outs,
            ins,
            [pltpu.SemaphoreType.DMA((nodes,))],
            0,
            aliases={1 + nodes: 0},
        )
        sel_panel = made_now[0]
    return (sel_panel, made_now[1])


def solution(mesh):
    in_specs = (
        P("col", None, None, None, "row", None),
        P("col", None, None, "row", None),
        P("col", None, None),
    )
    out_specs = (P("col", None, None, None, "row", None), P("col", None, None, "row", None))
    return jax.shard_map(body, mesh=mesh, in_specs=in_specs, out_specs=out_specs, check_vma=False)
```

```python
import functools

import jax
import jax.numpy as jnp
from jax import lax
from jax.experimental import pallas as pl
from jax.experimental.pallas import tpu as pltpu
from jax.sharding import PartitionSpec as P

LEVELS = 6
HALVES = 2
VMEM_BYTES = 18 * 2**20
PACK_BYTES = 58 * 2**20
F32 = jnp.float32
BF16 = jnp.bfloat16
ANY = pl.BlockSpec(memory_space=pl.ANY)
VMEM = pl.BlockSpec(memory_space=pltpu.VMEM)
SMEM = pl.BlockSpec(memory_space=pltpu.SMEM)


def turned(mask, rows):
    if rows < 4:
        return mask
    return (mask & ~3) | ((mask & 1) << 1) | ((mask >> 1) & 1)


def col_swap(value):
    count = lax.axis_size("col")
    return lax.ppermute(value, "col", [(source, source ^ 1) for source in range(count)])


def row_swap(value, mask):
    rows, columns = lax.axis_size("row"), lax.axis_size("col")
    pairs = []
    for row in range(rows):
        for col in range(columns):
            other = row ^ (turned(mask, rows) if col % 2 else mask)
            pairs.append((row * columns + col, other * columns + col))
    return lax.ppermute(value, ("row", "col"), pairs)


def rows_of(scalars, mask, chunk):
    away = mask & ~3
    if mask & 1:
        away = away | scalars[3]
    if mask & 2:
        away = away | scalars[4]
    return pl.multiple_of((scalars[0] ^ away) * chunk, chunk)


def split(value):
    high = value.astype(BF16)
    return high, (value - high.astype(F32)).astype(BF16)


WIDE = 3


def store_left(ref, rows, first, value):
    high, low = split(value)
    size = value.shape[1]
    for at, part in enumerate((high, high, low)):
        ref[rows, pl.ds(first + at * size, size)] = part


def store_right(ref, first, value):
    high, low = split(value)
    size = value.shape[0]
    for at, part in enumerate((high, low, high)):
        ref[pl.ds(first + at * size, size)] = part


def times(left, right):
    return jnp.dot(left, right, preferred_element_type=F32)


def complex_sum(product, half):
    count = product.shape[0] // 2
    by_real, by_imag = product[:count], product[count:]
    return jnp.concatenate(
        [by_real[:, :half] - by_imag[:, half:], by_real[:, half:] + by_imag[:, :half]], axis=1
    )


def run_kernel(kernel, outs, ins, scratch, flops, aliases=None, limit=VMEM_BYTES):
    moved = sum(value.size for value, _ in ins)
    return pl.pallas_call(
        kernel,
        out_shape=[jax.ShapeDtypeStruct(shape, dtype) for shape, dtype, _ in outs],
        in_specs=[spec for _, spec in ins],
        out_specs=[spec for _, _, spec in outs],
        scratch_shapes=scratch,
        input_output_aliases=aliases or {},
        compiler_params=pltpu.CompilerParams(vmem_limit_bytes=limit),
        cost_estimate=pl.CostEstimate(flops=flops, bytes_accessed=2 * moved, transcendentals=0),
    )(*[value for value, _ in ins])


class Loads:
    def __init__(self, sources, buffers, sems):
        self.buffers = buffers
        self.copies = [
            pltpu.make_async_copy(source, buffer, sems.at[at])
            for at, (source, buffer) in enumerate(zip(sources, buffers))
        ]
        for copy in self.copies:
            copy.start()

    def get(self, at):
        if self.copies[at] is not None:
            self.copies[at].wait()
            self.copies[at] = None
        return self.buffers[at]


def both_parts(mask, array, base=0):
    return [(mask, 0, array, 2 * base, 2), (mask, 1, array, 2 * base + 1, 2)]


def pack_kernel(spans, plan, n_outs, chunk, *refs):
    scalars, present, panel_ref, diag_ref = refs[:4]
    outs = refs[4 : 4 + n_outs]
    panel_bufs = refs[4 + n_outs : -2]
    diag_buf, sems = refs[-2:]
    sources, buffers = [], []
    for (first, nodes, depth), buffer in zip(spans, panel_bufs):
        sources.append(panel_ref.at[0, pl.ds(first, nodes), pl.ds(0, depth)])
        buffers.append(buffer)
    if any(block == 0 for blocks in plan for _, _, block in blocks):
        sources.append(diag_ref.at[0])
        buffers.append(diag_buf)
    loads = Loads(sources, buffers, sems)
    where = {first: at for at, (first, _, _) in enumerate(spans)}
    for out, blocks in zip(outs, plan):
        for at, (first, node_of, block) in enumerate(blocks):
            node = node_of(scalars[2])
            if block == 0:
                value = loads.get(len(spans))[first + node]
            else:
                scale = present[first + node, block - 1].astype(F32)
                value = loads.get(where[first])[node, block - 1] * scale
            out[pl.ds(2 * at, 2)] = value


def pack(plan, spans, scalars, present, lower_panel, diag_inverse, limit):
    chunk, width = lower_panel.shape[-2:]
    outs = [((2 * len(blocks), chunk, width), F32, VMEM) for blocks in plan]
    scratch = [pltpu.VMEM((nodes, depth, 2, chunk, width), F32) for _, nodes, depth in spans]
    scratch += [pltpu.VMEM(diag_inverse.shape[1:], F32), pltpu.SemaphoreType.DMA((len(spans) + 1,))]
    kernel = functools.partial(pack_kernel, spans, plan, len(outs), chunk)
    ins = [(scalars, SMEM), (present, SMEM), (lower_panel, ANY), (diag_inverse, ANY)]
    return run_kernel(kernel, outs, ins, scratch, 0, limit=limit)


def pack_last_kernel(first, nodes, depth, steps, cols, *refs):
    scalars, present, panel_ref = refs[:3]
    outs = refs[3 : 3 + len(steps) * HALVES]
    buffer, sem = refs[-2:]
    copy = pltpu.make_async_copy(panel_ref.at[0, pl.ds(first, nodes), pl.ds(0, depth)], buffer, sem)
    copy.start()
    copy.wait()
    for at, (step, group) in enumerate(steps):
        node = (scalars[2] // group) ^ step
        for block in range(depth):
            value = buffer[node, block] * present[first + node, block].astype(F32)
            for half in range(HALVES):
                outs[half * len(steps) + at][pl.ds(2 * block, 2)] = value[
                    :, :, half * cols : (half + 1) * cols
                ]


def pack_last(first, nodes, depth, steps, cols, scalars, present, lower_panel):
    chunk, width = lower_panel.shape[-2:]
    outs = [((2 * depth, chunk, cols), F32, VMEM)] * (len(steps) * HALVES)
    scratch = [pltpu.VMEM((nodes, depth, 2, chunk, width), F32), pltpu.SemaphoreType.DMA]
    kernel = functools.partial(pack_last_kernel, first, nodes, depth, steps, cols)
    ins = [(scalars, SMEM), (present, SMEM), (lower_panel, ANY)]
    return run_kernel(kernel, outs, ins, scratch, 0)


def prep_kernel(levels, table, rows_count, chunk, width, n_arrays, *refs):
    scalars, present = refs[:2]
    arrays = refs[2 : 2 + n_arrays]
    outs = list(refs[2 + n_arrays :])
    odd = scalars[1] == 1
    for depth, swapped, first, slot in levels:
        if depth:
            whole, forward = outs.pop(0), outs.pop(0)
        else:
            whole = None
        backward = outs.pop(0)
        for block in range(depth + 1):
            for mask, part, position, base, stride in table:
                plane = base + stride * (first + block)
                start = rows_of(scalars, mask, chunk)
                if swapped is None:
                    value = arrays[position][plane]
                else:
                    half = n_arrays // 2
                    from_odd = arrays[position + (0 if swapped else half)]
                    from_even = arrays[position + (half if swapped else 0)]
                    value = jnp.where(odd, from_odd[plane], from_even[plane])
                    away = turned(mask, rows_count) if swapped else mask
                    start = pl.multiple_of((scalars[0] ^ away) * chunk, chunk)
                if block == 0:
                    rows = pl.ds(pl.multiple_of(part * width + start, chunk), chunk)
                    store_left(backward, rows, WIDE * depth * width, value)
                else:
                    if slot is not None:
                        value = value * present[slot, block - 1].astype(F32)
                    rows = pl.ds(pl.multiple_of((depth - block) * width + start, chunk), chunk)
                    whole[rows, pl.ds(part * width, width)] = value
        for level in range(depth):
            for part in range(2):
                value = whole[pl.ds(level * width, width), pl.ds(part * width, width)]
                store_left(forward, pl.ds((2 * level + part) * width, width), 0, value)
                rows = pl.ds(part * width, width)
                store_left(backward, rows, WIDE * level * width, -value.T)


def prep(levels, pieces, scalars, present, rows, chunk, width, others=()):
    arrays, table = [], []
    for mask, part, array, base, stride in pieces:
        position = next((at for at, value in enumerate(arrays) if value is array), None)
        if position is None:
            position = len(arrays)
            arrays.append(array)
        table.append((mask, part, position, base, stride))
    arrays = arrays + list(others)
    outs = []
    for depth, _, _, _ in levels:
        if depth:
            outs.append(((depth * width, 2 * width), F32, VMEM))
            outs.append(((2 * depth * width, WIDE * width), BF16, VMEM))
        outs.append(((2 * width, WIDE * (depth + 1) * width), BF16, VMEM))
    kernel = functools.partial(prep_kernel, levels, table, rows, chunk, width, len(arrays))
    ins = [(scalars, SMEM), (present, SMEM)] + [(value, VMEM) for value in arrays]
    made = list(run_kernel(kernel, outs, ins, [], 0))
    result = {}
    for depth, _, _, _ in levels:
        if depth:
            result[depth], made = tuple(made[:3]), made[3:]
        else:
            result[depth], made = (None, None, made[0]), made[1:]
    return result


def substitute(depth, width, cols, get, sums, right, emit):
    def rows(first, count=1):
        return pl.ds(first * width, count * width)

    for level in range(depth - 1, 0, -1):
        store_right(right, WIDE * level * width, sums[rows(level)])
        forward = get("forward", level)
        for block in range(level - 1, -1, -1):
            product = times(forward[rows(2 * block, 2)], right[rows(WIDE * level, WIDE)])
            sums[rows(block)] -= complex_sum(product, cols)
    store_right(right, 0, sums[rows(0)])
    for level in range(depth):
        product = times(get("backward", level)[...], right[rows(0, WIDE * (level + 1))])
        solved = complex_sum(product, cols)
        store_right(right, WIDE * level * width, solved)
        emit(level, solved)


def solve_kernel(depths, chunk, width, steps, order, masked, *refs):
    refs = list(refs)
    scalars = refs.pop(0)
    sources = [refs.pop(0) for _ in order]
    outs = {depth: [(refs.pop(0), refs.pop(0)) for _ in steps] for depth in depths}
    sums_ref, right_ref, solved_ref = refs

    def get(kind, level):
        return sources[order.index((kind, level))]

    for depth in depths:
        sums = sums_ref.at[pl.ds(0, depth * width)]
        right = right_ref.at[pl.ds(0, WIDE * depth * width)]
        sums[...] = get("whole", depth)[...]

        def send(block, value, sign):
            solved_ref[...] = value
            for (out, correction), step in zip(outs[depth], steps):
                start = rows_of(scalars, step, chunk)
                piece = solved_ref[pl.ds(start, chunk)] * sign
                if depth in masked:
                    piece = jnp.where(scalars[5 + depth] == 1, piece, 0.0)
                for part in range(2):
                    plane = piece[:, part * width : (part + 1) * width]
                    if block == 0:
                        correction[part] = plane
                    else:
                        out[block - 1, part] = plane

        substitute(
            depth, width, width, get, sums, right,
            lambda level, solved: send(depth - level, solved, -1.0),
        )
        product = times(get("backward", depth)[:, : WIDE * depth * width], right[...])
        send(0, complex_sum(product, width), 1.0)


def operands(made, names):
    index = {"whole": 0, "forward": 1, "backward": 2}
    return [made[level][index[kind]] for kind, level in names]


def solve(depths, made, scalars, steps, chunk, width, masked):
    top = depths[0]
    order = [("whole", top)]
    for level in range(top - 1, 0, -1):
        order.append(("forward", level))
    for level in range(top + 1):
        order.append(("backward", level))
    order += [("whole", depth) for depth in depths[1:]]
    sources = operands(made, order)
    outs = []
    for depth in depths:
        for _ in steps:
            outs.append(((depth, 2, chunk, width), F32, VMEM))
            outs.append(((2, chunk, width), F32, VMEM))
    scratch = [
        pltpu.VMEM((top * width, 2 * width), F32),
        pltpu.VMEM((WIDE * top * width, 2 * width), BF16),
        pltpu.VMEM((width, 2 * width), F32),
    ]
    kernel = functools.partial(solve_kernel, depths, chunk, width, steps, order, masked)
    flops = sum(24 * (depth * depth + depth) * width**3 for depth in depths)
    ins = [(scalars, SMEM)] + [(value, VMEM) for value in sources]
    got = list(run_kernel(kernel, outs, ins, scratch, flops))
    result = {}
    for depth in depths:
        result[depth] = [(got.pop(0), got.pop(0)) for _ in steps]
    return result


def last_kernel(depth, chunk, width, cols, steps, table, n_arrays, order, n_done, *refs):
    refs = list(refs)
    scalars = refs.pop(0)
    arrays = [refs.pop(0) for _ in range(n_arrays)]
    sources = [refs.pop(0) for _ in order]
    lefts = [(refs.pop(0), refs.pop(0)) for _ in range(n_done)]
    outs = [refs.pop(0) for _ in steps]
    left, right = refs.pop(0), refs.pop(0)
    sums, solved_ref, total = refs

    def get(kind, level):
        return sources[order.index((kind, level))]

    for mask, part, position, base, stride in table:
        start = rows_of(scalars, mask, chunk)
        for block in range(depth):
            row = pl.multiple_of((depth - 1 - block) * width + start, chunk)
            sums[pl.ds(row, chunk), pl.ds(part * cols, cols)] = arrays[position][base + stride * block]
    for level in range(depth):
        for part in range(2):
            value = sums[pl.ds(level * width, width), pl.ds(part * cols, cols)]
            store_left(left, pl.ds(part * cols, cols), WIDE * level * width, value.T)

    def emit(level, value):
        solved_ref[...] = value
        for out, step in zip(outs, steps):
            start = rows_of(scalars, step, chunk)
            piece = -solved_ref[pl.ds(start, chunk)]
            out[depth - 1 - level, 0] = piece[:, :cols]
            out[depth - 1 - level, 1] = piece[:, cols:]

    substitute(depth, width, cols, get, sums, right, emit)


    if n_done + 1 < HALVES:
        return
    lefts.append((left, right))
    for row in range(HALVES):
        for col in range(HALVES):
            block = -complex_sum(times(lefts[row][0][...], lefts[col][1][...]), cols)
            for part in range(2):
                total[col, part, pl.ds(row * cols, cols)] = block[:, part * cols : (part + 1) * cols]
    for out, step in zip(outs, steps):
        start = rows_of(scalars, step, chunk)
        for col in range(HALVES):
            for part in range(2):
                out[depth + col, part] = total[col, part, pl.ds(start, chunk)]


def solve_last(depth, made, pieces, scalars, steps, chunk, width, cols, lefts):
    arrays, table = [], []
    for mask, part, array, base, stride in pieces:
        position = next((at for at, value in enumerate(arrays) if value is array), None)
        if position is None:
            position = len(arrays)
            arrays.append(array)
        table.append((mask, part, position, base, stride))
    order = []
    for level in range(depth - 1, 0, -1):
        order.append(("forward", level))
    for level in range(depth):
        order.append(("backward", level))
    done = len(lefts) + 1 == HALVES
    sources = operands(made, order) + ([value for left in lefts for value in left] if done else [])
    blocks = depth + (HALVES if done else 0)
    outs = [((blocks, 2, chunk, cols), F32, VMEM)] * len(steps)
    outs.append(((2 * cols, WIDE * depth * width), BF16, VMEM))
    outs.append(((WIDE * depth * width, 2 * cols), BF16, VMEM))
    scratch = [
        pltpu.VMEM((depth * width, 2 * cols), F32),
        pltpu.VMEM((width, 2 * cols), F32),
        pltpu.VMEM((HALVES, 2, width, cols), F32),
    ]
    kernel = functools.partial(
        last_kernel, depth, chunk, width, cols, steps, table, len(arrays), order,
        len(lefts) if done else 0,
    )
    flops = 24 * depth * depth * width * width * cols
    ins = [(scalars, SMEM)] + [(value, VMEM) for value in arrays]
    ins += [(value, VMEM) for value in sources]
    got = run_kernel(kernel, outs, ins, scratch, flops)
    return got[: len(steps)], got[len(steps) :]


def begin_kernel(plan, zeros, *refs):
    scalars = refs[0]
    pieces = refs[1 : 1 + len(plan)]
    out, zero_ref, sem = refs[1 + len(plan) :]
    zero_ref[...] = jnp.zeros_like(zero_ref)
    copies = []
    for slot, depth, count in zeros:
        copies.append((zero_ref.at[pl.ds(0, count)], out.at[0, slot, pl.ds(depth, count)]))
    for piece, (first, group, step, depth) in zip(pieces, plan):
        slot = first + ((scalars[2] // group) ^ step)
        copies.append((piece, out.at[0, slot, pl.ds(0, depth)]))
    copies = [
        pltpu.make_async_copy(source, target, sem.at[at])
        for at, (source, target) in enumerate(copies)
    ]
    for copy in copies:
        copy.start()
    for copy in copies:
        copy.wait()


def place_kernel(plan, depth, cols, half, diag_plan, shared, *refs):
    refs = list(refs)
    scalars = refs.pop(0)
    pieces = [refs.pop(0) for _ in plan]
    refs.pop(0)
    last_half = half + 1 == HALVES
    own = refs.pop(0) if last_half else None
    corrections = [refs.pop(0) for _ in diag_plan] if last_half else []
    out = refs.pop(0)
    diag = refs.pop(0) if last_half else None
    (sem,) = refs
    copies = []
    slots = [first + ((scalars[2] // group) ^ step) for first, group, step in plan]
    for at, (piece, slot) in enumerate(zip(pieces, slots)):
        target = out.at[0, slot, :, :, :, pl.ds(half * cols, cols)]
        copies.append(pltpu.make_async_copy(piece.at[pl.ds(0, depth)], target, sem.at[at]))
    for copy in copies:
        copy.start()
    if last_half:
        for slot in range(diag.shape[1]):
            value = own[0, slot]
            if slot in shared:
                value = jnp.where(scalars[5 + shared[slot]] == 1, value, 0.0)
            diag[0, slot] = value
        for correction, (first, group, step) in zip(corrections, diag_plan):
            slot = first + ((scalars[2] // group) ^ step)
            diag[0, slot] = diag[0, slot] - correction[...]
        for piece, slot in zip(pieces, slots):
            for col in range(HALVES):
                lanes = slice(col * cols, (col + 1) * cols)
                diag[0, slot, :, :, lanes] = diag[0, slot, :, :, lanes] - piece[depth + col]
    for copy in copies:
        copy.wait()


def body(lower_panel, diag_inverse, structure):
    columns = lax.axis_size("col")
    rows = lax.axis_size("row")
    position = lax.axis_index("col")
    place = lax.axis_index("row")
    slots, anc_count, _, chunk, width = lower_panel.shape[1:]
    per_col = [max(1, 2**depth // columns) for depth in range(LEVELS)]
    offsets = [sum(per_col[:depth]) for depth in range(LEVELS)]
    last = LEVELS - 1
    cols = width // HALVES
    groups = [rows // nodes for nodes in per_col]
    steps = [[step * groups[depth] for step in range(per_col[depth])] for depth in range(LEVELS)]
    shared = [depth for depth in range(LEVELS) if 2**depth < columns]
    middle = [depth for depth in range(LEVELS - 1) if 2**depth >= columns]
    active = [position % max(1, columns // 2**depth) == 0 for depth in range(LEVELS)]
    odd = position % 2 == 1
    scalars = [place, odd, jnp.where(odd, turned(place, rows), place)]
    scalars += [jnp.where(odd, turned(mask, rows), mask) for mask in (1, 2)]
    scalars = jnp.stack([jnp.asarray(value, jnp.int32) for value in scalars + active])
    present = structure[0]

    upper = shared[:-1]
    starts = [sum(1 + depth for depth in upper[:at]) for at in range(len(upper))]

    def level_blocks(depth, step=0):
        group = groups[depth]
        return [
            (offsets[depth], lambda at, group=group, step=step: (at // group) ^ step, block)
            for block in range(depth + 1)
        ]

    whole_plan, near_plan, far_plan, bases = [], [], [], {}
    for depth in middle:
        if groups[depth] > 2:
            bases[depth] = len(whole_plan)
            whole_plan += level_blocks(depth)
        else:
            bases[depth] = len(near_plan)
            near_plan += level_blocks(depth)
            far_plan += level_blocks(depth, 1)

    def packs(plan, depths, limit):
        spans = [(offsets[depth], per_col[depth], depth) for depth in depths if depth]
        return list(pack(plan, spans, scalars, present, lower_panel, diag_inverse, limit))

    plan = [sum([level_blocks(depth) for depth in upper], []), level_blocks(shared[-1])]
    whole_rows = []
    for depth in middle:
        if groups[depth] > 2:
            whole_rows.append(diag_inverse[0, offsets[depth]])
            whole_rows.append(
                lower_panel[0, offsets[depth], :depth].reshape(2 * depth, chunk, width)
            )
    packed = packs(plan, shared, PACK_BYTES)
    upper_pack, own_pack = packed[:2]

    stride = columns // 2
    while stride >= 4:
        held = [at for at, depth in enumerate(upper) if columns // 2**depth >= 2 * stride]
        count = 2 * (starts[held[-1]] + 1 + upper[held[-1]])
        pairs = [(source, source + stride) for source in range(0, columns, 2 * stride)]
        if stride == columns // 2 and count == 2:
            travelling = diag_inverse[0, 0]
        else:
            travelling = upper_pack[:count]
        arrived = lax.ppermute(travelling, "col", pairs)
        fresh = position % (2 * stride) == stride
        upper_pack = jnp.concatenate(
            [jnp.where(fresh, arrived, upper_pack[:count]), upper_pack[count:]], axis=0
        )
        stride //= 2
    from_one = lax.ppermute(
        upper_pack, "col", [(source, source + 1) for source in range(0, columns, 4)]
    )
    from_three = lax.ppermute(
        upper_pack, "col", [(source, source + 3) for source in range(0, columns, 4)]
    )
    if whole_plan:
        whole_pack = jnp.concatenate(whole_rows, axis=0)
        near_got = row_swap(whole_pack, 1)
        far_got = row_swap(whole_pack, 2)
        from_one, from_three, near_got, far_got = lax.optimization_barrier(
            (from_one, from_three, near_got, far_got)
        )
    upper_got = jnp.where(position % 4 == 1, from_one, from_three)
    planes = max(own_pack.shape[0], upper_got.shape[0])

    def fill(value):
        return jnp.pad(value, ((0, planes - value.shape[0]), (0, 0), (0, 0)))

    own = jnp.where(odd, fill(upper_got), fill(own_pack))

    near = row_swap(own, 1)
    far = row_swap(own, 2)

    def halves(value):
        return value.reshape(value.shape[0] // 2, 2, chunk, width)

    near_sends, far_sends = [halves(far)[:, 0]], [halves(near)[:, 1]]
    if whole_plan:
        near_sends.append(halves(far_got)[:, 0])
        far_sends.append(halves(near_got)[:, 1])
    near_sends = jnp.concatenate(near_sends, axis=0)
    far_sends = jnp.concatenate(far_sends, axis=0)
    pair_packs = []
    if near_plan:
        pairs = [depth for depth in middle if groups[depth] <= 2]
        pair_packs = packs([near_plan, far_plan], pairs, VMEM_BYTES)
    nodes, group = per_col[last], groups[last]
    last_packs = pack_last(
        offsets[last], nodes, last, [(step, group) for step in range(nodes)], cols,
        scalars, present, lower_panel,
    )
    near_sends, far_sends, pair_packs, last_packs = lax.optimization_barrier(
        (near_sends, far_sends, pair_packs, last_packs)
    )
    near_more = row_swap(near_sends, 1)
    far_more = row_swap(far_sends, 2)

    if near_plan:
        near_four, far_four = pair_packs
        near_four, far_four, near_more, far_more = lax.optimization_barrier(
            (near_four, far_four, near_more, far_more)
        )
        far_four_got = row_swap(far_four, 2)
        near_four_got = row_swap(near_four, 1)

    blocks = planes // 2
    mine = jnp.concatenate([own, near, far, near_more[:blocks], far_more[:blocks]], axis=0)
    theirs = col_swap(mine)
    shared_pieces = (
        both_parts(0, mine)
        + both_parts(1, mine, blocks)
        + both_parts(2, mine, 2 * blocks)
        + [(3, 0, mine, 6 * blocks, 1), (3, 1, mine, 7 * blocks, 1)]
    )

    made = {}
    for depth in middle:
        if groups[depth] > 2:
            base = bases[depth]
            pieces = both_parts(0, whole_pack, base) + both_parts(1, near_got, base)
            pieces += both_parts(2, far_got, base)
            pieces += [(3, 0, near_more, blocks + base, 1), (3, 1, far_more, blocks + base, 1)]
            level = (depth, None, 0, offsets[depth])
            made.update(prep([level], pieces, scalars, present, rows, chunk, width))
    levels = [(depth, True, starts[at], None) for at, depth in enumerate(upper)]
    levels.append((shared[-1], False, 0, None))
    made.update(
        prep(levels, shared_pieces, scalars, present, rows, chunk, width, others=[theirs])
    )
    single = [depth for depth in range(last - 1, 0, -1) if per_col[depth] == 1]
    early = [depth for depth in single if depth in middle]
    solved = {}
    if early:
        solved.update(solve(early, made, scalars, [0], chunk, width, ()))
    if near_plan:
        far_four_got, near_four_got, solved = lax.optimization_barrier(
            (far_four_got, near_four_got, solved)
        )
        near_four_more = row_swap(far_four_got, 1)
    last_pieces = []
    for half in range(HALVES):
        sent = last_packs[half * nodes : (half + 1) * nodes]
        if half:
            before = [value for _, value in last_pieces[-1]]
            sent, before = lax.optimization_barrier((sent, before))
            last_pieces[-1] = [(at, value) for (at, _), value in zip(last_pieces[-1], before)]
        elif near_plan:
            sent, near_four_more = lax.optimization_barrier((sent, near_four_more))
        pieces = []
        for step, value in zip(steps[last], sent):
            arrived = row_swap(value, step) if step else value
            if group == 1:
                pieces.append((step, arrived))
                continue
            listed = [(step, arrived)]
            mask = 1
            while mask < group:
                listed += [(mask | at, row_swap(held, mask)) for at, held in listed]
                mask *= 2
            pieces += listed
        last_pieces.append(pieces)

    for depth in middle:
        if groups[depth] <= 2:
            base = bases[depth]
            pieces = both_parts(0, near_four, base) + both_parts(1, near_four_got, base)
            pieces += both_parts(2, far_four_got, base) + both_parts(3, near_four_more, base)
            level = (depth, None, 0, None)
            made.update(prep([level], pieces, scalars, present, rows, chunk, width))

    for depth in range(1, last):
        if per_col[depth] > 1:
            solved.update(solve([depth], made, scalars, steps[depth], chunk, width, ()))
    solved, later = lax.optimization_barrier((solved, scalars))
    lefts, backs = [], []
    for half in range(HALVES):
        outward, left = solve_last(
            last, made, sum([both_parts(at, held) for at, held in last_pieces[half]], []),
            later, steps[last], chunk, width, cols, lefts
        )
        lefts.append(left)
        if half + 1 == HALVES:
            outward, later = lax.optimization_barrier((outward, scalars))
        backs.append(
            [row_swap(piece, step) if step else piece for piece, step in zip(outward, steps[last])]
        )
    late = [depth for depth in single if depth not in middle]
    solved.update(solve(late, made, later, [0], chunk, width, tuple(shared)))

    begin_plan, begin_pieces, diag_plan, diag_pieces = [], [], [], []
    for depth in range(1, last):
        for step, (piece, correction) in enumerate(solved[depth]):
            if step:
                both = jnp.concatenate([piece, correction[None]], axis=0)
                both = row_swap(both, steps[depth][step])
                piece, correction = both[:depth], both[depth]
            begin_plan.append((offsets[depth], groups[depth], step, depth))
            begin_pieces.append(piece)
            diag_plan.append((offsets[depth], groups[depth], step))
            diag_pieces.append(correction)
    zeros = [
        (offsets[depth] + node, depth, anc_count - depth)
        for depth in range(LEVELS)
        for node in range(per_col[depth])
        if depth < anc_count
    ]
    panel_shape = lower_panel.shape
    (sel_panel,) = run_kernel(
        functools.partial(begin_kernel, begin_plan, zeros),
        [(panel_shape, F32, ANY)],
        [(scalars, SMEM)] + [(piece, VMEM) for piece in begin_pieces],
        [
            pltpu.VMEM((anc_count, 2, chunk, width), F32),
            pltpu.SemaphoreType.DMA((len(zeros) + len(begin_plan),)),
        ],
        0,
    )
    last_plan = [(offsets[last], group, step) for step in range(nodes)]
    masked = {offsets[depth]: depth for depth in shared}
    for half, back in enumerate(backs):
        ins = [(scalars, SMEM)] + [(piece, VMEM) for piece in back] + [(sel_panel, ANY)]
        outs = [(panel_shape, F32, ANY)]
        if half + 1 == HALVES:
            ins += [(diag_inverse, VMEM)] + [(piece, VMEM) for piece in diag_pieces]
            outs.append((diag_inverse.shape, F32, VMEM))
        made_now = run_kernel(
            functools.partial(place_kernel, last_plan, last, cols, half, diag_plan, masked),
            outs,
            ins,
            [pltpu.SemaphoreType.DMA((nodes,))],
            0,
            aliases={1 + nodes: 0},
        )
        sel_panel = made_now[0]
    return (sel_panel, made_now[1])


def solution(mesh):
    in_specs = (
        P("col", None, None, None, "row", None),
        P("col", None, None, "row", None),
        P("col", None, None),
    )
    out_specs = (P("col", None, None, None, "row", None), P("col", None, None, "row", None))
    return jax.shard_map(body, mesh=mesh, in_specs=in_specs, out_specs=out_specs, check_vma=False)
```

```python
import functools

import jax
import jax.numpy as jnp
from jax import lax
from jax.experimental import pallas as pl
from jax.experimental.pallas import tpu as pltpu
from jax.sharding import PartitionSpec as P

LEVELS = 6
HALVES = 2
VMEM_BYTES = 18 * 2**20
PACK_BYTES = 58 * 2**20
F32 = jnp.float32
BF16 = jnp.bfloat16
ANY = pl.BlockSpec(memory_space=pl.ANY)
VMEM = pl.BlockSpec(memory_space=pltpu.VMEM)
SMEM = pl.BlockSpec(memory_space=pltpu.SMEM)


def turned(mask, rows):
    if rows < 4:
        return mask
    return (mask & ~3) | ((mask & 1) << 1) | ((mask >> 1) & 1)


def col_swap(value):
    count = lax.axis_size("col")
    return lax.ppermute(value, "col", [(source, source ^ 1) for source in range(count)])


def row_swap(value, mask):
    rows, columns = lax.axis_size("row"), lax.axis_size("col")
    pairs = []
    for row in range(rows):
        for col in range(columns):
            other = row ^ (turned(mask, rows) if col % 2 else mask)
            pairs.append((row * columns + col, other * columns + col))
    return lax.ppermute(value, ("row", "col"), pairs)


def rows_of(scalars, mask, chunk):
    away = mask & ~3
    if mask & 1:
        away = away | scalars[3]
    if mask & 2:
        away = away | scalars[4]
    return pl.multiple_of((scalars[0] ^ away) * chunk, chunk)


def split(value):
    high = value.astype(BF16)
    return high, (value - high.astype(F32)).astype(BF16)


WIDE = 3


def store_left(ref, rows, first, value):
    high, low = split(value)
    size = value.shape[1]
    for at, part in enumerate((high, high, low)):
        ref[rows, pl.ds(first + at * size, size)] = part


def store_right(ref, first, value):
    high, low = split(value)
    size = value.shape[0]
    for at, part in enumerate((high, low, high)):
        ref[pl.ds(first + at * size, size)] = part


def times(left, right):
    return jnp.dot(left, right, preferred_element_type=F32)


def complex_sum(product, half):
    count = product.shape[0] // 2
    by_real, by_imag = product[:count], product[count:]
    return jnp.concatenate(
        [by_real[:, :half] - by_imag[:, half:], by_real[:, half:] + by_imag[:, :half]], axis=1
    )


def run_kernel(kernel, outs, ins, scratch, flops, aliases=None, limit=VMEM_BYTES):
    moved = sum(value.size for value, _ in ins)
    return pl.pallas_call(
        kernel,
        out_shape=[jax.ShapeDtypeStruct(shape, dtype) for shape, dtype, _ in outs],
        in_specs=[spec for _, spec in ins],
        out_specs=[spec for _, _, spec in outs],
        scratch_shapes=scratch,
        input_output_aliases=aliases or {},
        compiler_params=pltpu.CompilerParams(vmem_limit_bytes=limit),
        cost_estimate=pl.CostEstimate(flops=flops // 64, bytes_accessed=moved // 64, transcendentals=0),
    )(*[value for value, _ in ins])


class Loads:
    def __init__(self, sources, buffers, sems):
        self.buffers = buffers
        self.copies = [
            pltpu.make_async_copy(source, buffer, sems.at[at])
            for at, (source, buffer) in enumerate(zip(sources, buffers))
        ]
        for copy in self.copies:
            copy.start()

    def get(self, at):
        if self.copies[at] is not None:
            self.copies[at].wait()
            self.copies[at] = None
        return self.buffers[at]


def both_parts(mask, array, base=0):
    return [(mask, 0, array, 2 * base, 2), (mask, 1, array, 2 * base + 1, 2)]


def pack_kernel(spans, plan, n_outs, chunk, *refs):
    scalars, present, panel_ref, diag_ref = refs[:4]
    outs = refs[4 : 4 + n_outs]
    panel_bufs = refs[4 + n_outs : -2]
    diag_buf, sems = refs[-2:]
    sources, buffers = [], []
    for (first, nodes, depth), buffer in zip(spans, panel_bufs):
        sources.append(panel_ref.at[0, pl.ds(first, nodes), pl.ds(0, depth)])
        buffers.append(buffer)
    if any(block == 0 for blocks in plan for _, _, block in blocks):
        sources.append(diag_ref.at[0])
        buffers.append(diag_buf)
    loads = Loads(sources, buffers, sems)
    where = {first: at for at, (first, _, _) in enumerate(spans)}
    for out, blocks in zip(outs, plan):
        for at, (first, node_of, block) in enumerate(blocks):
            node = node_of(scalars[2])
            if block == 0:
                value = loads.get(len(spans))[first + node]
            else:
                scale = present[first + node, block - 1].astype(F32)
                value = loads.get(where[first])[node, block - 1] * scale
            out[pl.ds(2 * at, 2)] = value


def pack(plan, spans, scalars, present, lower_panel, diag_inverse, limit):
    chunk, width = lower_panel.shape[-2:]
    outs = [((2 * len(blocks), chunk, width), F32, VMEM) for blocks in plan]
    scratch = [pltpu.VMEM((nodes, depth, 2, chunk, width), F32) for _, nodes, depth in spans]
    scratch += [pltpu.VMEM(diag_inverse.shape[1:], F32), pltpu.SemaphoreType.DMA((len(spans) + 1,))]
    kernel = functools.partial(pack_kernel, spans, plan, len(outs), chunk)
    ins = [(scalars, SMEM), (present, SMEM), (lower_panel, ANY), (diag_inverse, ANY)]
    return run_kernel(kernel, outs, ins, scratch, 0, limit=limit)


def pack_last_kernel(first, nodes, depth, steps, cols, *refs):
    scalars, present, panel_ref = refs[:3]
    outs = refs[3 : 3 + len(steps) * HALVES]
    buffer, sem = refs[-2:]
    copy = pltpu.make_async_copy(panel_ref.at[0, pl.ds(first, nodes), pl.ds(0, depth)], buffer, sem)
    copy.start()
    copy.wait()
    for at, (step, group) in enumerate(steps):
        node = (scalars[2] // group) ^ step
        for block in range(depth):
            value = buffer[node, block] * present[first + node, block].astype(F32)
            for half in range(HALVES):
                outs[half * len(steps) + at][pl.ds(2 * block, 2)] = value[
                    :, :, half * cols : (half + 1) * cols
                ]


def pack_last(first, nodes, depth, steps, cols, scalars, present, lower_panel):
    chunk, width = lower_panel.shape[-2:]
    outs = [((2 * depth, chunk, cols), F32, VMEM)] * (len(steps) * HALVES)
    scratch = [pltpu.VMEM((nodes, depth, 2, chunk, width), F32), pltpu.SemaphoreType.DMA]
    kernel = functools.partial(pack_last_kernel, first, nodes, depth, steps, cols)
    ins = [(scalars, SMEM), (present, SMEM), (lower_panel, ANY)]
    return run_kernel(kernel, outs, ins, scratch, 0)


def prep_kernel(levels, table, rows_count, chunk, width, n_arrays, *refs):
    scalars, present = refs[:2]
    arrays = refs[2 : 2 + n_arrays]
    outs = list(refs[2 + n_arrays :])
    odd = scalars[1] == 1
    for depth, swapped, first, slot in levels:
        if depth:
            whole, forward = outs.pop(0), outs.pop(0)
        else:
            whole = None
        backward = outs.pop(0)
        for block in range(depth + 1):
            for mask, part, position, base, stride in table:
                plane = base + stride * (first + block)
                start = rows_of(scalars, mask, chunk)
                if swapped is None:
                    value = arrays[position][plane]
                else:
                    half = n_arrays // 2
                    from_odd = arrays[position + (0 if swapped else half)]
                    from_even = arrays[position + (half if swapped else 0)]
                    value = jnp.where(odd, from_odd[plane], from_even[plane])
                    away = turned(mask, rows_count) if swapped else mask
                    start = pl.multiple_of((scalars[0] ^ away) * chunk, chunk)
                if block == 0:
                    rows = pl.ds(pl.multiple_of(part * width + start, chunk), chunk)
                    store_left(backward, rows, WIDE * depth * width, value)
                else:
                    if slot is not None:
                        at = slot[0] + scalars[2] // slot[1]
                        value = value * present[at, block - 1].astype(F32)
                    rows = pl.ds(pl.multiple_of((depth - block) * width + start, chunk), chunk)
                    whole[rows, pl.ds(part * width, width)] = value
        for level in range(depth):
            for part in range(2):
                value = whole[pl.ds(level * width, width), pl.ds(part * width, width)]
                store_left(forward, pl.ds((2 * level + part) * width, width), 0, value)
                rows = pl.ds(part * width, width)
                store_left(backward, rows, WIDE * level * width, -value.T)


def prep(levels, pieces, scalars, present, rows, chunk, width, others=()):
    arrays, table = [], []
    for mask, part, array, base, stride in pieces:
        position = next((at for at, value in enumerate(arrays) if value is array), None)
        if position is None:
            position = len(arrays)
            arrays.append(array)
        table.append((mask, part, position, base, stride))
    arrays = arrays + list(others)
    outs = []
    for depth, _, _, _ in levels:
        if depth:
            outs.append(((depth * width, 2 * width), F32, VMEM))
            outs.append(((2 * depth * width, WIDE * width), BF16, VMEM))
        outs.append(((2 * width, WIDE * (depth + 1) * width), BF16, VMEM))
    kernel = functools.partial(prep_kernel, levels, table, rows, chunk, width, len(arrays))
    ins = [(scalars, SMEM), (present, SMEM)] + [(value, VMEM) for value in arrays]
    made = list(run_kernel(kernel, outs, ins, [], 0))
    result = {}
    for depth, _, _, _ in levels:
        if depth:
            result[depth], made = tuple(made[:3]), made[3:]
        else:
            result[depth], made = (None, None, made[0]), made[1:]
    return result


def substitute(depth, width, cols, get, sums, right, emit):
    def rows(first, count=1):
        return pl.ds(first * width, count * width)

    for level in range(depth - 1, 0, -1):
        store_right(right, WIDE * level * width, sums[rows(level)])
        forward = get("forward", level)
        for block in range(level - 1, -1, -1):
            product = times(forward[rows(2 * block, 2)], right[rows(WIDE * level, WIDE)])
            sums[rows(block)] -= complex_sum(product, cols)
    store_right(right, 0, sums[rows(0)])
    for level in range(depth):
        product = times(get("backward", level)[...], right[rows(0, WIDE * (level + 1))])
        solved = complex_sum(product, cols)
        store_right(right, WIDE * level * width, solved)
        emit(level, solved)


def solve_kernel(depths, chunk, width, steps, order, masked, *refs):
    refs = list(refs)
    scalars = refs.pop(0)
    sources = [refs.pop(0) for _ in order]
    outs = {depth: [(refs.pop(0), refs.pop(0)) for _ in steps] for depth in depths}
    sums_ref, right_ref, solved_ref = refs

    def get(kind, level):
        return sources[order.index((kind, level))]

    for depth in depths:
        sums = sums_ref.at[pl.ds(0, depth * width)]
        right = right_ref.at[pl.ds(0, WIDE * depth * width)]
        sums[...] = get("whole", depth)[...]

        def send(block, value, sign):
            solved_ref[...] = value
            for (out, correction), step in zip(outs[depth], steps):
                start = rows_of(scalars, step, chunk)
                piece = solved_ref[pl.ds(start, chunk)] * sign
                if depth in masked:
                    piece = jnp.where(scalars[5 + depth] == 1, piece, 0.0)
                for part in range(2):
                    plane = piece[:, part * width : (part + 1) * width]
                    if block == 0:
                        correction[part] = plane
                    else:
                        out[block - 1, part] = plane

        substitute(
            depth, width, width, get, sums, right,
            lambda level, solved: send(depth - level, solved, -1.0),
        )
        product = times(get("backward", depth)[:, : WIDE * depth * width], right[...])
        send(0, complex_sum(product, width), 1.0)


def operands(made, names):
    index = {"whole": 0, "forward": 1, "backward": 2}
    return [made[level][index[kind]] for kind, level in names]


def solve(depths, made, scalars, steps, chunk, width, masked):
    top = depths[0]
    order = [("whole", top)]
    for level in range(top - 1, 0, -1):
        order.append(("forward", level))
    for level in range(top + 1):
        order.append(("backward", level))
    order += [("whole", depth) for depth in depths[1:]]
    sources = operands(made, order)
    outs = []
    for depth in depths:
        for _ in steps:
            outs.append(((depth, 2, chunk, width), F32, VMEM))
            outs.append(((2, chunk, width), F32, VMEM))
    scratch = [
        pltpu.VMEM((top * width, 2 * width), F32),
        pltpu.VMEM((WIDE * top * width, 2 * width), BF16),
        pltpu.VMEM((width, 2 * width), F32),
    ]
    kernel = functools.partial(solve_kernel, depths, chunk, width, steps, order, masked)
    flops = sum(24 * (depth * depth + depth) * width**3 for depth in depths)
    ins = [(scalars, SMEM)] + [(value, VMEM) for value in sources]
    got = list(run_kernel(kernel, outs, ins, scratch, flops))
    result = {}
    for depth in depths:
        result[depth] = [(got.pop(0), got.pop(0)) for _ in steps]
    return result


def last_kernel(depth, chunk, width, cols, steps, table, n_arrays, order, n_done, *refs):
    refs = list(refs)
    scalars = refs.pop(0)
    arrays = [refs.pop(0) for _ in range(n_arrays)]
    sources = [refs.pop(0) for _ in order]
    lefts = [(refs.pop(0), refs.pop(0)) for _ in range(n_done)]
    outs = [refs.pop(0) for _ in steps]
    left, right = refs.pop(0), refs.pop(0)
    sums, solved_ref, total = refs

    def get(kind, level):
        return sources[order.index((kind, level))]

    for mask, part, position, base, stride in table:
        start = rows_of(scalars, mask, chunk)
        for block in range(depth):
            row = pl.multiple_of((depth - 1 - block) * width + start, chunk)
            sums[pl.ds(row, chunk), pl.ds(part * cols, cols)] = arrays[position][base + stride * block]
    for level in range(depth):
        for part in range(2):
            value = sums[pl.ds(level * width, width), pl.ds(part * cols, cols)]
            store_left(left, pl.ds(part * cols, cols), WIDE * level * width, value.T)

    def emit(level, value):
        solved_ref[...] = value
        for out, step in zip(outs, steps):
            start = rows_of(scalars, step, chunk)
            piece = -solved_ref[pl.ds(start, chunk)]
            out[depth - 1 - level, 0] = piece[:, :cols]
            out[depth - 1 - level, 1] = piece[:, cols:]

    substitute(depth, width, cols, get, sums, right, emit)


    if n_done + 1 < HALVES:
        return
    lefts.append((left, right))
    for row in range(HALVES):
        for col in range(HALVES):
            block = -complex_sum(times(lefts[row][0][...], lefts[col][1][...]), cols)
            for part in range(2):
                total[col, part, pl.ds(row * cols, cols)] = block[:, part * cols : (part + 1) * cols]
    for out, step in zip(outs, steps):
        start = rows_of(scalars, step, chunk)
        for col in range(HALVES):
            for part in range(2):
                out[depth + col, part] = total[col, part, pl.ds(start, chunk)]


def solve_last(depth, made, pieces, scalars, steps, chunk, width, cols, lefts):
    arrays, table = [], []
    for mask, part, array, base, stride in pieces:
        position = next((at for at, value in enumerate(arrays) if value is array), None)
        if position is None:
            position = len(arrays)
            arrays.append(array)
        table.append((mask, part, position, base, stride))
    order = []
    for level in range(depth - 1, 0, -1):
        order.append(("forward", level))
    for level in range(depth):
        order.append(("backward", level))
    done = len(lefts) + 1 == HALVES
    sources = operands(made, order) + ([value for left in lefts for value in left] if done else [])
    blocks = depth + (HALVES if done else 0)
    outs = [((blocks, 2, chunk, cols), F32, VMEM)] * len(steps)
    outs.append(((2 * cols, WIDE * depth * width), BF16, VMEM))
    outs.append(((WIDE * depth * width, 2 * cols), BF16, VMEM))
    scratch = [
        pltpu.VMEM((depth * width, 2 * cols), F32),
        pltpu.VMEM((width, 2 * cols), F32),
        pltpu.VMEM((HALVES, 2, width, cols), F32),
    ]
    kernel = functools.partial(
        last_kernel, depth, chunk, width, cols, steps, table, len(arrays), order,
        len(lefts) if done else 0,
    )
    flops = 24 * depth * depth * width * width * cols
    ins = [(scalars, SMEM)] + [(value, VMEM) for value in arrays]
    ins += [(value, VMEM) for value in sources]
    got = run_kernel(kernel, outs, ins, scratch, flops)
    return got[: len(steps)], got[len(steps) :]


def begin_kernel(plan, zeros, *refs):
    scalars = refs[0]
    pieces = refs[1 : 1 + len(plan)]
    out, zero_ref, sem = refs[1 + len(plan) :]
    zero_ref[...] = jnp.zeros_like(zero_ref)
    copies = []
    for slot, depth, count in zeros:
        copies.append((zero_ref.at[pl.ds(0, count)], out.at[0, slot, pl.ds(depth, count)]))
    for piece, (first, group, step, depth) in zip(pieces, plan):
        slot = first + ((scalars[2] // group) ^ step)
        copies.append((piece, out.at[0, slot, pl.ds(0, depth)]))
    copies = [
        pltpu.make_async_copy(source, target, sem.at[at])
        for at, (source, target) in enumerate(copies)
    ]
    for copy in copies:
        copy.start()
    for copy in copies:
        copy.wait()


def place_kernel(plan, depth, cols, half, diag_plan, shared, *refs):
    refs = list(refs)
    scalars = refs.pop(0)
    pieces = [refs.pop(0) for _ in plan]
    refs.pop(0)
    last_half = half + 1 == HALVES
    own = refs.pop(0) if last_half else None
    corrections = [refs.pop(0) for _ in diag_plan] if last_half else []
    out = refs.pop(0)
    diag = refs.pop(0) if last_half else None
    (sem,) = refs
    copies = []
    slots = [first + ((scalars[2] // group) ^ step) for first, group, step in plan]
    for at, (piece, slot) in enumerate(zip(pieces, slots)):
        target = out.at[0, slot, :, :, :, pl.ds(half * cols, cols)]
        copies.append(pltpu.make_async_copy(piece.at[pl.ds(0, depth)], target, sem.at[at]))
    for copy in copies:
        copy.start()
    if last_half:
        for slot in range(diag.shape[1]):
            value = own[0, slot]
            if slot in shared:
                value = jnp.where(scalars[5 + shared[slot]] == 1, value, 0.0)
            diag[0, slot] = value
        for correction, (first, group, step) in zip(corrections, diag_plan):
            slot = first + ((scalars[2] // group) ^ step)
            diag[0, slot] = diag[0, slot] - correction[...]
        for piece, slot in zip(pieces, slots):
            for col in range(HALVES):
                lanes = slice(col * cols, (col + 1) * cols)
                diag[0, slot, :, :, lanes] = diag[0, slot, :, :, lanes] - piece[depth + col]
    for copy in copies:
        copy.wait()


def body(lower_panel, diag_inverse, structure):
    columns = lax.axis_size("col")
    rows = lax.axis_size("row")
    position = lax.axis_index("col")
    place = lax.axis_index("row")
    slots, anc_count, _, chunk, width = lower_panel.shape[1:]
    per_col = [max(1, 2**depth // columns) for depth in range(LEVELS)]
    offsets = [sum(per_col[:depth]) for depth in range(LEVELS)]
    last = LEVELS - 1
    cols = width // HALVES
    groups = [rows // nodes for nodes in per_col]
    steps = [[step * groups[depth] for step in range(per_col[depth])] for depth in range(LEVELS)]
    shared = [depth for depth in range(LEVELS) if 2**depth < columns]
    middle = [depth for depth in range(LEVELS - 1) if 2**depth >= columns]
    active = [position % max(1, columns // 2**depth) == 0 for depth in range(LEVELS)]
    odd = position % 2 == 1
    scalars = [place, odd, jnp.where(odd, turned(place, rows), place)]
    scalars += [jnp.where(odd, turned(mask, rows), mask) for mask in (1, 2)]
    scalars = jnp.stack([jnp.asarray(value, jnp.int32) for value in scalars + active])
    present = structure[0]

    upper = shared[:-1]
    starts = [sum(1 + depth for depth in upper[:at]) for at in range(len(upper))]

    def level_blocks(depth, step=0):
        group = groups[depth]
        return [
            (offsets[depth], lambda at, group=group, step=step: (at // group) ^ step, block)
            for block in range(depth + 1)
        ]

    def packs(plan, depths, limit):
        spans = [(offsets[depth], per_col[depth], depth) for depth in depths if depth]
        return list(pack(plan, spans, scalars, present, lower_panel, diag_inverse, limit))

    plan = [sum([level_blocks(depth) for depth in upper], []), level_blocks(shared[-1])]
    near_rows, far_rows, bases = [], [], {}
    virtual = jnp.where(odd, turned(place, rows), place)
    for depth in middle:
        bases[depth] = sum(1 + held for held in bases)
        group, first = groups[depth], offsets[depth]
        for kept, step in ((near_rows, 0), (far_rows, 0 if group > 2 else 1)):
            slot = first + ((virtual // group) ^ step)
            diag = lax.dynamic_index_in_dim(diag_inverse[0], slot, 0, keepdims=False)
            panels = lax.dynamic_index_in_dim(lower_panel[0], slot, 0, keepdims=False)[:depth]
            kept += [diag, panels.reshape(2 * depth, chunk, width)]
    packed = packs(plan, shared, PACK_BYTES)
    upper_pack, own_pack = packed[:2]

    stride = columns // 2
    while stride >= 4:
        held = [at for at, depth in enumerate(upper) if columns // 2**depth >= 2 * stride]
        count = 2 * (starts[held[-1]] + 1 + upper[held[-1]])
        pairs = [(source, source + stride) for source in range(0, columns, 2 * stride)]
        if stride == columns // 2 and count == 2:
            travelling = diag_inverse[0, 0]
        else:
            travelling = upper_pack[:count]
        arrived = lax.ppermute(travelling, "col", pairs)
        fresh = position % (2 * stride) == stride
        upper_pack = jnp.concatenate(
            [jnp.where(fresh, arrived, upper_pack[:count]), upper_pack[count:]], axis=0
        )
        stride //= 2
    from_one = lax.ppermute(
        upper_pack, "col", [(source, source + 1) for source in range(0, columns, 4)]
    )
    from_three = lax.ppermute(
        upper_pack, "col", [(source, source + 3) for source in range(0, columns, 4)]
    )
    if middle:
        near_pack = jnp.concatenate(near_rows, axis=0)
        far_pack = jnp.concatenate(far_rows, axis=0)
        near_got = row_swap(near_pack, 1)
        far_got = row_swap(far_pack, 2)
        from_one, from_three, near_got, far_got = lax.optimization_barrier(
            (from_one, from_three, near_got, far_got)
        )
    upper_got = jnp.where(position % 4 == 1, from_one, from_three)
    planes = max(own_pack.shape[0], upper_got.shape[0])

    def fill(value):
        return jnp.pad(value, ((0, planes - value.shape[0]), (0, 0), (0, 0)))

    own = jnp.where(odd, fill(upper_got), fill(own_pack))

    near = row_swap(own, 1)
    far = row_swap(own, 2)

    def halves(value):
        return value.reshape(value.shape[0] // 2, 2, chunk, width)

    near_sends, far_sends = [halves(far)[:, 0]], [halves(near)[:, 1]]
    homes = {}
    near_size = far_size = planes // 2
    for depth in middle:
        first, count = 2 * bases[depth], 2 * (depth + 1)
        homes[depth] = (near_size, far_size)
        if groups[depth] > 2:
            near_sends.append(halves(far_got[first : first + count])[:, 0])
            far_sends.append(halves(near_got[first : first + count])[:, 1])
            near_size += depth + 1
            far_size += depth + 1
        else:
            near_sends.append(far_got[first : first + count])
            near_size += count
    near_sends = jnp.concatenate(near_sends, axis=0)
    far_sends = jnp.concatenate(far_sends, axis=0)
    nodes, group = per_col[last], groups[last]
    last_packs = pack_last(
        offsets[last], nodes, last, [(step, group) for step in range(nodes)], cols,
        scalars, present, lower_panel,
    )
    near_sends, far_sends, last_packs = lax.optimization_barrier(
        (near_sends, far_sends, last_packs)
    )
    near_more = row_swap(near_sends, 1)
    far_more = row_swap(far_sends, 2)
    near_more, far_more, last_packs = lax.optimization_barrier((near_more, far_more, last_packs))

    blocks = planes // 2
    mine = jnp.concatenate([own, near, far, near_more[:blocks], far_more[:blocks]], axis=0)
    theirs = col_swap(mine)
    shared_pieces = (
        both_parts(0, mine)
        + both_parts(1, mine, blocks)
        + both_parts(2, mine, 2 * blocks)
        + [(3, 0, mine, 6 * blocks, 1), (3, 1, mine, 7 * blocks, 1)]
    )

    made = {}
    for depth in middle:
        base = bases[depth]
        near_home, far_home = homes[depth]
        pieces = both_parts(0, near_pack, base) + both_parts(1, near_got, base)
        pieces += both_parts(2, far_got, base)
        if groups[depth] > 2:
            pieces += [(3, 0, near_more, near_home, 1), (3, 1, far_more, far_home, 1)]
        else:
            pieces += [(3, 0, near_more, near_home, 2), (3, 1, near_more, near_home + 1, 2)]
        level = (depth, None, 0, (offsets[depth], groups[depth]))
        made.update(prep([level], pieces, scalars, present, rows, chunk, width))
    levels = [(depth, True, starts[at], None) for at, depth in enumerate(upper)]
    levels.append((shared[-1], False, 0, None))
    made.update(
        prep(levels, shared_pieces, scalars, present, rows, chunk, width, others=[theirs])
    )
    last_pieces = []
    for half in range(HALVES):
        sent = last_packs[half * nodes : (half + 1) * nodes]
        if half:
            sent, made = lax.optimization_barrier((sent, made))
        pieces = []
        for step, value in zip(steps[last], sent):
            arrived = row_swap(value, step) if step else value
            if group == 1:
                pieces.append((step, arrived))
                continue
            listed = [(step, arrived)]
            mask = 1
            while mask < group:
                listed += [(mask | at, row_swap(held, mask)) for at, held in listed]
                mask *= 2
            pieces += listed
        last_pieces.append(pieces)

    single = [depth for depth in range(last - 1, 0, -1) if per_col[depth] == 1]
    solved = {}
    for depth in range(1, last):
        if per_col[depth] > 1:
            solved.update(solve([depth], made, scalars, steps[depth], chunk, width, ()))
    second = [value for _, value in last_pieces[-1][:2]]
    solved, second, later = lax.optimization_barrier((solved, second, scalars))
    last_pieces[-1][:2] = [
        (at, value) for (at, _), value in zip(last_pieces[-1][:2], second)
    ]
    lefts, backs = [], []
    for half in range(HALVES):
        outward, left = solve_last(
            last, made, sum([both_parts(at, held) for at, held in last_pieces[half]], []),
            later, steps[last], chunk, width, cols, lefts
        )
        lefts.append(left)
        if half + 1 == HALVES:
            outward, later = lax.optimization_barrier((outward, scalars))
        backs.append(
            [row_swap(piece, step) if step else piece for piece, step in zip(outward, steps[last])]
        )
    solved.update(solve(single, made, later, [0], chunk, width, tuple(shared)))

    begin_plan, begin_pieces, diag_plan, diag_pieces = [], [], [], []
    for depth in range(1, last):
        for step, (piece, correction) in enumerate(solved[depth]):
            if step:
                both = jnp.concatenate([piece, correction[None]], axis=0)
                both = row_swap(both, steps[depth][step])
                piece, correction = both[:depth], both[depth]
            begin_plan.append((offsets[depth], groups[depth], step, depth))
            begin_pieces.append(piece)
            diag_plan.append((offsets[depth], groups[depth], step))
            diag_pieces.append(correction)
    zeros = [
        (offsets[depth] + node, depth, anc_count - depth)
        for depth in range(LEVELS)
        for node in range(per_col[depth])
        if depth < anc_count
    ]
    panel_shape = lower_panel.shape
    (sel_panel,) = run_kernel(
        functools.partial(begin_kernel, begin_plan, zeros),
        [(panel_shape, F32, ANY)],
        [(scalars, SMEM)] + [(piece, VMEM) for piece in begin_pieces],
        [
            pltpu.VMEM((anc_count, 2, chunk, width), F32),
            pltpu.SemaphoreType.DMA((len(zeros) + len(begin_plan),)),
        ],
        0,
    )
    last_plan = [(offsets[last], group, step) for step in range(nodes)]
    masked = {offsets[depth]: depth for depth in shared}
    for half, back in enumerate(backs):
        ins = [(scalars, SMEM)] + [(piece, VMEM) for piece in back] + [(sel_panel, ANY)]
        outs = [(panel_shape, F32, ANY)]
        if half + 1 == HALVES:
            ins += [(diag_inverse, VMEM)] + [(piece, VMEM) for piece in diag_pieces]
            outs.append((diag_inverse.shape, F32, VMEM))
        made_now = run_kernel(
            functools.partial(place_kernel, last_plan, last, cols, half, diag_plan, masked),
            outs,
            ins,
            [pltpu.SemaphoreType.DMA((nodes,))],
            0,
            aliases={1 + nodes: 0},
        )
        sel_panel = made_now[0]
    return (sel_panel, made_now[1])


def solution(mesh):
    in_specs = (
        P("col", None, None, None, "row", None),
        P("col", None, None, "row", None),
        P("col", None, None),
    )
    out_specs = (P("col", None, None, None, "row", None), P("col", None, None, "row", None))
    return jax.shard_map(body, mesh=mesh, in_specs=in_specs, out_specs=out_specs, check_vma=False)
```

```python
import functools

import jax
import jax.numpy as jnp
from jax import lax
from jax.experimental import pallas as pl
from jax.experimental.pallas import tpu as pltpu
from jax.sharding import PartitionSpec as P

LEVELS = 6
HALVES = 2
VMEM_BYTES = 18 * 2**20
PACK_BYTES = 58 * 2**20
F32 = jnp.float32
BF16 = jnp.bfloat16
ANY = pl.BlockSpec(memory_space=pl.ANY)
VMEM = pl.BlockSpec(memory_space=pltpu.VMEM)
SMEM = pl.BlockSpec(memory_space=pltpu.SMEM)


def turned(mask, rows):
    if rows < 4:
        return mask
    return (mask & ~3) | ((mask & 1) << 1) | ((mask >> 1) & 1)


def col_swap(value):
    count = lax.axis_size("col")
    return lax.ppermute(value, "col", [(source, source ^ 1) for source in range(count)])


def row_swap(value, mask):
    rows, columns = lax.axis_size("row"), lax.axis_size("col")
    pairs = []
    for row in range(rows):
        for col in range(columns):
            other = row ^ (turned(mask, rows) if col % 2 else mask)
            pairs.append((row * columns + col, other * columns + col))
    return lax.ppermute(value, ("row", "col"), pairs)


def rows_of(scalars, mask, chunk):
    away = mask & ~3
    if mask & 1:
        away = away | scalars[3]
    if mask & 2:
        away = away | scalars[4]
    return pl.multiple_of((scalars[0] ^ away) * chunk, chunk)


def split(value):
    high = value.astype(BF16)
    return high, (value - high.astype(F32)).astype(BF16)


WIDE = 3


def store_left(ref, rows, first, value):
    high, low = split(value)
    size = value.shape[1]
    for at, part in enumerate((high, high, low)):
        ref[rows, pl.ds(first + at * size, size)] = part


def store_right(ref, first, value):
    high, low = split(value)
    size = value.shape[0]
    for at, part in enumerate((high, low, high)):
        ref[pl.ds(first + at * size, size)] = part


def times(left, right):
    return jnp.dot(left, right, preferred_element_type=F32)


def complex_sum(product, half):
    count = product.shape[0] // 2
    by_real, by_imag = product[:count], product[count:]
    return jnp.concatenate(
        [by_real[:, :half] - by_imag[:, half:], by_real[:, half:] + by_imag[:, :half]], axis=1
    )


def run_kernel(kernel, outs, ins, scratch, flops, aliases=None, limit=VMEM_BYTES):
    moved = sum(value.size for value, _ in ins)
    return pl.pallas_call(
        kernel,
        out_shape=[jax.ShapeDtypeStruct(shape, dtype) for shape, dtype, _ in outs],
        in_specs=[spec for _, spec in ins],
        out_specs=[spec for _, _, spec in outs],
        scratch_shapes=scratch,
        input_output_aliases=aliases or {},
        compiler_params=pltpu.CompilerParams(vmem_limit_bytes=limit),
        cost_estimate=pl.CostEstimate(flops=flops // 64, bytes_accessed=moved // 64, transcendentals=0),
    )(*[value for value, _ in ins])


class Loads:
    def __init__(self, sources, buffers, sems):
        self.buffers = buffers
        self.copies = [
            pltpu.make_async_copy(source, buffer, sems.at[at])
            for at, (source, buffer) in enumerate(zip(sources, buffers))
        ]
        for copy in self.copies:
            copy.start()

    def get(self, at):
        if self.copies[at] is not None:
            self.copies[at].wait()
            self.copies[at] = None
        return self.buffers[at]


def both_parts(mask, array, base=0):
    return [(mask, 0, array, 2 * base, 2), (mask, 1, array, 2 * base + 1, 2)]


def pack_kernel(spans, plan, n_outs, chunk, *refs):
    scalars, present, panel_ref, diag_ref = refs[:4]
    outs = refs[4 : 4 + n_outs]
    panel_bufs = refs[4 + n_outs : -2]
    diag_buf, sems = refs[-2:]
    sources, buffers = [], []
    for (first, nodes, depth), buffer in zip(spans, panel_bufs):
        sources.append(panel_ref.at[0, pl.ds(first, nodes), pl.ds(0, depth)])
        buffers.append(buffer)
    if any(block == 0 for blocks in plan for _, _, block in blocks):
        sources.append(diag_ref.at[0])
        buffers.append(diag_buf)
    loads = Loads(sources, buffers, sems)
    where = {first: at for at, (first, _, _) in enumerate(spans)}
    for out, blocks in zip(outs, plan):
        for at, (first, node_of, block) in enumerate(blocks):
            node = node_of(scalars[2])
            if block == 0:
                value = loads.get(len(spans))[first + node]
            else:
                scale = present[first + node, block - 1].astype(F32)
                value = loads.get(where[first])[node, block - 1] * scale
            out[pl.ds(2 * at, 2)] = value


def pack(plan, spans, scalars, present, lower_panel, diag_inverse, limit):
    chunk, width = lower_panel.shape[-2:]
    outs = [((2 * len(blocks), chunk, width), F32, VMEM) for blocks in plan]
    scratch = [pltpu.VMEM((nodes, depth, 2, chunk, width), F32) for _, nodes, depth in spans]
    scratch += [pltpu.VMEM(diag_inverse.shape[1:], F32), pltpu.SemaphoreType.DMA((len(spans) + 1,))]
    kernel = functools.partial(pack_kernel, spans, plan, len(outs), chunk)
    ins = [(scalars, SMEM), (present, SMEM), (lower_panel, ANY), (diag_inverse, ANY)]
    return run_kernel(kernel, outs, ins, scratch, 0, limit=limit)


def pack_last_kernel(first, nodes, depth, steps, cols, *refs):
    scalars, present, panel_ref = refs[:3]
    outs = refs[3 : 3 + len(steps) * HALVES]
    buffer, sem = refs[-2:]
    copy = pltpu.make_async_copy(panel_ref.at[0, pl.ds(first, nodes), pl.ds(0, depth)], buffer, sem)
    copy.start()
    copy.wait()
    for at, (step, group) in enumerate(steps):
        node = (scalars[2] // group) ^ step
        for block in range(depth):
            value = buffer[node, block] * present[first + node, block].astype(F32)
            for half in range(HALVES):
                outs[half * len(steps) + at][pl.ds(2 * block, 2)] = value[
                    :, :, half * cols : (half + 1) * cols
                ]


def pack_last(first, nodes, depth, steps, cols, scalars, present, lower_panel):
    chunk, width = lower_panel.shape[-2:]
    outs = [((2 * depth, chunk, cols), F32, VMEM)] * (len(steps) * HALVES)
    scratch = [pltpu.VMEM((nodes, depth, 2, chunk, width), F32), pltpu.SemaphoreType.DMA]
    kernel = functools.partial(pack_last_kernel, first, nodes, depth, steps, cols)
    ins = [(scalars, SMEM), (present, SMEM), (lower_panel, ANY)]
    return run_kernel(kernel, outs, ins, scratch, 0)


def prep_kernel(levels, table, rows_count, chunk, width, n_arrays, *refs):
    scalars, present = refs[:2]
    arrays = refs[2 : 2 + n_arrays]
    outs = list(refs[2 + n_arrays :])
    odd = scalars[1] == 1
    for depth, swapped, first, slot in levels:
        if depth:
            whole, forward = outs.pop(0), outs.pop(0)
        else:
            whole = None
        backward = outs.pop(0)
        for block in range(depth + 1):
            for mask, part, position, base, stride in table:
                plane = base + stride * (first + block)
                start = rows_of(scalars, mask, chunk)
                if swapped is None:
                    value = arrays[position][plane]
                else:
                    half = n_arrays // 2
                    from_odd = arrays[position + (0 if swapped else half)]
                    from_even = arrays[position + (half if swapped else 0)]
                    value = jnp.where(odd, from_odd[plane], from_even[plane])
                    away = turned(mask, rows_count) if swapped else mask
                    start = pl.multiple_of((scalars[0] ^ away) * chunk, chunk)
                if block == 0:
                    rows = pl.ds(pl.multiple_of(part * width + start, chunk), chunk)
                    store_left(backward, rows, WIDE * depth * width, value)
                else:
                    if slot is not None:
                        at = slot[0] + scalars[2] // slot[1]
                        value = value * present[at, block - 1].astype(F32)
                    rows = pl.ds(pl.multiple_of((depth - block) * width + start, chunk), chunk)
                    whole[rows, pl.ds(part * width, width)] = value
        for level in range(depth):
            for part in range(2):
                value = whole[pl.ds(level * width, width), pl.ds(part * width, width)]
                store_left(forward, pl.ds((2 * level + part) * width, width), 0, value)
                rows = pl.ds(part * width, width)
                store_left(backward, rows, WIDE * level * width, -value.T)


def prep(levels, pieces, scalars, present, rows, chunk, width, others=()):
    arrays, table = [], []
    for mask, part, array, base, stride in pieces:
        position = next((at for at, value in enumerate(arrays) if value is array), None)
        if position is None:
            position = len(arrays)
            arrays.append(array)
        table.append((mask, part, position, base, stride))
    arrays = arrays + list(others)
    outs = []
    for depth, _, _, _ in levels:
        if depth:
            outs.append(((depth * width, 2 * width), F32, VMEM))
            outs.append(((2 * depth * width, WIDE * width), BF16, VMEM))
        outs.append(((2 * width, WIDE * (depth + 1) * width), BF16, VMEM))
    kernel = functools.partial(prep_kernel, levels, table, rows, chunk, width, len(arrays))
    ins = [(scalars, SMEM), (present, SMEM)] + [(value, VMEM) for value in arrays]
    made = list(run_kernel(kernel, outs, ins, [], 0))
    result = {}
    for depth, _, _, _ in levels:
        if depth:
            result[depth], made = tuple(made[:3]), made[3:]
        else:
            result[depth], made = (None, None, made[0]), made[1:]
    return result


def substitute(depth, width, cols, get, sums, right, emit):
    def rows(first, count=1):
        return pl.ds(first * width, count * width)

    for level in range(depth - 1, 0, -1):
        store_right(right, WIDE * level * width, sums[rows(level)])
        forward = get("forward", level)
        for block in range(level - 1, -1, -1):
            product = times(forward[rows(2 * block, 2)], right[rows(WIDE * level, WIDE)])
            sums[rows(block)] -= complex_sum(product, cols)
    store_right(right, 0, sums[rows(0)])
    for level in range(depth):
        product = times(get("backward", level)[...], right[rows(0, WIDE * (level + 1))])
        solved = complex_sum(product, cols)
        store_right(right, WIDE * level * width, solved)
        emit(level, solved)


def solve_kernel(depths, chunk, width, steps, order, masked, *refs):
    refs = list(refs)
    scalars = refs.pop(0)
    sources = [refs.pop(0) for _ in order]
    outs = {depth: [(refs.pop(0), refs.pop(0)) for _ in steps] for depth in depths}
    sums_ref, right_ref, solved_ref = refs

    def get(kind, level):
        return sources[order.index((kind, level))]

    for depth in depths:
        sums = sums_ref.at[pl.ds(0, depth * width)]
        right = right_ref.at[pl.ds(0, WIDE * depth * width)]
        sums[...] = get("whole", depth)[...]

        def send(block, value, sign):
            solved_ref[...] = value
            for (out, correction), step in zip(outs[depth], steps):
                start = rows_of(scalars, step, chunk)
                piece = solved_ref[pl.ds(start, chunk)] * sign
                if depth in masked:
                    piece = jnp.where(scalars[5 + depth] == 1, piece, 0.0)
                for part in range(2):
                    plane = piece[:, part * width : (part + 1) * width]
                    if block == 0:
                        correction[part] = plane
                    else:
                        out[block - 1, part] = plane

        substitute(
            depth, width, width, get, sums, right,
            lambda level, solved: send(depth - level, solved, -1.0),
        )
        product = times(get("backward", depth)[:, : WIDE * depth * width], right[...])
        send(0, complex_sum(product, width), 1.0)


def operands(made, names):
    index = {"whole": 0, "forward": 1, "backward": 2}
    return [made[level][index[kind]] for kind, level in names]


def solve(depths, made, scalars, steps, chunk, width, masked):
    top = depths[0]
    order = [("whole", top)]
    for level in range(top - 1, 0, -1):
        order.append(("forward", level))
    for level in range(top + 1):
        order.append(("backward", level))
    order += [("whole", depth) for depth in depths[1:]]
    sources = operands(made, order)
    outs = []
    for depth in depths:
        for _ in steps:
            outs.append(((depth, 2, chunk, width), F32, VMEM))
            outs.append(((2, chunk, width), F32, VMEM))
    scratch = [
        pltpu.VMEM((top * width, 2 * width), F32),
        pltpu.VMEM((WIDE * top * width, 2 * width), BF16),
        pltpu.VMEM((width, 2 * width), F32),
    ]
    kernel = functools.partial(solve_kernel, depths, chunk, width, steps, order, masked)
    flops = sum(24 * (depth * depth + depth) * width**3 for depth in depths)
    ins = [(scalars, SMEM)] + [(value, VMEM) for value in sources]
    got = list(run_kernel(kernel, outs, ins, scratch, flops))
    result = {}
    for depth in depths:
        result[depth] = [(got.pop(0), got.pop(0)) for _ in steps]
    return result


def last_kernel(depth, chunk, width, cols, steps, table, n_arrays, order, n_done, *refs):
    refs = list(refs)
    scalars = refs.pop(0)
    arrays = [refs.pop(0) for _ in range(n_arrays)]
    sources = [refs.pop(0) for _ in order]
    lefts = [(refs.pop(0), refs.pop(0)) for _ in range(n_done)]
    outs = [refs.pop(0) for _ in steps]
    left, right = refs.pop(0), refs.pop(0)
    sums, solved_ref, total = refs

    def get(kind, level):
        return sources[order.index((kind, level))]

    for mask, part, position, base, stride in table:
        start = rows_of(scalars, mask, chunk)
        for block in range(depth):
            row = pl.multiple_of((depth - 1 - block) * width + start, chunk)
            sums[pl.ds(row, chunk), pl.ds(part * cols, cols)] = arrays[position][base + stride * block]
    for level in range(depth):
        for part in range(2):
            value = sums[pl.ds(level * width, width), pl.ds(part * cols, cols)]
            store_left(left, pl.ds(part * cols, cols), WIDE * level * width, value.T)

    def emit(level, value):
        solved_ref[...] = value
        for out, step in zip(outs, steps):
            start = rows_of(scalars, step, chunk)
            piece = -solved_ref[pl.ds(start, chunk)]
            out[depth - 1 - level, 0] = piece[:, :cols]
            out[depth - 1 - level, 1] = piece[:, cols:]

    substitute(depth, width, cols, get, sums, right, emit)


    if n_done + 1 < HALVES:
        return
    lefts.append((left, right))
    for row in range(HALVES):
        for col in range(HALVES):
            block = -complex_sum(times(lefts[row][0][...], lefts[col][1][...]), cols)
            for part in range(2):
                total[col, part, pl.ds(row * cols, cols)] = block[:, part * cols : (part + 1) * cols]
    for out, step in zip(outs, steps):
        start = rows_of(scalars, step, chunk)
        for col in range(HALVES):
            for part in range(2):
                out[depth + col, part] = total[col, part, pl.ds(start, chunk)]


def solve_last(depth, made, pieces, scalars, steps, chunk, width, cols, lefts):
    arrays, table = [], []
    for mask, part, array, base, stride in pieces:
        position = next((at for at, value in enumerate(arrays) if value is array), None)
        if position is None:
            position = len(arrays)
            arrays.append(array)
        table.append((mask, part, position, base, stride))
    order = []
    for level in range(depth - 1, 0, -1):
        order.append(("forward", level))
    for level in range(depth):
        order.append(("backward", level))
    done = len(lefts) + 1 == HALVES
    sources = operands(made, order) + ([value for left in lefts for value in left] if done else [])
    blocks = depth + (HALVES if done else 0)
    outs = [((blocks, 2, chunk, cols), F32, VMEM)] * len(steps)
    outs.append(((2 * cols, WIDE * depth * width), BF16, VMEM))
    outs.append(((WIDE * depth * width, 2 * cols), BF16, VMEM))
    scratch = [
        pltpu.VMEM((depth * width, 2 * cols), F32),
        pltpu.VMEM((width, 2 * cols), F32),
        pltpu.VMEM((HALVES, 2, width, cols), F32),
    ]
    kernel = functools.partial(
        last_kernel, depth, chunk, width, cols, steps, table, len(arrays), order,
        len(lefts) if done else 0,
    )
    flops = 24 * depth * depth * width * width * cols
    ins = [(scalars, SMEM)] + [(value, VMEM) for value in arrays]
    ins += [(value, VMEM) for value in sources]
    got = run_kernel(kernel, outs, ins, scratch, flops)
    return got[: len(steps)], got[len(steps) :]


def begin_kernel(plan, zeros, *refs):
    scalars = refs[0]
    pieces = refs[1 : 1 + len(plan)]
    out, zero_ref, sem = refs[1 + len(plan) :]
    zero_ref[...] = jnp.zeros_like(zero_ref)
    copies = []
    for slot, depth, count in zeros:
        copies.append((zero_ref.at[pl.ds(0, count)], out.at[0, slot, pl.ds(depth, count)]))
    for piece, (first, group, step, depth) in zip(pieces, plan):
        slot = first + ((scalars[2] // group) ^ step)
        copies.append((piece, out.at[0, slot, pl.ds(0, depth)]))
    copies = [
        pltpu.make_async_copy(source, target, sem.at[at])
        for at, (source, target) in enumerate(copies)
    ]
    for copy in copies:
        copy.start()
    for copy in copies:
        copy.wait()


def place_kernel(plan, depth, cols, half, late_plan, diag_plan, shared, *refs):
    refs = list(refs)
    scalars = refs.pop(0)
    pieces = [refs.pop(0) for _ in plan]
    refs.pop(0)
    last_half = half + 1 == HALVES
    own = refs.pop(0) if last_half else None
    late = [refs.pop(0) for _ in late_plan] if last_half else []
    corrections = [refs.pop(0) for _ in diag_plan] if last_half else []
    out = refs.pop(0)
    diag = refs.pop(0) if last_half else None
    (sem,) = refs
    copies = []
    slots = [first + ((scalars[2] // group) ^ step) for first, group, step in plan]
    for at, (piece, slot) in enumerate(zip(pieces, slots)):
        target = out.at[0, slot, :, :, :, pl.ds(half * cols, cols)]
        copies.append(pltpu.make_async_copy(piece.at[pl.ds(0, depth)], target, sem.at[at]))
    for piece, (slot, level) in zip(late, late_plan):
        target = out.at[0, slot, pl.ds(0, level)]
        copies.append(pltpu.make_async_copy(piece, target, sem.at[len(copies)]))
    for copy in copies:
        copy.start()
    if last_half:
        for slot in range(diag.shape[1]):
            value = own[0, slot]
            if slot in shared:
                value = jnp.where(scalars[5 + shared[slot]] == 1, value, 0.0)
            diag[0, slot] = value
        for correction, (first, group, step) in zip(corrections, diag_plan):
            slot = first + ((scalars[2] // group) ^ step)
            diag[0, slot] = diag[0, slot] - correction[...]
        for piece, slot in zip(pieces, slots):
            for col in range(HALVES):
                lanes = slice(col * cols, (col + 1) * cols)
                diag[0, slot, :, :, lanes] = diag[0, slot, :, :, lanes] - piece[depth + col]
    for copy in copies:
        copy.wait()


def body(lower_panel, diag_inverse, structure):
    columns = lax.axis_size("col")
    rows = lax.axis_size("row")
    position = lax.axis_index("col")
    place = lax.axis_index("row")
    slots, anc_count, _, chunk, width = lower_panel.shape[1:]
    per_col = [max(1, 2**depth // columns) for depth in range(LEVELS)]
    offsets = [sum(per_col[:depth]) for depth in range(LEVELS)]
    last = LEVELS - 1
    cols = width // HALVES
    groups = [rows // nodes for nodes in per_col]
    steps = [[step * groups[depth] for step in range(per_col[depth])] for depth in range(LEVELS)]
    shared = [depth for depth in range(LEVELS) if 2**depth < columns]
    middle = [depth for depth in range(LEVELS - 1) if 2**depth >= columns]
    active = [position % max(1, columns // 2**depth) == 0 for depth in range(LEVELS)]
    odd = position % 2 == 1
    scalars = [place, odd, jnp.where(odd, turned(place, rows), place)]
    scalars += [jnp.where(odd, turned(mask, rows), mask) for mask in (1, 2)]
    scalars = jnp.stack([jnp.asarray(value, jnp.int32) for value in scalars + active])
    present = structure[0]

    upper = shared[:-1]
    starts = [sum(1 + depth for depth in upper[:at]) for at in range(len(upper))]

    def level_blocks(depth, step=0):
        group = groups[depth]
        return [
            (offsets[depth], lambda at, group=group, step=step: (at // group) ^ step, block)
            for block in range(depth + 1)
        ]

    def packs(plan, depths, limit):
        spans = [(offsets[depth], per_col[depth], depth) for depth in depths if depth]
        return list(pack(plan, spans, scalars, present, lower_panel, diag_inverse, limit))

    plan = [sum([level_blocks(depth) for depth in upper], []), level_blocks(shared[-1])]
    near_rows, far_rows, bases = [], [], {}
    virtual = jnp.where(odd, turned(place, rows), place)
    for depth in middle:
        bases[depth] = sum(1 + held for held in bases)
        group, first = groups[depth], offsets[depth]
        for kept, step in ((near_rows, 0), (far_rows, 0 if group > 2 else 1)):
            slot = first + ((virtual // group) ^ step)
            diag = lax.dynamic_index_in_dim(diag_inverse[0], slot, 0, keepdims=False)
            panels = lax.dynamic_index_in_dim(lower_panel[0], slot, 0, keepdims=False)[:depth]
            kept += [diag, panels.reshape(2 * depth, chunk, width)]
    packed = packs(plan, shared, PACK_BYTES)
    upper_pack, own_pack = packed[:2]

    stride = columns // 2
    while stride >= 4:
        held = [at for at, depth in enumerate(upper) if columns // 2**depth >= 2 * stride]
        count = 2 * (starts[held[-1]] + 1 + upper[held[-1]])
        pairs = [(source, source + stride) for source in range(0, columns, 2 * stride)]
        if stride == columns // 2 and count == 2:
            travelling = diag_inverse[0, 0]
        else:
            travelling = upper_pack[:count]
        arrived = lax.ppermute(travelling, "col", pairs)
        fresh = position % (2 * stride) == stride
        upper_pack = jnp.concatenate(
            [jnp.where(fresh, arrived, upper_pack[:count]), upper_pack[count:]], axis=0
        )
        stride //= 2
    from_one = lax.ppermute(
        upper_pack, "col", [(source, source + 1) for source in range(0, columns, 4)]
    )
    from_three = lax.ppermute(
        upper_pack, "col", [(source, source + 3) for source in range(0, columns, 4)]
    )
    if middle:
        near_pack = jnp.concatenate(near_rows, axis=0)
        far_pack = jnp.concatenate(far_rows, axis=0)
        near_got = row_swap(near_pack, 1)
        far_got = row_swap(far_pack, 2)
        from_one, from_three, near_got, far_got = lax.optimization_barrier(
            (from_one, from_three, near_got, far_got)
        )
    upper_got = jnp.where(position % 4 == 1, from_one, from_three)
    planes = max(own_pack.shape[0], upper_got.shape[0])

    def fill(value):
        return jnp.pad(value, ((0, planes - value.shape[0]), (0, 0), (0, 0)))

    own = jnp.where(odd, fill(upper_got), fill(own_pack))

    near = row_swap(own, 1)
    far = row_swap(own, 2)

    def halves(value):
        return value.reshape(value.shape[0] // 2, 2, chunk, width)

    near_sends, far_sends, pair_sends = [halves(far)[:, 0]], [halves(near)[:, 1]], []
    homes = {}
    size, pair_size = planes // 2, 0
    for depth in middle:
        first, count = 2 * bases[depth], 2 * (depth + 1)
        if groups[depth] > 2:
            homes[depth] = size
            near_sends.append(halves(far_got[first : first + count])[:, 0])
            far_sends.append(halves(near_got[first : first + count])[:, 1])
            size += depth + 1
        else:
            homes[depth] = pair_size
            pair_sends.append(far_got[first : first + count])
            pair_size += count
    near_sends = jnp.concatenate(near_sends, axis=0)
    far_sends = jnp.concatenate(far_sends, axis=0)
    pair_sends = [jnp.concatenate(pair_sends, axis=0)] if pair_sends else []
    nodes, group = per_col[last], groups[last]
    last_packs = pack_last(
        offsets[last], nodes, last, [(step, group) for step in range(nodes)], cols,
        scalars, present, lower_panel,
    )
    pair_more = [row_swap(value, 1) for value in pair_sends]
    near_sends, far_sends, pair_more, last_packs = lax.optimization_barrier(
        (near_sends, far_sends, pair_more, last_packs)
    )
    near_more = row_swap(near_sends, 1)
    far_more = row_swap(far_sends, 2)
    near_more, far_more, last_packs = lax.optimization_barrier((near_more, far_more, last_packs))

    blocks = planes // 2
    mine = jnp.concatenate([own, near, far, near_more[:blocks], far_more[:blocks]], axis=0)
    theirs = col_swap(mine)
    shared_pieces = (
        both_parts(0, mine)
        + both_parts(1, mine, blocks)
        + both_parts(2, mine, 2 * blocks)
        + [(3, 0, mine, 6 * blocks, 1), (3, 1, mine, 7 * blocks, 1)]
    )

    made = {}
    for depth in middle:
        base = bases[depth]
        home = homes[depth]
        pieces = both_parts(0, near_pack, base) + both_parts(1, near_got, base)
        pieces += both_parts(2, far_got, base)
        if groups[depth] > 2:
            pieces += [(3, 0, near_more, home, 1), (3, 1, far_more, home, 1)]
        else:
            pieces += [(3, 0, pair_more[0], home, 2), (3, 1, pair_more[0], home + 1, 2)]
        level = (depth, None, 0, (offsets[depth], groups[depth]))
        made.update(prep([level], pieces, scalars, present, rows, chunk, width))
    levels = [(depth, True, starts[at], None) for at, depth in enumerate(upper)]
    levels.append((shared[-1], False, 0, None))
    made.update(
        prep(levels, shared_pieces, scalars, present, rows, chunk, width, others=[theirs])
    )
    last_pieces = []
    for half in range(HALVES):
        sent = last_packs[half * nodes : (half + 1) * nodes]
        if half:
            sent, made = lax.optimization_barrier((sent, made))
        pieces = []
        for step, value in zip(steps[last], sent):
            arrived = row_swap(value, step) if step else value
            if group == 1:
                pieces.append((step, arrived))
                continue
            listed = [(step, arrived)]
            mask = 1
            while mask < group:
                listed += [(mask | at, row_swap(held, mask)) for at, held in listed]
                mask *= 2
            pieces += listed
        last_pieces.append(pieces)

    single = [depth for depth in range(last - 1, 0, -1) if per_col[depth] == 1]
    solved = {}
    for depth in range(1, last):
        if per_col[depth] > 1:
            solved.update(solve([depth], made, scalars, steps[depth], chunk, width, ()))
    second = [value for _, value in last_pieces[-1][:-1]]
    solved, second, later = lax.optimization_barrier((solved, second, scalars))
    last_pieces[-1][:-1] = [
        (at, value) for (at, _), value in zip(last_pieces[-1][:-1], second)
    ]
    lefts, backs = [], []
    for half in range(HALVES):
        outward, left = solve_last(
            last, made, sum([both_parts(at, held) for at, held in last_pieces[half]], []),
            later, steps[last], chunk, width, cols, lefts
        )
        lefts.append(left)
        if half + 1 == HALVES:
            outward, later = lax.optimization_barrier((outward, scalars))
        backs.append(
            [row_swap(piece, step) if step else piece for piece, step in zip(outward, steps[last])]
        )
    solved.update(solve(single, made, later, [0], chunk, width, tuple(shared)))

    begin_plan, begin_pieces, diag_plan, diag_pieces = [], [], [], []
    late_plan, late_pieces = [], []
    for depth in range(1, last):
        for step, (piece, correction) in enumerate(solved[depth]):
            if step:
                both = jnp.concatenate([piece, correction[None]], axis=0)
                both = row_swap(both, steps[depth][step])
                piece, correction = both[:depth], both[depth]
            if per_col[depth] == 1:
                late_plan.append((offsets[depth], depth))
                late_pieces.append(piece)
            else:
                begin_plan.append((offsets[depth], groups[depth], step, depth))
                begin_pieces.append(piece)
            diag_plan.append((offsets[depth], groups[depth], step))
            diag_pieces.append(correction)
    zeros = [
        (offsets[depth] + node, depth, anc_count - depth)
        for depth in range(LEVELS)
        for node in range(per_col[depth])
        if depth < anc_count
    ]
    panel_shape = lower_panel.shape
    (sel_panel,) = run_kernel(
        functools.partial(begin_kernel, begin_plan, zeros),
        [(panel_shape, F32, ANY)],
        [(scalars, SMEM)] + [(piece, VMEM) for piece in begin_pieces],
        [
            pltpu.VMEM((anc_count, 2, chunk, width), F32),
            pltpu.SemaphoreType.DMA((len(zeros) + len(begin_plan),)),
        ],
        0,
    )
    last_plan = [(offsets[last], group, step) for step in range(nodes)]
    masked = {offsets[depth]: depth for depth in shared}
    for half, back in enumerate(backs):
        ins = [(scalars, SMEM)] + [(piece, VMEM) for piece in back] + [(sel_panel, ANY)]
        outs = [(panel_shape, F32, ANY)]
        if half + 1 == HALVES:
            ins += [(diag_inverse, VMEM)]
            ins += [(piece, VMEM) for piece in late_pieces + diag_pieces]
            outs.append((diag_inverse.shape, F32, VMEM))
        made_now = run_kernel(
            functools.partial(
                place_kernel, last_plan, last, cols, half, late_plan, diag_plan, masked
            ),
            outs,
            ins,
            [pltpu.SemaphoreType.DMA((nodes + len(late_plan),))],
            0,
            aliases={1 + nodes: 0},
        )
        sel_panel = made_now[0]
    return (sel_panel, made_now[1])


def solution(mesh):
    in_specs = (
        P("col", None, None, None, "row", None),
        P("col", None, None, "row", None),
        P("col", None, None),
    )
    out_specs = (P("col", None, None, None, "row", None), P("col", None, None, "row", None))
    return jax.shard_map(body, mesh=mesh, in_specs=in_specs, out_specs=out_specs, check_vma=False)
```

```python
import functools

import jax
import jax.numpy as jnp
from jax import lax
from jax.experimental import pallas as pl
from jax.experimental.pallas import tpu as pltpu
from jax.sharding import PartitionSpec as P

LEVELS = 6
HALVES = 2
VMEM_BYTES = 18 * 2**20
PACK_BYTES = 58 * 2**20
F32 = jnp.float32
BF16 = jnp.bfloat16
ANY = pl.BlockSpec(memory_space=pl.ANY)
VMEM = pl.BlockSpec(memory_space=pltpu.VMEM)
SMEM = pl.BlockSpec(memory_space=pltpu.SMEM)


def turned(mask, rows):
    if rows < 4:
        return mask
    return (mask & ~3) | ((mask & 1) << 1) | ((mask >> 1) & 1)


def col_swap(value):
    count = lax.axis_size("col")
    return lax.ppermute(value, "col", [(source, source ^ 1) for source in range(count)])


def row_swap(value, mask):
    rows, columns = lax.axis_size("row"), lax.axis_size("col")
    pairs = []
    for row in range(rows):
        for col in range(columns):
            other = row ^ (turned(mask, rows) if col % 2 else mask)
            pairs.append((row * columns + col, other * columns + col))
    return lax.ppermute(value, ("row", "col"), pairs)


def rows_of(scalars, mask, chunk):
    away = mask & ~3
    if mask & 1:
        away = away | scalars[3]
    if mask & 2:
        away = away | scalars[4]
    return pl.multiple_of((scalars[0] ^ away) * chunk, chunk)


def split(value):
    high = value.astype(BF16)
    return high, (value - high.astype(F32)).astype(BF16)


WIDE = 3


def store_left(ref, rows, first, value):
    high, low = split(value)
    size = value.shape[1]
    for at, part in enumerate((high, high, low)):
        ref[rows, pl.ds(first + at * size, size)] = part


def store_right(ref, first, value):
    high, low = split(value)
    size = value.shape[0]
    for at, part in enumerate((high, low, high)):
        ref[pl.ds(first + at * size, size)] = part


def times(left, right):
    return jnp.dot(left, right, preferred_element_type=F32)


def complex_sum(product, half):
    count = product.shape[0] // 2
    by_real, by_imag = product[:count], product[count:]
    return jnp.concatenate(
        [by_real[:, :half] - by_imag[:, half:], by_real[:, half:] + by_imag[:, :half]], axis=1
    )


def run_kernel(kernel, outs, ins, scratch, flops, aliases=None, limit=VMEM_BYTES):
    moved = sum(value.size for value, _ in ins)
    return pl.pallas_call(
        kernel,
        out_shape=[jax.ShapeDtypeStruct(shape, dtype) for shape, dtype, _ in outs],
        in_specs=[spec for _, spec in ins],
        out_specs=[spec for _, _, spec in outs],
        scratch_shapes=scratch,
        input_output_aliases=aliases or {},
        compiler_params=pltpu.CompilerParams(vmem_limit_bytes=limit),
        cost_estimate=pl.CostEstimate(flops=flops // 64, bytes_accessed=moved // 64, transcendentals=0),
    )(*[value for value, _ in ins])


class Loads:
    def __init__(self, sources, buffers, sems):
        self.buffers = buffers
        self.copies = [
            pltpu.make_async_copy(source, buffer, sems.at[at])
            for at, (source, buffer) in enumerate(zip(sources, buffers))
        ]
        for copy in self.copies:
            copy.start()

    def get(self, at):
        if self.copies[at] is not None:
            self.copies[at].wait()
            self.copies[at] = None
        return self.buffers[at]


def both_parts(mask, array, base=0):
    return [(mask, 0, array, 2 * base, 2), (mask, 1, array, 2 * base + 1, 2)]


def pack_kernel(spans, plan, n_outs, chunk, *refs):
    scalars, present, panel_ref, diag_ref = refs[:4]
    outs = refs[4 : 4 + n_outs]
    panel_bufs = refs[4 + n_outs : -2]
    diag_buf, sems = refs[-2:]
    sources, buffers = [], []
    for (first, nodes, depth), buffer in zip(spans, panel_bufs):
        sources.append(panel_ref.at[0, pl.ds(first, nodes), pl.ds(0, depth)])
        buffers.append(buffer)
    if any(block == 0 for blocks in plan for _, _, block in blocks):
        sources.append(diag_ref.at[0])
        buffers.append(diag_buf)
    loads = Loads(sources, buffers, sems)
    where = {first: at for at, (first, _, _) in enumerate(spans)}
    for out, blocks in zip(outs, plan):
        for at, (first, node_of, block) in enumerate(blocks):
            node = node_of(scalars[2])
            if block == 0:
                value = loads.get(len(spans))[first + node]
            else:
                scale = present[first + node, block - 1].astype(F32)
                value = loads.get(where[first])[node, block - 1] * scale
            out[pl.ds(2 * at, 2)] = value


def pack(plan, spans, scalars, present, lower_panel, diag_inverse, limit):
    chunk, width = lower_panel.shape[-2:]
    outs = [((2 * len(blocks), chunk, width), F32, VMEM) for blocks in plan]
    scratch = [pltpu.VMEM((nodes, depth, 2, chunk, width), F32) for _, nodes, depth in spans]
    scratch += [pltpu.VMEM(diag_inverse.shape[1:], F32), pltpu.SemaphoreType.DMA((len(spans) + 1,))]
    kernel = functools.partial(pack_kernel, spans, plan, len(outs), chunk)
    ins = [(scalars, SMEM), (present, SMEM), (lower_panel, ANY), (diag_inverse, ANY)]
    return run_kernel(kernel, outs, ins, scratch, 0, limit=limit)


def pack_last_kernel(first, nodes, depth, steps, cols, *refs):
    scalars, present, panel_ref = refs[:3]
    outs = refs[3 : 3 + len(steps) * HALVES]
    buffer, sem = refs[-2:]
    copy = pltpu.make_async_copy(panel_ref.at[0, pl.ds(first, nodes), pl.ds(0, depth)], buffer, sem)
    copy.start()
    copy.wait()
    for at, (step, group) in enumerate(steps):
        node = (scalars[2] // group) ^ step
        for block in range(depth):
            value = buffer[node, block] * present[first + node, block].astype(F32)
            for half in range(HALVES):
                outs[half * len(steps) + at][pl.ds(2 * block, 2)] = value[
                    :, :, half * cols : (half + 1) * cols
                ]


def pack_last(first, nodes, depth, steps, cols, scalars, present, lower_panel):
    chunk, width = lower_panel.shape[-2:]
    outs = [((2 * depth, chunk, cols), F32, VMEM)] * (len(steps) * HALVES)
    scratch = [pltpu.VMEM((nodes, depth, 2, chunk, width), F32), pltpu.SemaphoreType.DMA]
    kernel = functools.partial(pack_last_kernel, first, nodes, depth, steps, cols)
    ins = [(scalars, SMEM), (present, SMEM), (lower_panel, ANY)]
    return run_kernel(kernel, outs, ins, scratch, 0)


def prep_kernel(levels, table, rows_count, chunk, width, n_arrays, *refs):
    scalars, present = refs[:2]
    arrays = refs[2 : 2 + n_arrays]
    outs = list(refs[2 + n_arrays :])
    odd = scalars[1] == 1
    for depth, swapped, first, slot in levels:
        if depth:
            whole, forward = outs.pop(0), outs.pop(0)
        else:
            whole = None
        backward = outs.pop(0)
        for block in range(depth + 1):
            for mask, part, position, base, stride in table:
                plane = base + stride * (first + block)
                start = rows_of(scalars, mask, chunk)
                if swapped is None:
                    value = arrays[position][plane]
                else:
                    half = n_arrays // 2
                    from_odd = arrays[position + (0 if swapped else half)]
                    from_even = arrays[position + (half if swapped else 0)]
                    value = jnp.where(odd, from_odd[plane], from_even[plane])
                    away = turned(mask, rows_count) if swapped else mask
                    start = pl.multiple_of((scalars[0] ^ away) * chunk, chunk)
                if block == 0:
                    rows = pl.ds(pl.multiple_of(part * width + start, chunk), chunk)
                    store_left(backward, rows, WIDE * depth * width, value)
                else:
                    if slot is not None:
                        at = slot[0] + scalars[2] // slot[1]
                        value = value * present[at, block - 1].astype(F32)
                    rows = pl.ds(pl.multiple_of((depth - block) * width + start, chunk), chunk)
                    whole[rows, pl.ds(part * width, width)] = value
        for level in range(depth):
            for part in range(2):
                value = whole[pl.ds(level * width, width), pl.ds(part * width, width)]
                store_left(forward, pl.ds((2 * level + part) * width, width), 0, value)
                rows = pl.ds(part * width, width)
                store_left(backward, rows, WIDE * level * width, -value.T)


def prep(levels, pieces, scalars, present, rows, chunk, width, others=()):
    arrays, table = [], []
    for mask, part, array, base, stride in pieces:
        position = next((at for at, value in enumerate(arrays) if value is array), None)
        if position is None:
            position = len(arrays)
            arrays.append(array)
        table.append((mask, part, position, base, stride))
    arrays = arrays + list(others)
    outs = []
    for depth, _, _, _ in levels:
        if depth:
            outs.append(((depth * width, 2 * width), F32, VMEM))
            outs.append(((2 * depth * width, WIDE * width), BF16, VMEM))
        outs.append(((2 * width, WIDE * (depth + 1) * width), BF16, VMEM))
    kernel = functools.partial(prep_kernel, levels, table, rows, chunk, width, len(arrays))
    ins = [(scalars, SMEM), (present, SMEM)] + [(value, VMEM) for value in arrays]
    made = list(run_kernel(kernel, outs, ins, [], 0))
    result = {}
    for depth, _, _, _ in levels:
        if depth:
            result[depth], made = tuple(made[:3]), made[3:]
        else:
            result[depth], made = (None, None, made[0]), made[1:]
    return result


def substitute(depth, width, cols, get, sums, right, emit):
    def rows(first, count=1):
        return pl.ds(first * width, count * width)

    for level in range(depth - 1, 0, -1):
        store_right(right, WIDE * level * width, sums[rows(level)])
        forward = get("forward", level)
        for block in range(level - 1, -1, -1):
            product = times(forward[rows(2 * block, 2)], right[rows(WIDE * level, WIDE)])
            sums[rows(block)] -= complex_sum(product, cols)
    store_right(right, 0, sums[rows(0)])
    for level in range(depth):
        product = times(get("backward", level)[...], right[rows(0, WIDE * (level + 1))])
        solved = complex_sum(product, cols)
        store_right(right, WIDE * level * width, solved)
        emit(level, solved)


def solve_kernel(depths, chunk, width, steps, order, masked, *refs):
    refs = list(refs)
    scalars = refs.pop(0)
    sources = [refs.pop(0) for _ in order]
    outs = {depth: [(refs.pop(0), refs.pop(0)) for _ in steps] for depth in depths}
    sums_ref, right_ref, solved_ref = refs

    def get(kind, level):
        return sources[order.index((kind, level))]

    for depth in depths:
        sums = sums_ref.at[pl.ds(0, depth * width)]
        right = right_ref.at[pl.ds(0, WIDE * depth * width)]
        sums[...] = get("whole", depth)[...]

        def send(block, value, sign):
            solved_ref[...] = value
            for (out, correction), step in zip(outs[depth], steps):
                start = rows_of(scalars, step, chunk)
                piece = solved_ref[pl.ds(start, chunk)] * sign
                if depth in masked:
                    piece = jnp.where(scalars[5 + depth] == 1, piece, 0.0)
                for part in range(2):
                    plane = piece[:, part * width : (part + 1) * width]
                    if block == 0:
                        correction[part] = plane
                    else:
                        out[block - 1, part] = plane

        substitute(
            depth, width, width, get, sums, right,
            lambda level, solved: send(depth - level, solved, -1.0),
        )
        product = times(get("backward", depth)[:, : WIDE * depth * width], right[...])
        send(0, complex_sum(product, width), 1.0)


def operands(made, names):
    index = {"whole": 0, "forward": 1, "backward": 2}
    return [made[level][index[kind]] for kind, level in names]


def solve(depths, made, scalars, steps, chunk, width, masked):
    top = depths[0]
    order = [("whole", top)]
    for level in range(top - 1, 0, -1):
        order.append(("forward", level))
    for level in range(top + 1):
        order.append(("backward", level))
    order += [("whole", depth) for depth in depths[1:]]
    sources = operands(made, order)
    outs = []
    for depth in depths:
        for _ in steps:
            outs.append(((depth, 2, chunk, width), F32, VMEM))
            outs.append(((2, chunk, width), F32, VMEM))
    scratch = [
        pltpu.VMEM((top * width, 2 * width), F32),
        pltpu.VMEM((WIDE * top * width, 2 * width), BF16),
        pltpu.VMEM((width, 2 * width), F32),
    ]
    kernel = functools.partial(solve_kernel, depths, chunk, width, steps, order, masked)
    flops = sum(24 * (depth * depth + depth) * width**3 for depth in depths)
    ins = [(scalars, SMEM)] + [(value, VMEM) for value in sources]
    got = list(run_kernel(kernel, outs, ins, scratch, flops))
    result = {}
    for depth in depths:
        result[depth] = [(got.pop(0), got.pop(0)) for _ in steps]
    return result


def last_kernel(depth, chunk, width, cols, steps, table, n_arrays, order, n_done, *refs):
    refs = list(refs)
    scalars = refs.pop(0)
    arrays = [refs.pop(0) for _ in range(n_arrays)]
    sources = [refs.pop(0) for _ in order]
    lefts = [(refs.pop(0), refs.pop(0)) for _ in range(n_done)]
    outs = [refs.pop(0) for _ in steps]
    left, right = refs.pop(0), refs.pop(0)
    sums, solved_ref, total = refs

    def get(kind, level):
        return sources[order.index((kind, level))]

    for mask, part, position, base, stride in table:
        start = rows_of(scalars, mask, chunk)
        for block in range(depth):
            row = pl.multiple_of((depth - 1 - block) * width + start, chunk)
            sums[pl.ds(row, chunk), pl.ds(part * cols, cols)] = arrays[position][base + stride * block]
    for level in range(depth):
        for part in range(2):
            value = sums[pl.ds(level * width, width), pl.ds(part * cols, cols)]
            store_left(left, pl.ds(part * cols, cols), WIDE * level * width, value.T)

    def emit(level, value):
        solved_ref[...] = value
        for out, step in zip(outs, steps):
            start = rows_of(scalars, step, chunk)
            piece = -solved_ref[pl.ds(start, chunk)]
            out[depth - 1 - level, 0] = piece[:, :cols]
            out[depth - 1 - level, 1] = piece[:, cols:]

    substitute(depth, width, cols, get, sums, right, emit)


    if n_done + 1 < HALVES:
        return
    lefts.append((left, right))
    for row in range(HALVES):
        for col in range(HALVES):
            block = -complex_sum(times(lefts[row][0][...], lefts[col][1][...]), cols)
            for part in range(2):
                total[col, part, pl.ds(row * cols, cols)] = block[:, part * cols : (part + 1) * cols]
    for out, step in zip(outs, steps):
        start = rows_of(scalars, step, chunk)
        for col in range(HALVES):
            for part in range(2):
                out[depth + col, part] = total[col, part, pl.ds(start, chunk)]


def solve_last(depth, made, pieces, scalars, steps, chunk, width, cols, lefts):
    arrays, table = [], []
    for mask, part, array, base, stride in pieces:
        position = next((at for at, value in enumerate(arrays) if value is array), None)
        if position is None:
            position = len(arrays)
            arrays.append(array)
        table.append((mask, part, position, base, stride))
    order = []
    for level in range(depth - 1, 0, -1):
        order.append(("forward", level))
    for level in range(depth):
        order.append(("backward", level))
    done = len(lefts) + 1 == HALVES
    sources = operands(made, order) + ([value for left in lefts for value in left] if done else [])
    blocks = depth + (HALVES if done else 0)
    outs = [((blocks, 2, chunk, cols), F32, VMEM)] * len(steps)
    outs.append(((2 * cols, WIDE * depth * width), BF16, VMEM))
    outs.append(((WIDE * depth * width, 2 * cols), BF16, VMEM))
    scratch = [
        pltpu.VMEM((depth * width, 2 * cols), F32),
        pltpu.VMEM((width, 2 * cols), F32),
        pltpu.VMEM((HALVES, 2, width, cols), F32),
    ]
    kernel = functools.partial(
        last_kernel, depth, chunk, width, cols, steps, table, len(arrays), order,
        len(lefts) if done else 0,
    )
    flops = 24 * depth * depth * width * width * cols
    ins = [(scalars, SMEM)] + [(value, VMEM) for value in arrays]
    ins += [(value, VMEM) for value in sources]
    got = run_kernel(kernel, outs, ins, scratch, flops)
    return got[: len(steps)], got[len(steps) :]


def begin_kernel(zeros, out, zero_ref, sem):
    zero_ref[...] = jnp.zeros_like(zero_ref)
    copies = []
    for slot, depth, count in zeros:
        copies.append((zero_ref.at[pl.ds(0, count)], out.at[0, slot, pl.ds(depth, count)]))
    copies = [
        pltpu.make_async_copy(source, target, sem.at[at])
        for at, (source, target) in enumerate(copies)
    ]
    for copy in copies:
        copy.start()
    for copy in copies:
        copy.wait()


def place_kernel(plan, depth, cols, half, late_plan, diag_plan, shared, *refs):
    refs = list(refs)
    scalars = refs.pop(0)
    pieces = [refs.pop(0) for _ in plan]
    refs.pop(0)
    last_half = half + 1 == HALVES
    own = refs.pop(0) if last_half else None
    late = [refs.pop(0) for _ in late_plan] if last_half else []
    corrections = [refs.pop(0) for _ in diag_plan] if last_half else []
    out = refs.pop(0)
    diag = refs.pop(0) if last_half else None
    (sem,) = refs
    copies = []
    slots = [first + ((scalars[2] // group) ^ step) for first, group, step in plan]
    for at, (piece, slot) in enumerate(zip(pieces, slots)):
        target = out.at[0, slot, :, :, :, pl.ds(half * cols, cols)]
        copies.append(pltpu.make_async_copy(piece.at[pl.ds(0, depth)], target, sem.at[at]))
    for piece, (first, group, step, level) in zip(late, late_plan):
        slot = first + ((scalars[2] // group) ^ step)
        target = out.at[0, slot, pl.ds(0, level)]
        copies.append(pltpu.make_async_copy(piece, target, sem.at[len(copies)]))
    for copy in copies:
        copy.start()
    if last_half:
        for slot in range(diag.shape[1]):
            value = own[0, slot]
            if slot in shared:
                value = jnp.where(scalars[5 + shared[slot]] == 1, value, 0.0)
            diag[0, slot] = value
        for correction, (first, group, step) in zip(corrections, diag_plan):
            slot = first + ((scalars[2] // group) ^ step)
            diag[0, slot] = diag[0, slot] - correction[...]
        for piece, slot in zip(pieces, slots):
            for col in range(HALVES):
                lanes = slice(col * cols, (col + 1) * cols)
                diag[0, slot, :, :, lanes] = diag[0, slot, :, :, lanes] - piece[depth + col]
    for copy in copies:
        copy.wait()


def body(lower_panel, diag_inverse, structure):
    columns = lax.axis_size("col")
    rows = lax.axis_size("row")
    position = lax.axis_index("col")
    place = lax.axis_index("row")
    slots, anc_count, _, chunk, width = lower_panel.shape[1:]
    per_col = [max(1, 2**depth // columns) for depth in range(LEVELS)]
    offsets = [sum(per_col[:depth]) for depth in range(LEVELS)]
    last = LEVELS - 1
    cols = width // HALVES
    groups = [rows // nodes for nodes in per_col]
    steps = [[step * groups[depth] for step in range(per_col[depth])] for depth in range(LEVELS)]
    shared = [depth for depth in range(LEVELS) if 2**depth < columns]
    middle = [depth for depth in range(LEVELS - 1) if 2**depth >= columns]
    active = [position % max(1, columns // 2**depth) == 0 for depth in range(LEVELS)]
    odd = position % 2 == 1
    scalars = [place, odd, jnp.where(odd, turned(place, rows), place)]
    scalars += [jnp.where(odd, turned(mask, rows), mask) for mask in (1, 2)]
    scalars = jnp.stack([jnp.asarray(value, jnp.int32) for value in scalars + active])
    present = structure[0]

    upper = shared[:-1]
    starts = [sum(1 + depth for depth in upper[:at]) for at in range(len(upper))]

    def level_blocks(depth, step=0):
        group = groups[depth]
        return [
            (offsets[depth], lambda at, group=group, step=step: (at // group) ^ step, block)
            for block in range(depth + 1)
        ]

    def packs(plan, depths, limit):
        spans = [(offsets[depth], per_col[depth], depth) for depth in depths if depth]
        return list(pack(plan, spans, scalars, present, lower_panel, diag_inverse, limit))

    plan = [sum([level_blocks(depth) for depth in upper], []), level_blocks(shared[-1])]
    near_rows, far_rows, bases = [], [], {}
    virtual = jnp.where(odd, turned(place, rows), place)
    for depth in middle:
        bases[depth] = sum(1 + held for held in bases)
        group, first = groups[depth], offsets[depth]
        for kept, step in ((near_rows, 0), (far_rows, 0 if group > 2 else 1)):
            slot = first + ((virtual // group) ^ step)
            diag = lax.dynamic_index_in_dim(diag_inverse[0], slot, 0, keepdims=False)
            panels = lax.dynamic_index_in_dim(lower_panel[0], slot, 0, keepdims=False)[:depth]
            kept += [diag, panels.reshape(2 * depth, chunk, width)]
    packed = packs(plan, shared, PACK_BYTES)
    upper_pack, own_pack = packed[:2]

    stride = columns // 2
    while stride >= 4:
        held = [at for at, depth in enumerate(upper) if columns // 2**depth >= 2 * stride]
        count = 2 * (starts[held[-1]] + 1 + upper[held[-1]])
        pairs = [(source, source + stride) for source in range(0, columns, 2 * stride)]
        if stride == columns // 2 and count == 2:
            travelling = diag_inverse[0, 0]
        else:
            travelling = upper_pack[:count]
        arrived = lax.ppermute(travelling, "col", pairs)
        fresh = position % (2 * stride) == stride
        upper_pack = jnp.concatenate(
            [jnp.where(fresh, arrived, upper_pack[:count]), upper_pack[count:]], axis=0
        )
        stride //= 2
    from_one = lax.ppermute(
        upper_pack, "col", [(source, source + 1) for source in range(0, columns, 4)]
    )
    from_three = lax.ppermute(
        upper_pack, "col", [(source, source + 3) for source in range(0, columns, 4)]
    )
    if middle:
        near_pack = jnp.concatenate(near_rows, axis=0)
        far_pack = jnp.concatenate(far_rows, axis=0)
        cut = 2 * sum(1 + depth for depth in middle if groups[depth] > 2)
        near_got = jnp.concatenate(
            [row_swap(part, 1) for part in (near_pack[:cut], near_pack[cut:]) if part.shape[0]], axis=0
        )
        far_got = row_swap(far_pack, 2)
        from_one, from_three, near_got, far_got = lax.optimization_barrier(
            (from_one, from_three, near_got, far_got)
        )
    upper_got = jnp.where(position % 4 == 1, from_one, from_three)
    planes = max(own_pack.shape[0], upper_got.shape[0])

    def fill(value):
        return jnp.pad(value, ((0, planes - value.shape[0]), (0, 0), (0, 0)))

    own = jnp.where(odd, fill(upper_got), fill(own_pack))

    near = row_swap(own, 1)
    far = row_swap(own, 2)

    def halves(value):
        return value.reshape(value.shape[0] // 2, 2, chunk, width)

    near_sends, far_sends, pair_sends = [halves(far)[:, 0]], [halves(near)[:, 1]], []
    homes = {}
    size, pair_size = planes // 2, 0
    for depth in middle:
        first, count = 2 * bases[depth], 2 * (depth + 1)
        if groups[depth] > 2:
            homes[depth] = size
            near_sends.append(halves(far_got[first : first + count])[:, 0])
            far_sends.append(halves(near_got[first : first + count])[:, 1])
            size += depth + 1
        else:
            homes[depth] = pair_size
            pair_sends.append(far_got[first : first + count])
            pair_size += count
    near_sends = jnp.concatenate(near_sends, axis=0)
    far_sends = jnp.concatenate(far_sends, axis=0)
    pair_sends = [jnp.concatenate(pair_sends, axis=0)] if pair_sends else []
    nodes, group = per_col[last], groups[last]
    last_packs = pack_last(
        offsets[last], nodes, last, [(step, group) for step in range(nodes)], cols,
        scalars, present, lower_panel,
    )
    zeros = [
        (offsets[depth] + node, depth, anc_count - depth)
        for depth in range(LEVELS)
        for node in range(per_col[depth])
        if depth < anc_count
    ]
    panel_shape = lower_panel.shape
    (sel_panel,) = run_kernel(
        functools.partial(begin_kernel, zeros),
        [(panel_shape, F32, ANY)],
        [],
        [
            pltpu.VMEM((anc_count, 2, chunk, width), F32),
            pltpu.SemaphoreType.DMA((len(zeros),)),
        ],
        0,
    )
    near_sends, far_sends, pair_sends, last_packs, sel_panel = lax.optimization_barrier(
        (near_sends, far_sends, pair_sends, last_packs, sel_panel)
    )
    near_more = row_swap(near_sends, 1)
    far_more = row_swap(far_sends, 2)
    pair_more = [row_swap(value, 1) for value in pair_sends]
    near_more, far_more, pair_more, last_packs = lax.optimization_barrier(
        (near_more, far_more, pair_more, last_packs)
    )

    blocks = planes // 2
    mine = jnp.concatenate([own, near, far, near_more[:blocks], far_more[:blocks]], axis=0)
    theirs = col_swap(mine)
    shared_pieces = (
        both_parts(0, mine)
        + both_parts(1, mine, blocks)
        + both_parts(2, mine, 2 * blocks)
        + [(3, 0, mine, 6 * blocks, 1), (3, 1, mine, 7 * blocks, 1)]
    )

    made = {}
    for depth in middle:
        base = bases[depth]
        home = homes[depth]
        pieces = both_parts(0, near_pack, base) + both_parts(1, near_got, base)
        pieces += both_parts(2, far_got, base)
        if groups[depth] > 2:
            pieces += [(3, 0, near_more, home, 1), (3, 1, far_more, home, 1)]
        else:
            pieces += [(3, 0, pair_more[0], home, 2), (3, 1, pair_more[0], home + 1, 2)]
        level = (depth, None, 0, (offsets[depth], groups[depth]))
        made.update(prep([level], pieces, scalars, present, rows, chunk, width))
    levels = [(depth, True, starts[at], None) for at, depth in enumerate(upper)]
    levels.append((shared[-1], False, 0, None))
    made.update(
        prep(levels, shared_pieces, scalars, present, rows, chunk, width, others=[theirs])
    )
    last_pieces = []
    for half in range(HALVES):
        sent = last_packs[half * nodes : (half + 1) * nodes]
        pieces = []
        for step, value in zip(steps[last], sent):
            arrived = row_swap(value, step) if step else value
            if group == 1:
                pieces.append((step, arrived))
                continue
            listed = [(step, arrived)]
            mask = 1
            while mask < group:
                listed += [(mask | at, row_swap(held, mask)) for at, held in listed]
                mask *= 2
            pieces += listed
        last_pieces.append(pieces)

    single = [depth for depth in range(last - 1, 0, -1) if per_col[depth] == 1]
    solved = {}
    for depth in range(1, last):
        if per_col[depth] > 1:
            solved.update(solve([depth], made, scalars, steps[depth], chunk, width, ()))
    second = [value for _, value in last_pieces[-1][:2]]
    solved, second, later = lax.optimization_barrier((solved, second, scalars))
    last_pieces[-1][:2] = [
        (at, value) for (at, _), value in zip(last_pieces[-1][:2], second)
    ]
    lefts, backs = [], []
    for half in range(HALVES):
        outward, left = solve_last(
            last, made, sum([both_parts(at, held) for at, held in last_pieces[half]], []),
            later, steps[last], chunk, width, cols, lefts
        )
        lefts.append(left)
        if half + 1 == HALVES:
            outward, later = lax.optimization_barrier((outward, scalars))
        backs.append(
            [row_swap(piece, step) if step else piece for piece, step in zip(outward, steps[last])]
        )
    last_plan = [(offsets[last], group, step) for step in range(nodes)]
    masked = {offsets[depth]: depth for depth in shared}
    for half, back in enumerate(backs):
        late_plan, late_pieces, diag_plan, diag_pieces = [], [], [], []
        if half + 1 == HALVES:
            sel_panel, later = lax.optimization_barrier((sel_panel, later))
            solved.update(solve(single, made, later, [0], chunk, width, tuple(shared)))
            for depth in range(1, last):
                for step, (piece, correction) in enumerate(solved[depth]):
                    if step:
                        both = jnp.concatenate([piece, correction[None]], axis=0)
                        both = row_swap(both, steps[depth][step])
                        piece, correction = both[:depth], both[depth]
                    late_plan.append((offsets[depth], groups[depth], step, depth))
                    late_pieces.append(piece)
                    diag_plan.append((offsets[depth], groups[depth], step))
                    diag_pieces.append(correction)
        ins = [(scalars, SMEM)] + [(piece, VMEM) for piece in back] + [(sel_panel, ANY)]
        outs = [(panel_shape, F32, ANY)]
        if half + 1 == HALVES:
            ins += [(diag_inverse, VMEM)]
            ins += [(piece, VMEM) for piece in late_pieces + diag_pieces]
            outs.append((diag_inverse.shape, F32, VMEM))
        made_now = run_kernel(
            functools.partial(
                place_kernel, last_plan, last, cols, half, late_plan, diag_plan, masked
            ),
            outs,
            ins,
            [pltpu.SemaphoreType.DMA((nodes + len(late_plan),))],
            0,
            aliases={1 + nodes: 0},
        )
        sel_panel = made_now[0]
    return (sel_panel, made_now[1])


def solution(mesh):
    in_specs = (
        P("col", None, None, None, "row", None),
        P("col", None, None, "row", None),
        P("col", None, None),
    )
    out_specs = (P("col", None, None, None, "row", None), P("col", None, None, "row", None))
    return jax.shard_map(body, mesh=mesh, in_specs=in_specs, out_specs=out_specs, check_vma=False)
```

```python
import functools

import jax
import jax.numpy as jnp
from jax import lax
from jax.experimental import pallas as pl
from jax.experimental.pallas import tpu as pltpu
from jax.sharding import PartitionSpec as P

LEVELS = 6
HALVES = 2
VMEM_BYTES = 18 * 2**20
PACK_BYTES = 58 * 2**20
F32 = jnp.float32
BF16 = jnp.bfloat16
ANY = pl.BlockSpec(memory_space=pl.ANY)
VMEM = pl.BlockSpec(memory_space=pltpu.VMEM)
SMEM = pl.BlockSpec(memory_space=pltpu.SMEM)


def turned(mask, rows):
    if rows < 4:
        return mask
    return (mask & ~3) | ((mask & 1) << 1) | ((mask >> 1) & 1)


def col_swap(value):
    count = lax.axis_size("col")
    return lax.ppermute(value, "col", [(source, source ^ 1) for source in range(count)])


def row_swap(value, mask):
    rows, columns = lax.axis_size("row"), lax.axis_size("col")
    pairs = []
    for row in range(rows):
        for col in range(columns):
            other = row ^ (turned(mask, rows) if col % 2 else mask)
            pairs.append((row * columns + col, other * columns + col))
    return lax.ppermute(value, ("row", "col"), pairs)


def rows_of(scalars, mask, chunk):
    away = mask & ~3
    if mask & 1:
        away = away | scalars[3]
    if mask & 2:
        away = away | scalars[4]
    return pl.multiple_of((scalars[0] ^ away) * chunk, chunk)


def split(value):
    high = value.astype(BF16)
    return high, (value - high.astype(F32)).astype(BF16)


WIDE = 3


def store_left(ref, rows, first, value):
    high, low = split(value)
    size = value.shape[1]
    for at, part in enumerate((high, high, low)):
        ref[rows, pl.ds(first + at * size, size)] = part


def store_right(ref, first, value):
    high, low = split(value)
    size = value.shape[0]
    for at, part in enumerate((high, low, high)):
        ref[pl.ds(first + at * size, size)] = part


def times(left, right):
    return jnp.dot(left, right, preferred_element_type=F32)


def complex_sum(product, half):
    count = product.shape[0] // 2
    by_real, by_imag = product[:count], product[count:]
    return jnp.concatenate(
        [by_real[:, :half] - by_imag[:, half:], by_real[:, half:] + by_imag[:, :half]], axis=1
    )


def run_kernel(kernel, outs, ins, scratch, flops, aliases=None, limit=VMEM_BYTES):
    moved = sum(value.size for value, _ in ins)
    return pl.pallas_call(
        kernel,
        out_shape=[jax.ShapeDtypeStruct(shape, dtype) for shape, dtype, _ in outs],
        in_specs=[spec for _, spec in ins],
        out_specs=[spec for _, _, spec in outs],
        scratch_shapes=scratch,
        input_output_aliases=aliases or {},
        compiler_params=pltpu.CompilerParams(vmem_limit_bytes=limit),
        cost_estimate=pl.CostEstimate(flops=flops // 64, bytes_accessed=moved // 64, transcendentals=0),
    )(*[value for value, _ in ins])


class Loads:
    def __init__(self, sources, buffers, sems):
        self.buffers = buffers
        self.copies = [
            pltpu.make_async_copy(source, buffer, sems.at[at])
            for at, (source, buffer) in enumerate(zip(sources, buffers))
        ]
        for copy in self.copies:
            copy.start()

    def get(self, at):
        if self.copies[at] is not None:
            self.copies[at].wait()
            self.copies[at] = None
        return self.buffers[at]


def both_parts(mask, array, base=0):
    return [(mask, 0, array, 2 * base, 2), (mask, 1, array, 2 * base + 1, 2)]


def pack_kernel(spans, plan, n_outs, chunk, *refs):
    scalars, present, panel_ref, diag_ref = refs[:4]
    outs = refs[4 : 4 + n_outs]
    panel_bufs = refs[4 + n_outs : -2]
    diag_buf, sems = refs[-2:]
    sources, buffers = [], []
    for (first, nodes, depth), buffer in zip(spans, panel_bufs):
        sources.append(panel_ref.at[0, pl.ds(first, nodes), pl.ds(0, depth)])
        buffers.append(buffer)
    if any(block == 0 for blocks in plan for _, _, block in blocks):
        sources.append(diag_ref.at[0])
        buffers.append(diag_buf)
    loads = Loads(sources, buffers, sems)
    where = {first: at for at, (first, _, _) in enumerate(spans)}
    for out, blocks in zip(outs, plan):
        for at, (first, node_of, block) in enumerate(blocks):
            node = node_of(scalars[2])
            if block == 0:
                value = loads.get(len(spans))[first + node]
            else:
                scale = present[first + node, block - 1].astype(F32)
                value = loads.get(where[first])[node, block - 1] * scale
            out[pl.ds(2 * at, 2)] = value


def pack(plan, spans, scalars, present, lower_panel, diag_inverse, limit):
    chunk, width = lower_panel.shape[-2:]
    outs = [((2 * len(blocks), chunk, width), F32, VMEM) for blocks in plan]
    scratch = [pltpu.VMEM((nodes, depth, 2, chunk, width), F32) for _, nodes, depth in spans]
    scratch += [pltpu.VMEM(diag_inverse.shape[1:], F32), pltpu.SemaphoreType.DMA((len(spans) + 1,))]
    kernel = functools.partial(pack_kernel, spans, plan, len(outs), chunk)
    ins = [(scalars, SMEM), (present, SMEM), (lower_panel, ANY), (diag_inverse, ANY)]
    return run_kernel(kernel, outs, ins, scratch, 0, limit=limit)


def pack_last_kernel(first, nodes, depth, steps, cols, *refs):
    scalars, present, panel_ref = refs[:3]
    outs = refs[3 : 3 + len(steps) * HALVES]
    buffer, sem = refs[-2:]
    copy = pltpu.make_async_copy(panel_ref.at[0, pl.ds(first, nodes), pl.ds(0, depth)], buffer, sem)
    copy.start()
    copy.wait()
    for at, (step, group) in enumerate(steps):
        node = (scalars[2] // group) ^ step
        for block in range(depth):
            value = buffer[node, block] * present[first + node, block].astype(F32)
            for half in range(HALVES):
                outs[half * len(steps) + at][pl.ds(2 * block, 2)] = value[
                    :, :, half * cols : (half + 1) * cols
                ]


def pack_last(first, nodes, depth, steps, cols, scalars, present, lower_panel):
    chunk, width = lower_panel.shape[-2:]
    outs = [((2 * depth, chunk, cols), F32, VMEM)] * (len(steps) * HALVES)
    scratch = [pltpu.VMEM((nodes, depth, 2, chunk, width), F32), pltpu.SemaphoreType.DMA]
    kernel = functools.partial(pack_last_kernel, first, nodes, depth, steps, cols)
    ins = [(scalars, SMEM), (present, SMEM), (lower_panel, ANY)]
    return run_kernel(kernel, outs, ins, scratch, 0)


def prep_kernel(levels, table, rows_count, chunk, width, n_arrays, *refs):
    scalars, present = refs[:2]
    arrays = refs[2 : 2 + n_arrays]
    outs = list(refs[2 + n_arrays :])
    odd = scalars[1] == 1
    for depth, swapped, first, slot in levels:
        if depth:
            whole, forward = outs.pop(0), outs.pop(0)
        else:
            whole = None
        backward = outs.pop(0)
        for block in range(depth + 1):
            for mask, part, position, base, stride in table:
                plane = base + stride * (first + block)
                start = rows_of(scalars, mask, chunk)
                if swapped is None:
                    value = arrays[position][plane]
                else:
                    half = n_arrays // 2
                    from_odd = arrays[position + (0 if swapped else half)]
                    from_even = arrays[position + (half if swapped else 0)]
                    value = jnp.where(odd, from_odd[plane], from_even[plane])
                    away = turned(mask, rows_count) if swapped else mask
                    start = pl.multiple_of((scalars[0] ^ away) * chunk, chunk)
                if block == 0:
                    rows = pl.ds(pl.multiple_of(part * width + start, chunk), chunk)
                    store_left(backward, rows, WIDE * depth * width, value)
                else:
                    if slot is not None:
                        at = slot[0] + scalars[2] // slot[1]
                        value = value * present[at, block - 1].astype(F32)
                    rows = pl.ds(pl.multiple_of((depth - block) * width + start, chunk), chunk)
                    whole[rows, pl.ds(part * width, width)] = value
        for level in range(depth):
            for part in range(2):
                value = whole[pl.ds(level * width, width), pl.ds(part * width, width)]
                store_left(forward, pl.ds((2 * level + part) * width, width), 0, value)
                rows = pl.ds(part * width, width)
                store_left(backward, rows, WIDE * level * width, -value.T)


def prep(levels, pieces, scalars, present, rows, chunk, width, others=()):
    arrays, table = [], []
    for mask, part, array, base, stride in pieces:
        position = next((at for at, value in enumerate(arrays) if value is array), None)
        if position is None:
            position = len(arrays)
            arrays.append(array)
        table.append((mask, part, position, base, stride))
    arrays = arrays + list(others)
    outs = []
    for depth, _, _, _ in levels:
        if depth:
            outs.append(((depth * width, 2 * width), F32, VMEM))
            outs.append(((2 * depth * width, WIDE * width), BF16, VMEM))
        outs.append(((2 * width, WIDE * (depth + 1) * width), BF16, VMEM))
    kernel = functools.partial(prep_kernel, levels, table, rows, chunk, width, len(arrays))
    ins = [(scalars, SMEM), (present, SMEM)] + [(value, VMEM) for value in arrays]
    made = list(run_kernel(kernel, outs, ins, [], 0))
    result = {}
    for depth, _, _, _ in levels:
        if depth:
            result[depth], made = tuple(made[:3]), made[3:]
        else:
            result[depth], made = (None, None, made[0]), made[1:]
    return result


def substitute(depth, width, cols, get, sums, right, emit):
    def rows(first, count=1):
        return pl.ds(first * width, count * width)

    for level in range(depth - 1, 0, -1):
        store_right(right, WIDE * level * width, sums[rows(level)])
        forward = get("forward", level)
        for block in range(level - 1, -1, -1):
            product = times(forward[rows(2 * block, 2)], right[rows(WIDE * level, WIDE)])
            sums[rows(block)] -= complex_sum(product, cols)
    store_right(right, 0, sums[rows(0)])
    for level in range(depth):
        product = times(get("backward", level)[...], right[rows(0, WIDE * (level + 1))])
        solved = complex_sum(product, cols)
        store_right(right, WIDE * level * width, solved)
        emit(level, solved)


def solve_kernel(depths, chunk, width, steps, order, masked, *refs):
    refs = list(refs)
    scalars = refs.pop(0)
    sources = [refs.pop(0) for _ in order]
    outs = {depth: [(refs.pop(0), refs.pop(0)) for _ in steps] for depth in depths}
    sums_ref, right_ref, solved_ref = refs

    def get(kind, level):
        return sources[order.index((kind, level))]

    for depth in depths:
        sums = sums_ref.at[pl.ds(0, depth * width)]
        right = right_ref.at[pl.ds(0, WIDE * depth * width)]
        sums[...] = get("whole", depth)[...]

        def send(block, value, sign):
            solved_ref[...] = value
            for (out, correction), step in zip(outs[depth], steps):
                start = rows_of(scalars, step, chunk)
                piece = solved_ref[pl.ds(start, chunk)] * sign
                if depth in masked:
                    piece = jnp.where(scalars[5 + depth] == 1, piece, 0.0)
                for part in range(2):
                    plane = piece[:, part * width : (part + 1) * width]
                    if block == 0:
                        correction[part] = plane
                    else:
                        out[block - 1, part] = plane

        substitute(
            depth, width, width, get, sums, right,
            lambda level, solved: send(depth - level, solved, -1.0),
        )
        product = times(get("backward", depth)[:, : WIDE * depth * width], right[...])
        send(0, complex_sum(product, width), 1.0)


def operands(made, names):
    index = {"whole": 0, "forward": 1, "backward": 2}
    return [made[level][index[kind]] for kind, level in names]


def solve(depths, made, scalars, steps, chunk, width, masked):
    top = depths[0]
    order = [("whole", top)]
    for level in range(top - 1, 0, -1):
        order.append(("forward", level))
    for level in range(top + 1):
        order.append(("backward", level))
    order += [("whole", depth) for depth in depths[1:]]
    sources = operands(made, order)
    outs = []
    for depth in depths:
        for _ in steps:
            outs.append(((depth, 2, chunk, width), F32, VMEM))
            outs.append(((2, chunk, width), F32, VMEM))
    scratch = [
        pltpu.VMEM((top * width, 2 * width), F32),
        pltpu.VMEM((WIDE * top * width, 2 * width), BF16),
        pltpu.VMEM((width, 2 * width), F32),
    ]
    kernel = functools.partial(solve_kernel, depths, chunk, width, steps, order, masked)
    flops = sum(24 * (depth * depth + depth) * width**3 for depth in depths)
    ins = [(scalars, SMEM)] + [(value, VMEM) for value in sources]
    got = list(run_kernel(kernel, outs, ins, scratch, flops))
    result = {}
    for depth in depths:
        result[depth] = [(got.pop(0), got.pop(0)) for _ in steps]
    return result


def last_kernel(depth, chunk, width, cols, steps, table, n_arrays, order, n_done, *refs):
    refs = list(refs)
    scalars = refs.pop(0)
    arrays = [refs.pop(0) for _ in range(n_arrays)]
    sources = [refs.pop(0) for _ in order]
    lefts = [(refs.pop(0), refs.pop(0)) for _ in range(n_done)]
    outs = [refs.pop(0) for _ in steps]
    left, right = refs.pop(0), refs.pop(0)
    sums, solved_ref, total = refs

    def get(kind, level):
        return sources[order.index((kind, level))]

    for mask, part, position, base, stride in table:
        start = rows_of(scalars, mask, chunk)
        for block in range(depth):
            row = pl.multiple_of((depth - 1 - block) * width + start, chunk)
            sums[pl.ds(row, chunk), pl.ds(part * cols, cols)] = arrays[position][base + stride * block]
    for level in range(depth):
        for part in range(2):
            value = sums[pl.ds(level * width, width), pl.ds(part * cols, cols)]
            store_left(left, pl.ds(part * cols, cols), WIDE * level * width, value.T)

    def emit(level, value):
        solved_ref[...] = value
        for out, step in zip(outs, steps):
            start = rows_of(scalars, step, chunk)
            piece = -solved_ref[pl.ds(start, chunk)]
            out[depth - 1 - level, 0] = piece[:, :cols]
            out[depth - 1 - level, 1] = piece[:, cols:]

    substitute(depth, width, cols, get, sums, right, emit)


    if n_done + 1 < HALVES:
        return
    lefts.append((left, right))
    for row in range(HALVES):
        for col in range(HALVES):
            block = -complex_sum(times(lefts[row][0][...], lefts[col][1][...]), cols)
            for part in range(2):
                total[col, part, pl.ds(row * cols, cols)] = block[:, part * cols : (part + 1) * cols]
    for out, step in zip(outs, steps):
        start = rows_of(scalars, step, chunk)
        for col in range(HALVES):
            for part in range(2):
                out[depth + col, part] = total[col, part, pl.ds(start, chunk)]


def solve_last(depth, made, pieces, scalars, steps, chunk, width, cols, lefts):
    arrays, table = [], []
    for mask, part, array, base, stride in pieces:
        position = next((at for at, value in enumerate(arrays) if value is array), None)
        if position is None:
            position = len(arrays)
            arrays.append(array)
        table.append((mask, part, position, base, stride))
    order = []
    for level in range(depth - 1, 0, -1):
        order.append(("forward", level))
    for level in range(depth):
        order.append(("backward", level))
    done = len(lefts) + 1 == HALVES
    sources = operands(made, order) + ([value for left in lefts for value in left] if done else [])
    blocks = depth + (HALVES if done else 0)
    outs = [((blocks, 2, chunk, cols), F32, VMEM)] * len(steps)
    outs.append(((2 * cols, WIDE * depth * width), BF16, VMEM))
    outs.append(((WIDE * depth * width, 2 * cols), BF16, VMEM))
    scratch = [
        pltpu.VMEM((depth * width, 2 * cols), F32),
        pltpu.VMEM((width, 2 * cols), F32),
        pltpu.VMEM((HALVES, 2, width, cols), F32),
    ]
    kernel = functools.partial(
        last_kernel, depth, chunk, width, cols, steps, table, len(arrays), order,
        len(lefts) if done else 0,
    )
    flops = 24 * depth * depth * width * width * cols
    ins = [(scalars, SMEM)] + [(value, VMEM) for value in arrays]
    ins += [(value, VMEM) for value in sources]
    got = run_kernel(kernel, outs, ins, scratch, flops)
    return got[: len(steps)], got[len(steps) :]


def begin_kernel(zeros, out, zero_ref, sem):
    zero_ref[...] = jnp.zeros_like(zero_ref)
    copies = []
    for slot, depth, count in zeros:
        copies.append((zero_ref.at[pl.ds(0, count)], out.at[0, slot, pl.ds(depth, count)]))
    copies = [
        pltpu.make_async_copy(source, target, sem.at[at])
        for at, (source, target) in enumerate(copies)
    ]
    for copy in copies:
        copy.start()
    for copy in copies:
        copy.wait()


def place_kernel(plan, depth, cols, half, late_plan, diag_plan, shared, *refs):
    refs = list(refs)
    scalars = refs.pop(0)
    pieces = [refs.pop(0) for _ in plan]
    refs.pop(0)
    last_half = half + 1 == HALVES
    own = refs.pop(0) if last_half else None
    late = [refs.pop(0) for _ in late_plan] if last_half else []
    corrections = [refs.pop(0) for _ in diag_plan] if last_half else []
    out = refs.pop(0)
    diag = refs.pop(0) if last_half else None
    (sem,) = refs
    copies = []
    slots = [first + ((scalars[2] // group) ^ step) for first, group, step in plan]
    for at, (piece, slot) in enumerate(zip(pieces, slots)):
        target = out.at[0, slot, :, :, :, pl.ds(half * cols, cols)]
        copies.append(pltpu.make_async_copy(piece.at[pl.ds(0, depth)], target, sem.at[at]))
    for piece, (first, group, step, level) in zip(late, late_plan):
        slot = first + ((scalars[2] // group) ^ step)
        target = out.at[0, slot, pl.ds(0, level)]
        copies.append(pltpu.make_async_copy(piece, target, sem.at[len(copies)]))
    for copy in copies:
        copy.start()
    if last_half:
        for slot in range(diag.shape[1]):
            value = own[0, slot]
            if slot in shared:
                value = jnp.where(scalars[5 + shared[slot]] == 1, value, 0.0)
            diag[0, slot] = value
        for correction, (first, group, step) in zip(corrections, diag_plan):
            slot = first + ((scalars[2] // group) ^ step)
            diag[0, slot] = diag[0, slot] - correction[...]
        for piece, slot in zip(pieces, slots):
            for col in range(HALVES):
                lanes = slice(col * cols, (col + 1) * cols)
                diag[0, slot, :, :, lanes] = diag[0, slot, :, :, lanes] - piece[depth + col]
    for copy in copies:
        copy.wait()


def body(lower_panel, diag_inverse, structure):
    columns = lax.axis_size("col")
    rows = lax.axis_size("row")
    position = lax.axis_index("col")
    place = lax.axis_index("row")
    slots, anc_count, _, chunk, width = lower_panel.shape[1:]
    per_col = [max(1, 2**depth // columns) for depth in range(LEVELS)]
    offsets = [sum(per_col[:depth]) for depth in range(LEVELS)]
    last = LEVELS - 1
    cols = width // HALVES
    groups = [rows // nodes for nodes in per_col]
    steps = [[step * groups[depth] for step in range(per_col[depth])] for depth in range(LEVELS)]
    shared = [depth for depth in range(LEVELS) if 2**depth < columns]
    middle = [depth for depth in range(LEVELS - 1) if 2**depth >= columns]
    active = [position % max(1, columns // 2**depth) == 0 for depth in range(LEVELS)]
    odd = position % 2 == 1
    scalars = [place, odd, jnp.where(odd, turned(place, rows), place)]
    scalars += [jnp.where(odd, turned(mask, rows), mask) for mask in (1, 2)]
    scalars = jnp.stack([jnp.asarray(value, jnp.int32) for value in scalars + active])
    present = structure[0]

    upper = shared[:-1]
    starts = [sum(1 + depth for depth in upper[:at]) for at in range(len(upper))]

    def level_blocks(depth, step=0):
        group = groups[depth]
        return [
            (offsets[depth], lambda at, group=group, step=step: (at // group) ^ step, block)
            for block in range(depth + 1)
        ]

    def packs(plan, depths, limit):
        spans = [(offsets[depth], per_col[depth], depth) for depth in depths if depth]
        return list(pack(plan, spans, scalars, present, lower_panel, diag_inverse, limit))

    plan = [sum([level_blocks(depth) for depth in upper], []), level_blocks(shared[-1])]
    whole_rows, near_rows, far_rows, bases = [], [], [], {}
    virtual = jnp.where(odd, turned(place, rows), place)
    for depth in middle:
        group, first = groups[depth], offsets[depth]
        kept_rows = [(whole_rows, 0)] if group > 2 else [(near_rows, 0), (far_rows, 1)]
        bases[depth] = sum(value.shape[0] for value in kept_rows[0][0]) // 2
        for kept, step in kept_rows:
            slot = first if group == rows else first + ((virtual // group) ^ step)
            diag = lax.dynamic_index_in_dim(diag_inverse[0], slot, 0, keepdims=False)
            panels = lax.dynamic_index_in_dim(lower_panel[0], slot, 0, keepdims=False)[:depth]
            kept += [diag, panels.reshape(2 * depth, chunk, width)]
    packed = packs(plan, shared, PACK_BYTES)
    upper_pack, own_pack = packed[:2]

    stride = columns // 2
    while stride >= 4:
        held = [at for at, depth in enumerate(upper) if columns // 2**depth >= 2 * stride]
        count = 2 * (starts[held[-1]] + 1 + upper[held[-1]])
        pairs = [(source, source + stride) for source in range(0, columns, 2 * stride)]
        if stride == columns // 2 and count == 2:
            travelling = diag_inverse[0, 0]
        else:
            travelling = upper_pack[:count]
        arrived = lax.ppermute(travelling, "col", pairs)
        fresh = position % (2 * stride) == stride
        upper_pack = jnp.concatenate(
            [jnp.where(fresh, arrived, upper_pack[:count]), upper_pack[count:]], axis=0
        )
        stride //= 2
    if whole_rows:
        whole_pack = jnp.concatenate(whole_rows, axis=0)
        near_got = row_swap(whole_pack, 1)
        far_got = row_swap(whole_pack, 2)
        upper_pack, near_got, far_got = lax.optimization_barrier((upper_pack, near_got, far_got))
    if near_rows:
        near_pack = jnp.concatenate(near_rows, axis=0)
        far_pack = jnp.concatenate(far_rows, axis=0)
        pair_got = row_swap(near_pack, 1), row_swap(far_pack, 2)
    from_one = lax.ppermute(
        upper_pack, "col", [(source, source + 1) for source in range(0, columns, 4)]
    )
    from_three = lax.ppermute(
        upper_pack, "col", [(source, source + 3) for source in range(0, columns, 4)]
    )
    upper_got = jnp.where(position % 4 == 1, from_one, from_three)
    planes = max(own_pack.shape[0], upper_got.shape[0])

    def fill(value):
        return jnp.pad(value, ((0, planes - value.shape[0]), (0, 0), (0, 0)))

    own = jnp.where(odd, fill(upper_got), fill(own_pack))

    near = row_swap(own, 1)
    far = row_swap(own, 2)

    def halves(value):
        return value.reshape(value.shape[0] // 2, 2, chunk, width)

    near_sends, far_sends, pair_sends = [halves(far)[:, 0]], [halves(near)[:, 1]], []
    homes = {}
    size, pair_size = planes // 2, 0
    for depth in middle:
        first, count = 2 * bases[depth], 2 * (depth + 1)
        if groups[depth] > 2:
            homes[depth] = size
            near_sends.append(halves(far_got[first : first + count])[:, 0])
            far_sends.append(halves(near_got[first : first + count])[:, 1])
            size += depth + 1
        else:
            homes[depth] = pair_size
            pair_sends.append(pair_got[1][first : first + count])
            pair_size += count
    near_sends = jnp.concatenate(near_sends, axis=0)
    far_sends = jnp.concatenate(far_sends, axis=0)
    pair_sends = [jnp.concatenate(pair_sends, axis=0)] if pair_sends else []
    nodes, group = per_col[last], groups[last]
    after = scalars
    if near_rows:
        after, pair_got = lax.optimization_barrier((scalars, pair_got))
    last_packs = pack_last(
        offsets[last], nodes, last, [(step, group) for step in range(nodes)], cols,
        after, present, lower_panel,
    )
    zeros = [
        (offsets[depth] + node, depth, anc_count - depth)
        for depth in range(LEVELS)
        for node in range(per_col[depth])
        if depth < anc_count
    ]
    panel_shape = lower_panel.shape
    (sel_panel,) = run_kernel(
        functools.partial(begin_kernel, zeros),
        [(panel_shape, F32, ANY)],
        [],
        [
            pltpu.VMEM((anc_count, 2, chunk, width), F32),
            pltpu.SemaphoreType.DMA((len(zeros),)),
        ],
        0,
    )
    near_sends, far_sends, pair_sends, last_packs, sel_panel = lax.optimization_barrier(
        (near_sends, far_sends, pair_sends, last_packs, sel_panel)
    )
    near_more = row_swap(near_sends, 1)
    far_more = row_swap(far_sends, 2)
    pair_more = [row_swap(value, 1) for value in pair_sends]
    near_more, far_more, pair_more, last_packs = lax.optimization_barrier(
        (near_more, far_more, pair_more, last_packs)
    )

    blocks = planes // 2
    mine = jnp.concatenate([own, near, far, near_more[:blocks], far_more[:blocks]], axis=0)
    theirs = col_swap(mine)
    shared_pieces = (
        both_parts(0, mine)
        + both_parts(1, mine, blocks)
        + both_parts(2, mine, 2 * blocks)
        + [(3, 0, mine, 6 * blocks, 1), (3, 1, mine, 7 * blocks, 1)]
    )

    made = {}
    for depth in middle:
        base = bases[depth]
        home = homes[depth]
        if groups[depth] > 2:
            pieces = both_parts(0, whole_pack, base) + both_parts(1, near_got, base)
            pieces += both_parts(2, far_got, base)
            pieces += [(3, 0, near_more, home, 1), (3, 1, far_more, home, 1)]
        else:
            pieces = both_parts(0, near_pack, base) + both_parts(1, pair_got[0], base)
            pieces += both_parts(2, pair_got[1], base)
            pieces += [(3, 0, pair_more[0], home, 2), (3, 1, pair_more[0], home + 1, 2)]
        level = (depth, None, 0, (offsets[depth], groups[depth]))
        made.update(prep([level], pieces, scalars, present, rows, chunk, width))
    levels = [(depth, True, starts[at], None) for at, depth in enumerate(upper)]
    levels.append((shared[-1], False, 0, None))
    made.update(
        prep(levels, shared_pieces, scalars, present, rows, chunk, width, others=[theirs])
    )
    last_pieces = []
    for half in range(HALVES):
        sent = last_packs[half * nodes : (half + 1) * nodes]
        pieces = []
        for step, value in zip(steps[last], sent):
            arrived = row_swap(value, step) if step else value
            if group == 1:
                pieces.append((step, arrived))
                continue
            listed = [(step, arrived)]
            mask = 1
            while mask < group:
                listed += [(mask | at, row_swap(held, mask)) for at, held in listed]
                mask *= 2
            pieces += listed
        last_pieces.append(pieces)

    single = [depth for depth in range(last - 1, 0, -1) if per_col[depth] == 1]
    solved = {}
    for depth in range(1, last):
        if per_col[depth] > 1:
            solved.update(solve([depth], made, scalars, steps[depth], chunk, width, ()))
    second = [value for _, value in last_pieces[-1][:2]]
    solved, second, later = lax.optimization_barrier((solved, second, scalars))
    last_pieces[-1][:2] = [
        (at, value) for (at, _), value in zip(last_pieces[-1][:2], second)
    ]
    lefts, backs = [], []
    for half in range(HALVES):
        outward, left = solve_last(
            last, made, sum([both_parts(at, held) for at, held in last_pieces[half]], []),
            later, steps[last], chunk, width, cols, lefts
        )
        lefts.append(left)
        if half + 1 == HALVES:
            outward, later = lax.optimization_barrier((outward, scalars))
        backs.append(
            [row_swap(piece, step) if step else piece for piece, step in zip(outward, steps[last])]
        )
    last_plan = [(offsets[last], group, step) for step in range(nodes)]
    masked = {offsets[depth]: depth for depth in shared}
    for half, back in enumerate(backs):
        late_plan, late_pieces, diag_plan, diag_pieces = [], [], [], []
        if half + 1 == HALVES:
            sel_panel, later = lax.optimization_barrier((sel_panel, later))
            solved.update(solve(single, made, later, [0], chunk, width, tuple(shared)))
            for depth in range(1, last):
                for step, (piece, correction) in enumerate(solved[depth]):
                    if step:
                        both = jnp.concatenate([piece, correction[None]], axis=0)
                        both = row_swap(both, steps[depth][step])
                        piece, correction = both[:depth], both[depth]
                    late_plan.append((offsets[depth], groups[depth], step, depth))
                    late_pieces.append(piece)
                    diag_plan.append((offsets[depth], groups[depth], step))
                    diag_pieces.append(correction)
        ins = [(scalars, SMEM)] + [(piece, VMEM) for piece in back] + [(sel_panel, ANY)]
        outs = [(panel_shape, F32, ANY)]
        if half + 1 == HALVES:
            ins += [(diag_inverse, VMEM)]
            ins += [(piece, VMEM) for piece in late_pieces + diag_pieces]
            outs.append((diag_inverse.shape, F32, VMEM))
        made_now = run_kernel(
            functools.partial(
                place_kernel, last_plan, last, cols, half, late_plan, diag_plan, masked
            ),
            outs,
            ins,
            [pltpu.SemaphoreType.DMA((nodes + len(late_plan),))],
            0,
            aliases={1 + nodes: 0},
        )
        sel_panel = made_now[0]
    return (sel_panel, made_now[1])


def solution(mesh):
    in_specs = (
        P("col", None, None, None, "row", None),
        P("col", None, None, "row", None),
        P("col", None, None),
    )
    out_specs = (P("col", None, None, None, "row", None), P("col", None, None, "row", None))
    return jax.shard_map(body, mesh=mesh, in_specs=in_specs, out_specs=out_specs, check_vma=False)
```

```python
import functools

import jax
import jax.numpy as jnp
from jax import lax
from jax.experimental import pallas as pl
from jax.experimental.pallas import tpu as pltpu
from jax.sharding import PartitionSpec as P

LEVELS = 6
HALVES = 2
VMEM_BYTES = 18 * 2**20
PACK_BYTES = 58 * 2**20
F32 = jnp.float32
BF16 = jnp.bfloat16
ANY = pl.BlockSpec(memory_space=pl.ANY)
VMEM = pl.BlockSpec(memory_space=pltpu.VMEM)
SMEM = pl.BlockSpec(memory_space=pltpu.SMEM)


def turned(mask, rows):
    if rows < 4:
        return mask
    return (mask & ~3) | ((mask & 1) << 1) | ((mask >> 1) & 1)


def col_swap(value):
    count = lax.axis_size("col")
    return lax.ppermute(value, "col", [(source, source ^ 1) for source in range(count)])


def row_swap(value, mask):
    rows, columns = lax.axis_size("row"), lax.axis_size("col")
    pairs = []
    for row in range(rows):
        for col in range(columns):
            other = row ^ (turned(mask, rows) if col % 2 else mask)
            pairs.append((row * columns + col, other * columns + col))
    return lax.ppermute(value, ("row", "col"), pairs)


def rows_of(scalars, mask, chunk):
    away = mask & ~3
    if mask & 1:
        away = away | scalars[3]
    if mask & 2:
        away = away | scalars[4]
    return pl.multiple_of((scalars[0] ^ away) * chunk, chunk)


def split(value):
    high = value.astype(BF16)
    return high, (value - high.astype(F32)).astype(BF16)


WIDE = 3


def store_left(ref, rows, first, value):
    high, low = split(value)
    size = value.shape[1]
    for at, part in enumerate((high, high, low)):
        ref[rows, pl.ds(first + at * size, size)] = part


def store_right(ref, first, value):
    high, low = split(value)
    size = value.shape[0]
    for at, part in enumerate((high, low, high)):
        ref[pl.ds(first + at * size, size)] = part


def times(left, right):
    return jnp.dot(left, right, preferred_element_type=F32)


def complex_sum(product, half):
    count = product.shape[0] // 2
    by_real, by_imag = product[:count], product[count:]
    return jnp.concatenate(
        [by_real[:, :half] - by_imag[:, half:], by_real[:, half:] + by_imag[:, :half]], axis=1
    )


def run_kernel(kernel, outs, ins, scratch, flops, aliases=None, limit=VMEM_BYTES):
    moved = sum(value.size for value, _ in ins)
    return pl.pallas_call(
        kernel,
        out_shape=[jax.ShapeDtypeStruct(shape, dtype) for shape, dtype, _ in outs],
        in_specs=[spec for _, spec in ins],
        out_specs=[spec for _, _, spec in outs],
        scratch_shapes=scratch,
        input_output_aliases=aliases or {},
        compiler_params=pltpu.CompilerParams(vmem_limit_bytes=limit),
        cost_estimate=pl.CostEstimate(flops=flops // 64, bytes_accessed=moved // 64, transcendentals=0),
    )(*[value for value, _ in ins])


class Loads:
    def __init__(self, sources, buffers, sems):
        self.buffers = buffers
        self.copies = [
            pltpu.make_async_copy(source, buffer, sems.at[at])
            for at, (source, buffer) in enumerate(zip(sources, buffers))
        ]
        for copy in self.copies:
            copy.start()

    def get(self, at):
        if self.copies[at] is not None:
            self.copies[at].wait()
            self.copies[at] = None
        return self.buffers[at]


def both_parts(mask, array, base=0):
    return [(mask, 0, array, 2 * base, 2), (mask, 1, array, 2 * base + 1, 2)]


def pack_kernel(spans, plan, n_outs, chunk, *refs):
    scalars, present, panel_ref, diag_ref = refs[:4]
    outs = refs[4 : 4 + n_outs]
    panel_bufs = refs[4 + n_outs : -2]
    diag_buf, sems = refs[-2:]
    sources, buffers = [], []
    for (first, nodes, depth), buffer in zip(spans, panel_bufs):
        sources.append(panel_ref.at[0, pl.ds(first, nodes), pl.ds(0, depth)])
        buffers.append(buffer)
    if any(block == 0 for blocks in plan for _, _, block in blocks):
        sources.append(diag_ref.at[0])
        buffers.append(diag_buf)
    loads = Loads(sources, buffers, sems)
    where = {first: at for at, (first, _, _) in enumerate(spans)}
    for out, blocks in zip(outs, plan):
        for at, (first, node_of, block) in enumerate(blocks):
            node = node_of(scalars[2])
            if block == 0:
                value = loads.get(len(spans))[first + node]
            else:
                scale = present[first + node, block - 1].astype(F32)
                value = loads.get(where[first])[node, block - 1] * scale
            out[pl.ds(2 * at, 2)] = value


def pack(plan, spans, scalars, present, lower_panel, diag_inverse, limit):
    chunk, width = lower_panel.shape[-2:]
    outs = [((2 * len(blocks), chunk, width), F32, VMEM) for blocks in plan]
    scratch = [pltpu.VMEM((nodes, depth, 2, chunk, width), F32) for _, nodes, depth in spans]
    scratch += [pltpu.VMEM(diag_inverse.shape[1:], F32), pltpu.SemaphoreType.DMA((len(spans) + 1,))]
    kernel = functools.partial(pack_kernel, spans, plan, len(outs), chunk)
    ins = [(scalars, SMEM), (present, SMEM), (lower_panel, ANY), (diag_inverse, ANY)]
    return run_kernel(kernel, outs, ins, scratch, 0, limit=limit)


def pack_last_kernel(first, nodes, depth, steps, cols, *refs):
    scalars, present, panel_ref = refs[:3]
    outs = refs[3 : 3 + len(steps) * HALVES]
    buffer, sem = refs[-2:]
    copy = pltpu.make_async_copy(panel_ref.at[0, pl.ds(first, nodes), pl.ds(0, depth)], buffer, sem)
    copy.start()
    copy.wait()
    for at, (step, group) in enumerate(steps):
        node = (scalars[2] // group) ^ step
        for block in range(depth):
            value = buffer[node, block] * present[first + node, block].astype(F32)
            for half in range(HALVES):
                outs[half * len(steps) + at][pl.ds(2 * block, 2)] = value[
                    :, :, half * cols : (half + 1) * cols
                ]


def pack_last(first, nodes, depth, steps, cols, scalars, present, lower_panel):
    chunk, width = lower_panel.shape[-2:]
    outs = [((2 * depth, chunk, cols), F32, VMEM)] * (len(steps) * HALVES)
    scratch = [pltpu.VMEM((nodes, depth, 2, chunk, width), F32), pltpu.SemaphoreType.DMA]
    kernel = functools.partial(pack_last_kernel, first, nodes, depth, steps, cols)
    ins = [(scalars, SMEM), (present, SMEM), (lower_panel, ANY)]
    return run_kernel(kernel, outs, ins, scratch, 0)


def prep_kernel(levels, table, rows_count, chunk, width, n_arrays, *refs):
    scalars, present = refs[:2]
    arrays = refs[2 : 2 + n_arrays]
    outs = list(refs[2 + n_arrays :])
    odd = scalars[1] == 1
    for depth, swapped, first, slot in levels:
        if depth:
            whole, forward = outs.pop(0), outs.pop(0)
        else:
            whole = None
        backward = outs.pop(0)
        for block in range(depth + 1):
            for mask, part, position, base, stride in table:
                plane = base + stride * (first + block)
                start = rows_of(scalars, mask, chunk)
                if swapped is None:
                    value = arrays[position][plane]
                else:
                    half = n_arrays // 2
                    from_odd = arrays[position + (0 if swapped else half)]
                    from_even = arrays[position + (half if swapped else 0)]
                    value = jnp.where(odd, from_odd[plane], from_even[plane])
                    away = turned(mask, rows_count) if swapped else mask
                    start = pl.multiple_of((scalars[0] ^ away) * chunk, chunk)
                if block == 0:
                    rows = pl.ds(pl.multiple_of(part * width + start, chunk), chunk)
                    store_left(backward, rows, WIDE * depth * width, value)
                else:
                    if slot is not None:
                        at = slot[0] + scalars[2] // slot[1]
                        value = value * present[at, block - 1].astype(F32)
                    rows = pl.ds(pl.multiple_of((depth - block) * width + start, chunk), chunk)
                    whole[rows, pl.ds(part * width, width)] = value
        for level in range(depth):
            for part in range(2):
                value = whole[pl.ds(level * width, width), pl.ds(part * width, width)]
                store_left(forward, pl.ds((2 * level + part) * width, width), 0, value)
                rows = pl.ds(part * width, width)
                store_left(backward, rows, WIDE * level * width, -value.T)


def prep(levels, pieces, scalars, present, rows, chunk, width, others=()):
    arrays, table = [], []
    for mask, part, array, base, stride in pieces:
        position = next((at for at, value in enumerate(arrays) if value is array), None)
        if position is None:
            position = len(arrays)
            arrays.append(array)
        table.append((mask, part, position, base, stride))
    arrays = arrays + list(others)
    outs = []
    for depth, _, _, _ in levels:
        if depth:
            outs.append(((depth * width, 2 * width), F32, VMEM))
            outs.append(((2 * depth * width, WIDE * width), BF16, VMEM))
        outs.append(((2 * width, WIDE * (depth + 1) * width), BF16, VMEM))
    kernel = functools.partial(prep_kernel, levels, table, rows, chunk, width, len(arrays))
    ins = [(scalars, SMEM), (present, SMEM)] + [(value, VMEM) for value in arrays]
    made = list(run_kernel(kernel, outs, ins, [], 0))
    result = {}
    for depth, _, _, _ in levels:
        if depth:
            result[depth], made = tuple(made[:3]), made[3:]
        else:
            result[depth], made = (None, None, made[0]), made[1:]
    return result


def substitute(depth, width, cols, get, sums, right, emit):
    def rows(first, count=1):
        return pl.ds(first * width, count * width)

    for level in range(depth - 1, 0, -1):
        store_right(right, WIDE * level * width, sums[rows(level)])
        forward = get("forward", level)
        for block in range(level - 1, -1, -1):
            product = times(forward[rows(2 * block, 2)], right[rows(WIDE * level, WIDE)])
            sums[rows(block)] -= complex_sum(product, cols)
    store_right(right, 0, sums[rows(0)])
    for level in range(depth):
        product = times(get("backward", level)[...], right[rows(0, WIDE * (level + 1))])
        solved = complex_sum(product, cols)
        store_right(right, WIDE * level * width, solved)
        emit(level, solved)


def solve_kernel(depths, chunk, width, steps, order, masked, *refs):
    refs = list(refs)
    scalars = refs.pop(0)
    sources = [refs.pop(0) for _ in order]
    outs = {depth: [(refs.pop(0), refs.pop(0)) for _ in steps] for depth in depths}
    sums_ref, right_ref, solved_ref = refs

    def get(kind, level):
        return sources[order.index((kind, level))]

    for depth in depths:
        sums = sums_ref.at[pl.ds(0, depth * width)]
        right = right_ref.at[pl.ds(0, WIDE * depth * width)]
        sums[...] = get("whole", depth)[...]

        def send(block, value, sign):
            solved_ref[...] = value
            for (out, correction), step in zip(outs[depth], steps):
                start = rows_of(scalars, step, chunk)
                piece = solved_ref[pl.ds(start, chunk)] * sign
                if depth in masked:
                    piece = jnp.where(scalars[5 + depth] == 1, piece, 0.0)
                for part in range(2):
                    plane = piece[:, part * width : (part + 1) * width]
                    if block == 0:
                        correction[part] = plane
                    else:
                        out[block - 1, part] = plane

        substitute(
            depth, width, width, get, sums, right,
            lambda level, solved: send(depth - level, solved, -1.0),
        )
        product = times(get("backward", depth)[:, : WIDE * depth * width], right[...])
        send(0, complex_sum(product, width), 1.0)


def operands(made, names):
    index = {"whole": 0, "forward": 1, "backward": 2}
    return [made[level][index[kind]] for kind, level in names]


def solve(depths, made, scalars, steps, chunk, width, masked):
    top = depths[0]
    order = [("whole", top)]
    for level in range(top - 1, 0, -1):
        order.append(("forward", level))
    for level in range(top + 1):
        order.append(("backward", level))
    order += [("whole", depth) for depth in depths[1:]]
    sources = operands(made, order)
    outs = []
    for depth in depths:
        for _ in steps:
            outs.append(((depth, 2, chunk, width), F32, VMEM))
            outs.append(((2, chunk, width), F32, VMEM))
    scratch = [
        pltpu.VMEM((top * width, 2 * width), F32),
        pltpu.VMEM((WIDE * top * width, 2 * width), BF16),
        pltpu.VMEM((width, 2 * width), F32),
    ]
    kernel = functools.partial(solve_kernel, depths, chunk, width, steps, order, masked)
    flops = sum(24 * (depth * depth + depth) * width**3 for depth in depths)
    ins = [(scalars, SMEM)] + [(value, VMEM) for value in sources]
    got = list(run_kernel(kernel, outs, ins, scratch, flops))
    result = {}
    for depth in depths:
        result[depth] = [(got.pop(0), got.pop(0)) for _ in steps]
    return result


def last_kernel(depth, chunk, width, cols, steps, table, n_arrays, order, n_done, *refs):
    refs = list(refs)
    scalars = refs.pop(0)
    arrays = [refs.pop(0) for _ in range(n_arrays)]
    sources = [refs.pop(0) for _ in order]
    lefts = [(refs.pop(0), refs.pop(0)) for _ in range(n_done)]
    outs = [refs.pop(0) for _ in steps]
    left, right = refs.pop(0), refs.pop(0)
    sums, solved_ref, total = refs

    def get(kind, level):
        return sources[order.index((kind, level))]

    for mask, part, position, base, stride in table:
        start = rows_of(scalars, mask, chunk)
        for block in range(depth):
            row = pl.multiple_of((depth - 1 - block) * width + start, chunk)
            sums[pl.ds(row, chunk), pl.ds(part * cols, cols)] = arrays[position][base + stride * block]
    for level in range(depth):
        for part in range(2):
            value = sums[pl.ds(level * width, width), pl.ds(part * cols, cols)]
            store_left(left, pl.ds(part * cols, cols), WIDE * level * width, value.T)

    def emit(level, value):
        solved_ref[...] = value
        for out, step in zip(outs, steps):
            start = rows_of(scalars, step, chunk)
            piece = -solved_ref[pl.ds(start, chunk)]
            out[depth - 1 - level, 0] = piece[:, :cols]
            out[depth - 1 - level, 1] = piece[:, cols:]

    substitute(depth, width, cols, get, sums, right, emit)


    if n_done + 1 < HALVES:
        return
    lefts.append((left, right))
    for row in range(HALVES):
        for col in range(HALVES):
            block = -complex_sum(times(lefts[row][0][...], lefts[col][1][...]), cols)
            for part in range(2):
                total[col, part, pl.ds(row * cols, cols)] = block[:, part * cols : (part + 1) * cols]
    for out, step in zip(outs, steps):
        start = rows_of(scalars, step, chunk)
        for col in range(HALVES):
            for part in range(2):
                out[depth + col, part] = total[col, part, pl.ds(start, chunk)]


def solve_last(depth, made, pieces, scalars, steps, chunk, width, cols, lefts):
    arrays, table = [], []
    for mask, part, array, base, stride in pieces:
        position = next((at for at, value in enumerate(arrays) if value is array), None)
        if position is None:
            position = len(arrays)
            arrays.append(array)
        table.append((mask, part, position, base, stride))
    order = []
    for level in range(depth - 1, 0, -1):
        order.append(("forward", level))
    for level in range(depth):
        order.append(("backward", level))
    done = len(lefts) + 1 == HALVES
    sources = operands(made, order) + ([value for left in lefts for value in left] if done else [])
    blocks = depth + (HALVES if done else 0)
    outs = [((blocks, 2, chunk, cols), F32, VMEM)] * len(steps)
    outs.append(((2 * cols, WIDE * depth * width), BF16, VMEM))
    outs.append(((WIDE * depth * width, 2 * cols), BF16, VMEM))
    scratch = [
        pltpu.VMEM((depth * width, 2 * cols), F32),
        pltpu.VMEM((width, 2 * cols), F32),
        pltpu.VMEM((HALVES, 2, width, cols), F32),
    ]
    kernel = functools.partial(
        last_kernel, depth, chunk, width, cols, steps, table, len(arrays), order,
        len(lefts) if done else 0,
    )
    flops = 24 * depth * depth * width * width * cols
    ins = [(scalars, SMEM)] + [(value, VMEM) for value in arrays]
    ins += [(value, VMEM) for value in sources]
    got = run_kernel(kernel, outs, ins, scratch, flops)
    return got[: len(steps)], got[len(steps) :]


def begin_kernel(zeros, out, zero_ref, sem):
    zero_ref[...] = jnp.zeros_like(zero_ref)
    copies = []
    for slot, depth, count in zeros:
        copies.append((zero_ref.at[pl.ds(0, count)], out.at[0, slot, pl.ds(depth, count)]))
    copies = [
        pltpu.make_async_copy(source, target, sem.at[at])
        for at, (source, target) in enumerate(copies)
    ]
    for copy in copies:
        copy.start()
    for copy in copies:
        copy.wait()


def place_kernel(plan, depth, cols, half, late_plan, diag_plan, shared, *refs):
    refs = list(refs)
    scalars = refs.pop(0)
    pieces = [refs.pop(0) for _ in plan]
    refs.pop(0)
    last_half = half + 1 == HALVES
    own = refs.pop(0) if last_half else None
    late = [refs.pop(0) for _ in late_plan] if last_half else []
    corrections = [refs.pop(0) for _ in diag_plan] if last_half else []
    out = refs.pop(0)
    diag = refs.pop(0) if last_half else None
    (sem,) = refs
    copies = []
    slots = [first + ((scalars[2] // group) ^ step) for first, group, step in plan]
    for at, (piece, slot) in enumerate(zip(pieces, slots)):
        target = out.at[0, slot, :, :, :, pl.ds(half * cols, cols)]
        copies.append(pltpu.make_async_copy(piece.at[pl.ds(0, depth)], target, sem.at[at]))
    for piece, (first, group, step, level) in zip(late, late_plan):
        slot = first + ((scalars[2] // group) ^ step)
        target = out.at[0, slot, pl.ds(0, level)]
        copies.append(pltpu.make_async_copy(piece, target, sem.at[len(copies)]))
    for copy in copies:
        copy.start()
    if last_half:
        for slot in range(diag.shape[1]):
            value = own[0, slot]
            if slot in shared:
                value = jnp.where(scalars[5 + shared[slot]] == 1, value, 0.0)
            diag[0, slot] = value
        for correction, (first, group, step) in zip(corrections, diag_plan):
            slot = first + ((scalars[2] // group) ^ step)
            diag[0, slot] = diag[0, slot] - correction[...]
        for piece, slot in zip(pieces, slots):
            for col in range(HALVES):
                lanes = slice(col * cols, (col + 1) * cols)
                diag[0, slot, :, :, lanes] = diag[0, slot, :, :, lanes] - piece[depth + col]
    for copy in copies:
        copy.wait()


def body(lower_panel, diag_inverse, structure):
    columns = lax.axis_size("col")
    rows = lax.axis_size("row")
    position = lax.axis_index("col")
    place = lax.axis_index("row")
    slots, anc_count, _, chunk, width = lower_panel.shape[1:]
    per_col = [max(1, 2**depth // columns) for depth in range(LEVELS)]
    offsets = [sum(per_col[:depth]) for depth in range(LEVELS)]
    last = LEVELS - 1
    cols = width // HALVES
    groups = [rows // nodes for nodes in per_col]
    steps = [[step * groups[depth] for step in range(per_col[depth])] for depth in range(LEVELS)]
    shared = [depth for depth in range(LEVELS) if 2**depth < columns]
    middle = [depth for depth in range(LEVELS - 1) if 2**depth >= columns]
    active = [position % max(1, columns // 2**depth) == 0 for depth in range(LEVELS)]
    odd = position % 2 == 1
    scalars = [place, odd, jnp.where(odd, turned(place, rows), place)]
    scalars += [jnp.where(odd, turned(mask, rows), mask) for mask in (1, 2)]
    scalars = jnp.stack([jnp.asarray(value, jnp.int32) for value in scalars + active])
    present = structure[0]

    upper = shared[:-1]
    starts = [sum(1 + depth for depth in upper[:at]) for at in range(len(upper))]

    def level_blocks(depth, step=0):
        group = groups[depth]
        return [
            (offsets[depth], lambda at, group=group, step=step: (at // group) ^ step, block)
            for block in range(depth + 1)
        ]

    def packs(plan, depths, limit):
        spans = [(offsets[depth], per_col[depth], depth) for depth in depths if depth]
        return list(pack(plan, spans, scalars, present, lower_panel, diag_inverse, limit))

    plan = [sum([level_blocks(depth) for depth in upper], []), level_blocks(shared[-1])]
    whole_rows, near_rows, far_rows, bases = [], [], [], {}
    virtual = jnp.where(odd, turned(place, rows), place)
    for depth in middle:
        group, first = groups[depth], offsets[depth]
        kept_rows = [(whole_rows, 0)] if group > 2 else [(near_rows, 0), (far_rows, 1)]
        bases[depth] = sum(value.shape[0] for value in kept_rows[0][0]) // 2
        for kept, step in kept_rows:
            slot = first if group == rows else first + ((virtual // group) ^ step)
            diag = lax.dynamic_index_in_dim(diag_inverse[0], slot, 0, keepdims=False)
            panels = lax.dynamic_index_in_dim(lower_panel[0], slot, 0, keepdims=False)[:depth]
            kept += [diag, panels.reshape(2 * depth, chunk, width)]
    packed = packs(plan, shared, PACK_BYTES)
    upper_pack, own_pack = packed[:2]

    stride = columns // 2
    while stride >= 4:
        held = [at for at, depth in enumerate(upper) if columns // 2**depth >= 2 * stride]
        count = 2 * (starts[held[-1]] + 1 + upper[held[-1]])
        pairs = [(source, source + stride) for source in range(0, columns, 2 * stride)]
        if stride == columns // 2 and count == 2:
            travelling = diag_inverse[0, 0]
        else:
            travelling = upper_pack[:count]
        arrived = lax.ppermute(travelling, "col", pairs)
        fresh = position % (2 * stride) == stride
        upper_pack = jnp.concatenate(
            [jnp.where(fresh, arrived, upper_pack[:count]), upper_pack[count:]], axis=0
        )
        stride //= 2
    if whole_rows:
        whole_pack = jnp.concatenate(whole_rows, axis=0)
        near_got = row_swap(whole_pack, 1)
        far_got = row_swap(whole_pack, 2)
        upper_pack, near_got, far_got = lax.optimization_barrier((upper_pack, near_got, far_got))
    if near_rows:
        near_pack = jnp.concatenate(near_rows, axis=0)
        far_pack = jnp.concatenate(far_rows, axis=0)
        pair_got = row_swap(near_pack, 1), row_swap(far_pack, 2)
    from_one = lax.ppermute(
        upper_pack, "col", [(source, source + 1) for source in range(0, columns, 4)]
    )
    from_three = lax.ppermute(
        upper_pack, "col", [(source, source + 3) for source in range(0, columns, 4)]
    )
    upper_got = jnp.where(position % 4 == 1, from_one, from_three)
    planes = max(own_pack.shape[0], upper_got.shape[0])

    def fill(value):
        return jnp.pad(value, ((0, planes - value.shape[0]), (0, 0), (0, 0)))

    own = jnp.where(odd, fill(upper_got), fill(own_pack))

    near = row_swap(own, 1)
    far = row_swap(own, 2)

    def halves(value):
        return value.reshape(value.shape[0] // 2, 2, chunk, width)

    near_sends, far_sends, pair_sends = [halves(far)[:, 0]], [halves(near)[:, 1]], []
    homes = {}
    size, pair_size = planes // 2, 0
    for depth in middle:
        first, count = 2 * bases[depth], 2 * (depth + 1)
        if groups[depth] > 2:
            homes[depth] = size
            near_sends.append(halves(far_got[first : first + count])[:, 0])
            far_sends.append(halves(near_got[first : first + count])[:, 1])
            size += depth + 1
        else:
            homes[depth] = pair_size
            pair_sends.append(pair_got[1][first : first + count])
            pair_size += count
    near_sends = jnp.concatenate(near_sends, axis=0)
    far_sends = jnp.concatenate(far_sends, axis=0)
    pair_sends = [jnp.concatenate(pair_sends, axis=0)] if pair_sends else []
    nodes, group = per_col[last], groups[last]
    after = scalars
    if near_rows:
        after, pair_got = lax.optimization_barrier((scalars, pair_got))
    last_packs = pack_last(
        offsets[last], nodes, last, [(step, group) for step in range(nodes)], cols,
        after, present, lower_panel,
    )
    zeros = [
        (offsets[depth] + node, depth, anc_count - depth)
        for depth in range(LEVELS)
        for node in range(per_col[depth])
        if depth < anc_count
    ]
    panel_shape = lower_panel.shape
    (sel_panel,) = run_kernel(
        functools.partial(begin_kernel, zeros),
        [(panel_shape, F32, ANY)],
        [],
        [
            pltpu.VMEM((anc_count, 2, chunk, width), F32),
            pltpu.SemaphoreType.DMA((len(zeros),)),
        ],
        0,
    )
    near_sends, far_sends, pair_sends, last_packs, sel_panel = lax.optimization_barrier(
        (near_sends, far_sends, pair_sends, last_packs, sel_panel)
    )
    near_more = row_swap(near_sends, 1)
    far_more = row_swap(far_sends, 2)
    pair_more = [row_swap(value, 1) for value in pair_sends]
    near_more, far_more, pair_more, last_packs = lax.optimization_barrier(
        (near_more, far_more, pair_more, last_packs)
    )

    blocks = planes // 2
    mine = jnp.concatenate([own, near, far, near_more[:blocks], far_more[:blocks]], axis=0)
    theirs = col_swap(mine)
    shared_pieces = (
        both_parts(0, mine)
        + both_parts(1, mine, blocks)
        + both_parts(2, mine, 2 * blocks)
        + [(3, 0, mine, 6 * blocks, 1), (3, 1, mine, 7 * blocks, 1)]
    )

    made = {}
    for depth in middle:
        base = bases[depth]
        home = homes[depth]
        if groups[depth] > 2:
            pieces = both_parts(0, whole_pack, base) + both_parts(1, near_got, base)
            pieces += both_parts(2, far_got, base)
            pieces += [(3, 0, near_more, home, 1), (3, 1, far_more, home, 1)]
        else:
            pieces = both_parts(0, near_pack, base) + both_parts(1, pair_got[0], base)
            pieces += both_parts(2, pair_got[1], base)
            pieces += [(3, 0, pair_more[0], home, 2), (3, 1, pair_more[0], home + 1, 2)]
        level = (depth, None, 0, (offsets[depth], groups[depth]))
        made.update(prep([level], pieces, scalars, present, rows, chunk, width))
    levels = [(depth, True, starts[at], None) for at, depth in enumerate(upper)]
    levels.append((shared[-1], False, 0, None))
    made.update(
        prep(levels, shared_pieces, scalars, present, rows, chunk, width, others=[theirs])
    )
    last_pieces = []
    for half in range(HALVES):
        sent = last_packs[half * nodes : (half + 1) * nodes]
        pieces = []
        for step, value in zip(steps[last], sent):
            arrived = row_swap(value, step) if step else value
            if group == 1:
                pieces.append((step, arrived))
                continue
            listed = [(step, arrived)]
            mask = 1
            while mask < group:
                listed += [(mask | at, row_swap(held, mask)) for at, held in listed]
                mask *= 2
            pieces += listed
        last_pieces.append(pieces)

    single = [depth for depth in range(last - 1, 0, -1) if per_col[depth] == 1]
    solved = {}
    for depth in range(1, last):
        if per_col[depth] > 1:
            solved.update(solve([depth], made, scalars, steps[depth], chunk, width, ()))
    second = [value for _, value in last_pieces[-1][:2]]
    solved, second, later = lax.optimization_barrier((solved, second, scalars))
    last_pieces[-1][:2] = [
        (at, value) for (at, _), value in zip(last_pieces[-1][:2], second)
    ]
    lefts, backs = [], []
    for half in range(HALVES):
        outward, left = solve_last(
            last, made, sum([both_parts(at, held) for at, held in last_pieces[half]], []),
            later, steps[last], chunk, width, cols, lefts
        )
        lefts.append(left)
        if half + 1 == HALVES:
            outward, later = lax.optimization_barrier((outward, scalars))
        backs.append(
            [row_swap(piece, step) if step else piece for piece, step in zip(outward, steps[last])]
        )
    last_plan = [(offsets[last], group, step) for step in range(nodes)]
    masked = {offsets[depth]: depth for depth in shared}
    upper_solved = solve(single, made, later, [0], chunk, width, tuple(shared))
    upper_solved, sel_panel = lax.optimization_barrier((upper_solved, sel_panel))
    solved.update(upper_solved)
    for half, back in enumerate(backs):
        late_plan, late_pieces, diag_plan, diag_pieces = [], [], [], []
        if half + 1 == HALVES:
            for depth in range(1, last):
                for step, (piece, correction) in enumerate(solved[depth]):
                    if step:
                        both = jnp.concatenate([piece, correction[None]], axis=0)
                        both = row_swap(both, steps[depth][step])
                        piece, correction = both[:depth], both[depth]
                    late_plan.append((offsets[depth], groups[depth], step, depth))
                    late_pieces.append(piece)
                    diag_plan.append((offsets[depth], groups[depth], step))
                    diag_pieces.append(correction)
        ins = [(scalars, SMEM)] + [(piece, VMEM) for piece in back] + [(sel_panel, ANY)]
        outs = [(panel_shape, F32, ANY)]
        if half + 1 == HALVES:
            ins += [(diag_inverse, VMEM)]
            ins += [(piece, VMEM) for piece in late_pieces + diag_pieces]
            outs.append((diag_inverse.shape, F32, VMEM))
        made_now = run_kernel(
            functools.partial(
                place_kernel, last_plan, last, cols, half, late_plan, diag_plan, masked
            ),
            outs,
            ins,
            [pltpu.SemaphoreType.DMA((nodes + len(late_plan),))],
            0,
            aliases={1 + nodes: 0},
        )
        sel_panel = made_now[0]
    return (sel_panel, made_now[1])


def solution(mesh):
    in_specs = (
        P("col", None, None, None, "row", None),
        P("col", None, None, "row", None),
        P("col", None, None),
    )
    out_specs = (P("col", None, None, None, "row", None), P("col", None, None, "row", None))
    return jax.shard_map(body, mesh=mesh, in_specs=in_specs, out_specs=out_specs, check_vma=False)
```

```python
import functools

import jax
import jax.numpy as jnp
from jax import lax
from jax.experimental import pallas as pl
from jax.experimental.pallas import tpu as pltpu
from jax.sharding import PartitionSpec as P

LEVELS = 6
HALVES = 2
VMEM_BYTES = 18 * 2**20
PACK_BYTES = 58 * 2**20
F32 = jnp.float32
BF16 = jnp.bfloat16
ANY = pl.BlockSpec(memory_space=pl.ANY)
VMEM = pl.BlockSpec(memory_space=pltpu.VMEM)
SMEM = pl.BlockSpec(memory_space=pltpu.SMEM)


def turned(mask, rows):
    if rows < 4:
        return mask
    return (mask & ~3) | ((mask & 1) << 1) | ((mask >> 1) & 1)


def col_swap(value):
    count = lax.axis_size("col")
    return lax.ppermute(value, "col", [(source, source ^ 1) for source in range(count)])


def row_swap(value, mask):
    rows, columns = lax.axis_size("row"), lax.axis_size("col")
    pairs = []
    for row in range(rows):
        for col in range(columns):
            other = row ^ (turned(mask, rows) if col % 2 else mask)
            pairs.append((row * columns + col, other * columns + col))
    return lax.ppermute(value, ("row", "col"), pairs)


def rows_of(scalars, mask, chunk):
    away = mask & ~3
    if mask & 1:
        away = away | scalars[3]
    if mask & 2:
        away = away | scalars[4]
    return pl.multiple_of((scalars[0] ^ away) * chunk, chunk)


def split(value):
    high = value.astype(BF16)
    return high, (value - high.astype(F32)).astype(BF16)


WIDE = 3


def store_left(ref, rows, first, value):
    high, low = split(value)
    size = value.shape[1]
    for at, part in enumerate((high, high, low)):
        ref[rows, pl.ds(first + at * size, size)] = part


def store_right(ref, first, value):
    high, low = split(value)
    size = value.shape[0]
    for at, part in enumerate((high, low, high)):
        ref[pl.ds(first + at * size, size)] = part


def times(left, right):
    return jnp.dot(left, right, preferred_element_type=F32)


def complex_sum(product, half):
    count = product.shape[0] // 2
    by_real, by_imag = product[:count], product[count:]
    return jnp.concatenate(
        [by_real[:, :half] - by_imag[:, half:], by_real[:, half:] + by_imag[:, :half]], axis=1
    )


def run_kernel(kernel, outs, ins, scratch, flops, aliases=None, limit=VMEM_BYTES):
    moved = sum(value.size for value, _ in ins)
    return pl.pallas_call(
        kernel,
        out_shape=[jax.ShapeDtypeStruct(shape, dtype) for shape, dtype, _ in outs],
        in_specs=[spec for _, spec in ins],
        out_specs=[spec for _, _, spec in outs],
        scratch_shapes=scratch,
        input_output_aliases=aliases or {},
        compiler_params=pltpu.CompilerParams(vmem_limit_bytes=limit),
        cost_estimate=pl.CostEstimate(flops=flops // 64, bytes_accessed=moved // 64, transcendentals=0),
    )(*[value for value, _ in ins])


class Loads:
    def __init__(self, sources, buffers, sems):
        self.buffers = buffers
        self.copies = [
            pltpu.make_async_copy(source, buffer, sems.at[at])
            for at, (source, buffer) in enumerate(zip(sources, buffers))
        ]
        for copy in self.copies:
            copy.start()

    def get(self, at):
        if self.copies[at] is not None:
            self.copies[at].wait()
            self.copies[at] = None
        return self.buffers[at]


def both_parts(mask, array, base=0):
    return [(mask, 0, array, 2 * base, 2), (mask, 1, array, 2 * base + 1, 2)]


def pack_kernel(spans, plan, n_outs, chunk, *refs):
    scalars, present, panel_ref, diag_ref = refs[:4]
    outs = refs[4 : 4 + n_outs]
    panel_bufs = refs[4 + n_outs : -2]
    diag_buf, sems = refs[-2:]
    sources, buffers = [], []
    for (first, nodes, depth), buffer in zip(spans, panel_bufs):
        sources.append(panel_ref.at[0, pl.ds(first, nodes), pl.ds(0, depth)])
        buffers.append(buffer)
    if any(block == 0 for blocks in plan for _, _, block in blocks):
        sources.append(diag_ref.at[0])
        buffers.append(diag_buf)
    loads = Loads(sources, buffers, sems)
    where = {first: at for at, (first, _, _) in enumerate(spans)}
    for out, blocks in zip(outs, plan):
        for at, (first, node_of, block) in enumerate(blocks):
            node = node_of(scalars[2])
            if block == 0:
                value = loads.get(len(spans))[first + node]
            else:
                scale = present[first + node, block - 1].astype(F32)
                value = loads.get(where[first])[node, block - 1] * scale
            out[pl.ds(2 * at, 2)] = value


def pack(plan, spans, scalars, present, lower_panel, diag_inverse, limit):
    chunk, width = lower_panel.shape[-2:]
    outs = [((2 * len(blocks), chunk, width), F32, VMEM) for blocks in plan]
    scratch = [pltpu.VMEM((nodes, depth, 2, chunk, width), F32) for _, nodes, depth in spans]
    scratch += [pltpu.VMEM(diag_inverse.shape[1:], F32), pltpu.SemaphoreType.DMA((len(spans) + 1,))]
    kernel = functools.partial(pack_kernel, spans, plan, len(outs), chunk)
    ins = [(scalars, SMEM), (present, SMEM), (lower_panel, ANY), (diag_inverse, ANY)]
    return run_kernel(kernel, outs, ins, scratch, 0, limit=limit)


def pack_last_kernel(first, nodes, depth, steps, cols, *refs):
    scalars, present, panel_ref = refs[:3]
    outs = refs[3 : 3 + len(steps) * HALVES]
    buffer, sem = refs[-2:]
    copy = pltpu.make_async_copy(panel_ref.at[0, pl.ds(first, nodes), pl.ds(0, depth)], buffer, sem)
    copy.start()
    copy.wait()
    for at, (step, group) in enumerate(steps):
        node = (scalars[2] // group) ^ step
        for block in range(depth):
            value = buffer[node, block] * present[first + node, block].astype(F32)
            for half in range(HALVES):
                outs[half * len(steps) + at][pl.ds(2 * block, 2)] = value[
                    :, :, half * cols : (half + 1) * cols
                ]


def pack_last(first, nodes, depth, steps, cols, scalars, present, lower_panel):
    chunk, width = lower_panel.shape[-2:]
    outs = [((2 * depth, chunk, cols), F32, VMEM)] * (len(steps) * HALVES)
    scratch = [pltpu.VMEM((nodes, depth, 2, chunk, width), F32), pltpu.SemaphoreType.DMA]
    kernel = functools.partial(pack_last_kernel, first, nodes, depth, steps, cols)
    ins = [(scalars, SMEM), (present, SMEM), (lower_panel, ANY)]
    return run_kernel(kernel, outs, ins, scratch, 0)


def prep_kernel(levels, table, rows_count, chunk, width, n_arrays, *refs):
    scalars, present = refs[:2]
    arrays = refs[2 : 2 + n_arrays]
    outs = list(refs[2 + n_arrays :])
    odd = scalars[1] == 1
    for depth, swapped, first, slot in levels:
        if depth:
            whole, forward = outs.pop(0), outs.pop(0)
        else:
            whole = None
        backward = outs.pop(0)
        for block in range(depth + 1):
            for mask, part, position, base, stride in table:
                plane = base + stride * (first + block)
                start = rows_of(scalars, mask, chunk)
                if swapped is None:
                    value = arrays[position][plane]
                else:
                    half = n_arrays // 2
                    from_odd = arrays[position + (0 if swapped else half)]
                    from_even = arrays[position + (half if swapped else 0)]
                    value = jnp.where(odd, from_odd[plane], from_even[plane])
                    away = turned(mask, rows_count) if swapped else mask
                    start = pl.multiple_of((scalars[0] ^ away) * chunk, chunk)
                if block == 0:
                    rows = pl.ds(pl.multiple_of(part * width + start, chunk), chunk)
                    store_left(backward, rows, WIDE * depth * width, value)
                else:
                    if slot is not None:
                        at = slot[0] + scalars[2] // slot[1]
                        value = value * present[at, block - 1].astype(F32)
                    rows = pl.ds(pl.multiple_of((depth - block) * width + start, chunk), chunk)
                    whole[rows, pl.ds(part * width, width)] = value
        for level in range(depth):
            for part in range(2):
                value = whole[pl.ds(level * width, width), pl.ds(part * width, width)]
                store_left(forward, pl.ds((2 * level + part) * width, width), 0, value)
                rows = pl.ds(part * width, width)
                store_left(backward, rows, WIDE * level * width, -value.T)


def prep(levels, pieces, scalars, present, rows, chunk, width, others=()):
    arrays, table = [], []
    for mask, part, array, base, stride in pieces:
        position = next((at for at, value in enumerate(arrays) if value is array), None)
        if position is None:
            position = len(arrays)
            arrays.append(array)
        table.append((mask, part, position, base, stride))
    arrays = arrays + list(others)
    outs = []
    for depth, _, _, _ in levels:
        if depth:
            outs.append(((depth * width, 2 * width), F32, VMEM))
            outs.append(((2 * depth * width, WIDE * width), BF16, VMEM))
        outs.append(((2 * width, WIDE * (depth + 1) * width), BF16, VMEM))
    kernel = functools.partial(prep_kernel, levels, table, rows, chunk, width, len(arrays))
    ins = [(scalars, SMEM), (present, SMEM)] + [(value, VMEM) for value in arrays]
    made = list(run_kernel(kernel, outs, ins, [], 0))
    result = {}
    for depth, _, _, _ in levels:
        if depth:
            result[depth], made = tuple(made[:3]), made[3:]
        else:
            result[depth], made = (None, None, made[0]), made[1:]
    return result


def substitute(depth, width, cols, get, sums, right, emit):
    def rows(first, count=1):
        return pl.ds(first * width, count * width)

    for level in range(depth - 1, 0, -1):
        store_right(right, WIDE * level * width, sums[rows(level)])
        forward = get("forward", level)
        for block in range(level - 1, -1, -1):
            product = times(forward[rows(2 * block, 2)], right[rows(WIDE * level, WIDE)])
            sums[rows(block)] -= complex_sum(product, cols)
    store_right(right, 0, sums[rows(0)])
    for level in range(depth):
        product = times(get("backward", level)[...], right[rows(0, WIDE * (level + 1))])
        solved = complex_sum(product, cols)
        store_right(right, WIDE * level * width, solved)
        emit(level, solved)


def solve_kernel(depths, chunk, width, steps, order, masked, *refs):
    refs = list(refs)
    scalars = refs.pop(0)
    sources = [refs.pop(0) for _ in order]
    outs = {depth: [(refs.pop(0), refs.pop(0)) for _ in steps] for depth in depths}
    sums_ref, right_ref, solved_ref = refs

    def get(kind, level):
        return sources[order.index((kind, level))]

    for depth in depths:
        sums = sums_ref.at[pl.ds(0, depth * width)]
        right = right_ref.at[pl.ds(0, WIDE * depth * width)]
        sums[...] = get("whole", depth)[...]

        def send(block, value, sign):
            solved_ref[...] = value
            for (out, correction), step in zip(outs[depth], steps):
                start = rows_of(scalars, step, chunk)
                piece = solved_ref[pl.ds(start, chunk)] * sign
                if depth in masked:
                    piece = jnp.where(scalars[5 + depth] == 1, piece, 0.0)
                for part in range(2):
                    plane = piece[:, part * width : (part + 1) * width]
                    if block == 0:
                        correction[part] = plane
                    else:
                        out[block - 1, part] = plane

        substitute(
            depth, width, width, get, sums, right,
            lambda level, solved: send(depth - level, solved, -1.0),
        )
        product = times(get("backward", depth)[:, : WIDE * depth * width], right[...])
        send(0, complex_sum(product, width), 1.0)


def operands(made, names):
    index = {"whole": 0, "forward": 1, "backward": 2}
    return [made[level][index[kind]] for kind, level in names]


def solve(depths, made, scalars, steps, chunk, width, masked):
    top = depths[0]
    order = [("whole", top)]
    for level in range(top - 1, 0, -1):
        order.append(("forward", level))
    for level in range(top + 1):
        order.append(("backward", level))
    order += [("whole", depth) for depth in depths[1:]]
    sources = operands(made, order)
    outs = []
    for depth in depths:
        for _ in steps:
            outs.append(((depth, 2, chunk, width), F32, VMEM))
            outs.append(((2, chunk, width), F32, VMEM))
    scratch = [
        pltpu.VMEM((top * width, 2 * width), F32),
        pltpu.VMEM((WIDE * top * width, 2 * width), BF16),
        pltpu.VMEM((width, 2 * width), F32),
    ]
    kernel = functools.partial(solve_kernel, depths, chunk, width, steps, order, masked)
    flops = sum(24 * (depth * depth + depth) * width**3 for depth in depths)
    ins = [(scalars, SMEM)] + [(value, VMEM) for value in sources]
    got = list(run_kernel(kernel, outs, ins, scratch, flops))
    result = {}
    for depth in depths:
        result[depth] = [(got.pop(0), got.pop(0)) for _ in steps]
    return result


def last_kernel(depth, chunk, width, cols, steps, table, n_arrays, order, n_done, *refs):
    refs = list(refs)
    scalars = refs.pop(0)
    arrays = [refs.pop(0) for _ in range(n_arrays)]
    sources = [refs.pop(0) for _ in order]
    lefts = [(refs.pop(0), refs.pop(0)) for _ in range(n_done)]
    outs = [refs.pop(0) for _ in steps]
    left, right = refs.pop(0), refs.pop(0)
    sums, solved_ref, total = refs

    def get(kind, level):
        return sources[order.index((kind, level))]

    for mask, part, position, base, stride in table:
        start = rows_of(scalars, mask, chunk)
        for block in range(depth):
            row = pl.multiple_of((depth - 1 - block) * width + start, chunk)
            sums[pl.ds(row, chunk), pl.ds(part * cols, cols)] = arrays[position][base + stride * block]
    for level in range(depth):
        for part in range(2):
            value = sums[pl.ds(level * width, width), pl.ds(part * cols, cols)]
            store_left(left, pl.ds(part * cols, cols), WIDE * level * width, value.T)

    def emit(level, value):
        solved_ref[...] = value
        for out, step in zip(outs, steps):
            start = rows_of(scalars, step, chunk)
            piece = -solved_ref[pl.ds(start, chunk)]
            out[depth - 1 - level, 0] = piece[:, :cols]
            out[depth - 1 - level, 1] = piece[:, cols:]

    substitute(depth, width, cols, get, sums, right, emit)


    if n_done + 1 < HALVES:
        return
    lefts.append((left, right))
    for row in range(HALVES):
        for col in range(HALVES):
            block = -complex_sum(times(lefts[row][0][...], lefts[col][1][...]), cols)
            for part in range(2):
                total[col, part, pl.ds(row * cols, cols)] = block[:, part * cols : (part + 1) * cols]
    for out, step in zip(outs, steps):
        start = rows_of(scalars, step, chunk)
        for col in range(HALVES):
            for part in range(2):
                out[depth + col, part] = total[col, part, pl.ds(start, chunk)]


def solve_last(depth, made, pieces, scalars, steps, chunk, width, cols, lefts):
    arrays, table = [], []
    for mask, part, array, base, stride in pieces:
        position = next((at for at, value in enumerate(arrays) if value is array), None)
        if position is None:
            position = len(arrays)
            arrays.append(array)
        table.append((mask, part, position, base, stride))
    order = []
    for level in range(depth - 1, 0, -1):
        order.append(("forward", level))
    for level in range(depth):
        order.append(("backward", level))
    done = len(lefts) + 1 == HALVES
    sources = operands(made, order) + ([value for left in lefts for value in left] if done else [])
    blocks = depth + (HALVES if done else 0)
    outs = [((blocks, 2, chunk, cols), F32, VMEM)] * len(steps)
    outs.append(((2 * cols, WIDE * depth * width), BF16, VMEM))
    outs.append(((WIDE * depth * width, 2 * cols), BF16, VMEM))
    scratch = [
        pltpu.VMEM((depth * width, 2 * cols), F32),
        pltpu.VMEM((width, 2 * cols), F32),
        pltpu.VMEM((HALVES, 2, width, cols), F32),
    ]
    kernel = functools.partial(
        last_kernel, depth, chunk, width, cols, steps, table, len(arrays), order,
        len(lefts) if done else 0,
    )
    flops = 24 * depth * depth * width * width * cols
    ins = [(scalars, SMEM)] + [(value, VMEM) for value in arrays]
    ins += [(value, VMEM) for value in sources]
    got = run_kernel(kernel, outs, ins, scratch, flops)
    return got[: len(steps)], got[len(steps) :]


def begin_kernel(zeros, out, zero_ref, sem):
    zero_ref[...] = jnp.zeros_like(zero_ref)
    copies = []
    for slot, depth, count in zeros:
        copies.append((zero_ref.at[pl.ds(0, count)], out.at[0, slot, pl.ds(depth, count)]))
    copies = [
        pltpu.make_async_copy(source, target, sem.at[at])
        for at, (source, target) in enumerate(copies)
    ]
    for copy in copies:
        copy.start()
    for copy in copies:
        copy.wait()


def place_kernel(plan, depth, cols, half, late_plan, diag_plan, shared, *refs):
    refs = list(refs)
    scalars = refs.pop(0)
    pieces = [refs.pop(0) for _ in plan]
    refs.pop(0)
    last_half = half + 1 == HALVES
    own = refs.pop(0) if last_half else None
    late = [refs.pop(0) for _ in late_plan] if last_half else []
    corrections = [refs.pop(0) for _ in diag_plan] if last_half else []
    out = refs.pop(0)
    diag = refs.pop(0) if last_half else None
    (sem,) = refs
    copies = []
    slots = [first + ((scalars[2] // group) ^ step) for first, group, step in plan]
    for at, (piece, slot) in enumerate(zip(pieces, slots)):
        target = out.at[0, slot, :, :, :, pl.ds(half * cols, cols)]
        copies.append(pltpu.make_async_copy(piece.at[pl.ds(0, depth)], target, sem.at[at]))
    for piece, (first, group, step, level) in zip(late, late_plan):
        slot = first + ((scalars[2] // group) ^ step)
        target = out.at[0, slot, pl.ds(0, level)]
        copies.append(pltpu.make_async_copy(piece, target, sem.at[len(copies)]))
    for copy in copies:
        copy.start()
    if last_half:
        for slot in range(diag.shape[1]):
            value = own[0, slot]
            if slot in shared:
                value = jnp.where(scalars[5 + shared[slot]] == 1, value, 0.0)
            diag[0, slot] = value
        for correction, (first, group, step) in zip(corrections, diag_plan):
            slot = first + ((scalars[2] // group) ^ step)
            diag[0, slot] = diag[0, slot] - correction[...]
        for piece, slot in zip(pieces, slots):
            for col in range(HALVES):
                lanes = slice(col * cols, (col + 1) * cols)
                diag[0, slot, :, :, lanes] = diag[0, slot, :, :, lanes] - piece[depth + col]
    for copy in copies:
        copy.wait()


def body(lower_panel, diag_inverse, structure):
    columns = lax.axis_size("col")
    rows = lax.axis_size("row")
    position = lax.axis_index("col")
    place = lax.axis_index("row")
    slots, anc_count, _, chunk, width = lower_panel.shape[1:]
    per_col = [max(1, 2**depth // columns) for depth in range(LEVELS)]
    offsets = [sum(per_col[:depth]) for depth in range(LEVELS)]
    last = LEVELS - 1
    cols = width // HALVES
    groups = [rows // nodes for nodes in per_col]
    steps = [[step * groups[depth] for step in range(per_col[depth])] for depth in range(LEVELS)]
    shared = [depth for depth in range(LEVELS) if 2**depth < columns]
    middle = [depth for depth in range(LEVELS - 1) if 2**depth >= columns]
    active = [position % max(1, columns // 2**depth) == 0 for depth in range(LEVELS)]
    odd = position % 2 == 1
    scalars = [place, odd, jnp.where(odd, turned(place, rows), place)]
    scalars += [jnp.where(odd, turned(mask, rows), mask) for mask in (1, 2)]
    scalars = jnp.stack([jnp.asarray(value, jnp.int32) for value in scalars + active])
    present = structure[0]

    upper = shared[:-1]
    starts = [sum(1 + depth for depth in upper[:at]) for at in range(len(upper))]

    def level_blocks(depth, step=0):
        group = groups[depth]
        return [
            (offsets[depth], lambda at, group=group, step=step: (at // group) ^ step, block)
            for block in range(depth + 1)
        ]

    def packs(plan, depths, limit):
        spans = [(offsets[depth], per_col[depth], depth) for depth in depths if depth]
        return list(pack(plan, spans, scalars, present, lower_panel, diag_inverse, limit))

    plan = [sum([level_blocks(depth) for depth in upper], []), level_blocks(shared[-1])]
    whole_rows, near_rows, far_rows, bases = [], [], [], {}
    virtual = jnp.where(odd, turned(place, rows), place)
    for depth in middle:
        group, first = groups[depth], offsets[depth]
        kept_rows = [(whole_rows, 0)] if group > 2 else [(near_rows, 0), (far_rows, 1)]
        bases[depth] = sum(value.shape[0] for value in kept_rows[0][0]) // 2
        for kept, step in kept_rows:
            slot = first if group == rows else first + ((virtual // group) ^ step)
            diag = lax.dynamic_index_in_dim(diag_inverse[0], slot, 0, keepdims=False)
            panels = lax.dynamic_index_in_dim(lower_panel[0], slot, 0, keepdims=False)[:depth]
            kept += [diag, panels.reshape(2 * depth, chunk, width)]
    packed = packs(plan, shared, PACK_BYTES)
    upper_pack, own_pack = packed[:2]

    stride = columns // 2
    while stride >= 4:
        held = [at for at, depth in enumerate(upper) if columns // 2**depth >= 2 * stride]
        count = 2 * (starts[held[-1]] + 1 + upper[held[-1]])
        pairs = [(source, source + stride) for source in range(0, columns, 2 * stride)]
        if stride == columns // 2 and count == 2:
            travelling = diag_inverse[0, 0]
        else:
            travelling = upper_pack[:count]
        arrived = lax.ppermute(travelling, "col", pairs)
        fresh = position % (2 * stride) == stride
        upper_pack = jnp.concatenate(
            [jnp.where(fresh, arrived, upper_pack[:count]), upper_pack[count:]], axis=0
        )
        stride //= 2
    if whole_rows:
        whole_pack = jnp.concatenate(whole_rows, axis=0)
        near_got = row_swap(whole_pack, 1)
        far_got = row_swap(whole_pack, 2)
    if near_rows:
        near_pack = jnp.concatenate(near_rows, axis=0)
        far_pack = jnp.concatenate(far_rows, axis=0)
        pair_got = row_swap(near_pack, 1), row_swap(far_pack, 2)
    from_one = lax.ppermute(
        upper_pack, "col", [(source, source + 1) for source in range(0, columns, 4)]
    )
    from_three = lax.ppermute(
        upper_pack, "col", [(source, source + 3) for source in range(0, columns, 4)]
    )
    if whole_rows:
        from_one, from_three, near_got, far_got = lax.optimization_barrier(
            (from_one, from_three, near_got, far_got)
        )
    upper_got = jnp.where(position % 4 == 1, from_one, from_three)
    planes = max(own_pack.shape[0], upper_got.shape[0])

    def fill(value):
        return jnp.pad(value, ((0, planes - value.shape[0]), (0, 0), (0, 0)))

    own = jnp.where(odd, fill(upper_got), fill(own_pack))

    near = row_swap(own, 1)
    far = row_swap(own, 2)

    def halves(value):
        return value.reshape(value.shape[0] // 2, 2, chunk, width)

    near_sends, far_sends, pair_sends = [halves(far)[:, 0]], [halves(near)[:, 1]], []
    homes = {}
    size, pair_size = planes // 2, 0
    for depth in middle:
        first, count = 2 * bases[depth], 2 * (depth + 1)
        if groups[depth] > 2:
            homes[depth] = size
            near_sends.append(halves(far_got[first : first + count])[:, 0])
            far_sends.append(halves(near_got[first : first + count])[:, 1])
            size += depth + 1
        else:
            homes[depth] = pair_size
            pair_sends.append(pair_got[1][first : first + count])
            pair_size += count
    near_sends = jnp.concatenate(near_sends, axis=0)
    far_sends = jnp.concatenate(far_sends, axis=0)
    pair_sends = [jnp.concatenate(pair_sends, axis=0)] if pair_sends else []
    nodes, group = per_col[last], groups[last]
    after = scalars
    if near_rows:
        after, pair_got = lax.optimization_barrier((scalars, pair_got))
    last_packs = pack_last(
        offsets[last], nodes, last, [(step, group) for step in range(nodes)], cols,
        after, present, lower_panel,
    )
    zeros = [
        (offsets[depth] + node, depth, anc_count - depth)
        for depth in range(LEVELS)
        for node in range(per_col[depth])
        if depth < anc_count
    ]
    panel_shape = lower_panel.shape
    (sel_panel,) = run_kernel(
        functools.partial(begin_kernel, zeros),
        [(panel_shape, F32, ANY)],
        [],
        [
            pltpu.VMEM((anc_count, 2, chunk, width), F32),
            pltpu.SemaphoreType.DMA((len(zeros),)),
        ],
        0,
    )
    near_sends, far_sends, pair_sends, last_packs, sel_panel = lax.optimization_barrier(
        (near_sends, far_sends, pair_sends, last_packs, sel_panel)
    )
    near_more = row_swap(near_sends, 1)
    far_more = row_swap(far_sends, 2)
    pair_more = [row_swap(value, 1) for value in pair_sends]
    near_more, far_more, pair_more, last_packs = lax.optimization_barrier(
        (near_more, far_more, pair_more, last_packs)
    )

    blocks = planes // 2
    mine = jnp.concatenate([own, near, far, near_more[:blocks], far_more[:blocks]], axis=0)
    theirs = col_swap(mine)
    shared_pieces = (
        both_parts(0, mine)
        + both_parts(1, mine, blocks)
        + both_parts(2, mine, 2 * blocks)
        + [(3, 0, mine, 6 * blocks, 1), (3, 1, mine, 7 * blocks, 1)]
    )

    made = {}
    for depth in middle:
        base = bases[depth]
        home = homes[depth]
        if groups[depth] > 2:
            pieces = both_parts(0, whole_pack, base) + both_parts(1, near_got, base)
            pieces += both_parts(2, far_got, base)
            pieces += [(3, 0, near_more, home, 1), (3, 1, far_more, home, 1)]
        else:
            pieces = both_parts(0, near_pack, base) + both_parts(1, pair_got[0], base)
            pieces += both_parts(2, pair_got[1], base)
            pieces += [(3, 0, pair_more[0], home, 2), (3, 1, pair_more[0], home + 1, 2)]
        level = (depth, None, 0, (offsets[depth], groups[depth]))
        made.update(prep([level], pieces, scalars, present, rows, chunk, width))
    levels = [(depth, True, starts[at], None) for at, depth in enumerate(upper)]
    levels.append((shared[-1], False, 0, None))
    made.update(
        prep(levels, shared_pieces, scalars, present, rows, chunk, width, others=[theirs])
    )
    last_pieces = []
    for half in range(HALVES):
        sent = last_packs[half * nodes : (half + 1) * nodes]
        pieces = []
        for step, value in zip(steps[last], sent):
            arrived = row_swap(value, step) if step else value
            if group == 1:
                pieces.append((step, arrived))
                continue
            listed = [(step, arrived)]
            mask = 1
            while mask < group:
                listed += [(mask | at, row_swap(held, mask)) for at, held in listed]
                mask *= 2
            pieces += listed
        last_pieces.append(pieces)

    single = [depth for depth in range(last - 1, 0, -1) if per_col[depth] == 1]
    solved = {}
    for depth in range(1, last):
        if per_col[depth] > 1:
            solved.update(solve([depth], made, scalars, steps[depth], chunk, width, ()))
    second = [value for _, value in last_pieces[-1][:2]]
    solved, second, later = lax.optimization_barrier((solved, second, scalars))
    last_pieces[-1][:2] = [
        (at, value) for (at, _), value in zip(last_pieces[-1][:2], second)
    ]
    lefts, backs = [], []
    for half in range(HALVES):
        outward, left = solve_last(
            last, made, sum([both_parts(at, held) for at, held in last_pieces[half]], []),
            later, steps[last], chunk, width, cols, lefts
        )
        lefts.append(left)
        if half + 1 == HALVES:
            outward, later = lax.optimization_barrier((outward, scalars))
        backs.append(
            [row_swap(piece, step) if step else piece for piece, step in zip(outward, steps[last])]
        )
    last_plan = [(offsets[last], group, step) for step in range(nodes)]
    masked = {offsets[depth]: depth for depth in shared}
    upper_solved = solve(single, made, later, [0], chunk, width, tuple(shared))
    upper_solved, sel_panel = lax.optimization_barrier((upper_solved, sel_panel))
    solved.update(upper_solved)
    for half, back in enumerate(backs):
        late_plan, late_pieces, diag_plan, diag_pieces = [], [], [], []
        if half + 1 == HALVES:
            for depth in range(1, last):
                for step, (piece, correction) in enumerate(solved[depth]):
                    if step:
                        both = jnp.concatenate([piece, correction[None]], axis=0)
                        both = row_swap(both, steps[depth][step])
                        piece, correction = both[:depth], both[depth]
                    late_plan.append((offsets[depth], groups[depth], step, depth))
                    late_pieces.append(piece)
                    diag_plan.append((offsets[depth], groups[depth], step))
                    diag_pieces.append(correction)
        ins = [(scalars, SMEM)] + [(piece, VMEM) for piece in back] + [(sel_panel, ANY)]
        outs = [(panel_shape, F32, ANY)]
        if half + 1 == HALVES:
            ins += [(diag_inverse, VMEM)]
            ins += [(piece, VMEM) for piece in late_pieces + diag_pieces]
            outs.append((diag_inverse.shape, F32, VMEM))
        made_now = run_kernel(
            functools.partial(
                place_kernel, last_plan, last, cols, half, late_plan, diag_plan, masked
            ),
            outs,
            ins,
            [pltpu.SemaphoreType.DMA((nodes + len(late_plan),))],
            0,
            aliases={1 + nodes: 0},
        )
        sel_panel = made_now[0]
    return (sel_panel, made_now[1])


def solution(mesh):
    in_specs = (
        P("col", None, None, None, "row", None),
        P("col", None, None, "row", None),
        P("col", None, None),
    )
    out_specs = (P("col", None, None, None, "row", None), P("col", None, None, "row", None))
    return jax.shard_map(body, mesh=mesh, in_specs=in_specs, out_specs=out_specs, check_vma=False)
```
